32 devices in a mesh: section: 4 (over y, x), dp: 4 (over z), mp: 2 (over core).
Axes of the slice: x: 2, y: 2, z: 4, core: 2. Of those that a mesh axis runs over, the one named last changes fastest.
Arguments:
- hidden_in: bfloat16 [8, 512, 768], P('dp', 'mp'), may hold values from -6 to 6
- segments: int32 [8, 512], P('dp'), may hold values from 0 to 5, never falling along the last dimension, each value on 1 to 256 neighbouring positions
- partners: int32 [8, 6], P('dp'), may hold values from 0 to 5, as said below
- queue: bfloat16 [16384, 768], P(('section', 'dp', 'mp')), may hold values from -6 to 6
- first_weight: bfloat16 [2, 4, 768, 4, 768], P(None, 'section', None, None, 'mp')
- second_weight: bfloat16 [2, 4, 2, 768, 768], P(None, 'section', None, 'mp'), may hold values from -0.109375 to 0.109375
- out_bias: float32 [2, 4, 768], P(None, 'section'), may hold values from -3 to 3
- ln_gain: float32 [2, 4, 768], P(None, 'section'), may hold values from 0.5 to 1.5
- ln_bias: float32 [2, 4, 768], P(None, 'section'), may hold values from -3 to 3
Outputs:
- loss: float32 [], replicated
- grad_input: bfloat16 [8, 512, 768], P('dp', 'mp', 'section')
- grad_first: float32 [4, 768, 4, 768], P('section', None, None, 'mp')
- grad_second: float32 [4, 2, 768, 768], P('section', None, 'mp')
- grad_out_bias: float32 [4, 768], P('section')
- grad_gain: float32 [4, 768], P('section')
- grad_ln_bias: float32 [4, 768], P('section')
The draws below stay inside these ranges and needn't reach their ends.
Inputs may be any that keep to these rules, and one draw needn't show every extreme that they name: In each row the crops form pairs: partners[r, c] differs from c, and partners[r, partners[r, c]] = c.
All inputs are finite; a program needn't handle non-finite values.
Results may differ from the reference program's by a relative error of at most 0.025.
Values may be sent and summed in bfloat16 or wider, within the bound.
A program may use at most 256 MiB of HBM per device.

```python
import math
import jax
import jax.numpy as jnp
import numpy as np
from jax import lax

D = 768
HEADS = 12
HD = 64
FF = 3072
SEQ = 512
SEGS = 6
MOST = 256
ROWS = 8
CROPS = 48
QUEUE = 16384
N_SECTION = 4


def draw_partners(key, part):
    key = jax.random.fold_in(key, 7)
    row_keys = jax.random.split(key, ROWS)

    def one_row(row_key):
        ordering = jax.random.permutation(row_key, SEGS).astype(jnp.int32)
        first_half = ordering[0::2]
        second_half = ordering[1::2]
        partner_ids = jnp.zeros((SEGS,), jnp.int32)
        partner_ids = partner_ids.at[first_half].set(second_half)
        return partner_ids.at[second_half].set(first_half)
    return jax.vmap(one_row)(row_keys).astype(jnp.int32)


def draw_first_weight(key, part):
    key = jax.random.fold_in(key, 3)
    full_shape = (2, N_SECTION, D, 4, D)
    base = jax.random.normal(key, full_shape, jnp.float32)
    even_section = (jnp.arange(N_SECTION) % 2 == 0)[None, :, None, None, None]
    output_slot = (jnp.arange(4) == 3)[None, None, None, :, None]
    factor = jnp.where(even_section & output_slot, 6.0, 1.0)
    return (base * factor * D ** (-0.5)).astype(jnp.bfloat16)


def levels(rng, dims, cuts, least, top_value):
    loudness = 1.0
    for axis_at, blocks in cuts:
        heights = jax.random.uniform(jax.random.fold_in(jax.random.fold_in(rng, 6), axis_at), (blocks,), jnp.float32, least / len(cuts), top_value / len(cuts))
        loudness = loudness * jnp.repeat(jnp.exp(heights), dims[axis_at] // blocks).reshape((-1,) + (1,) * (len(dims) - 1 - axis_at))
    return loudness


def length_profile(count, total, reach, lean):
    weights = [(1 << 20) // math.isqrt(grade ** lean) + 1 for grade in range(2, count + 1)]
    rest, holding = total - reach - (count - 1), [1] * (count - 1)
    while rest > 0:
        candidates = [i for i in range(count - 1) if holding[i] < reach]
        pool, budget = sum([weights[i] for i in candidates]), rest
        for i in candidates:
            more = min(reach - holding[i], max(1, budget * weights[i] // pool), rest)
            holding[i] = holding[i] + more
            rest = rest - more
    return np.array([reach] + holding)


def uneven_parts(stream_key, number_of, total, bound, lean):
    if number_of == 2:
        one = jax.random.randint(stream_key, (), max(1, total - bound), min(bound, total - 1) + 1)
        return jnp.stack([one, total - one])
    sizes = jnp.asarray(length_profile(number_of, total, bound, lean), jnp.int32)
    couples = (number_of - 1) // 2
    giver, sink = sizes[1:1 + 2 * couples:2], sizes[2:2 + 2 * couples:2]
    room = jnp.minimum(giver - 1, bound - sink)
    passed = jax.random.randint(jax.random.fold_in(stream_key, 1), (couples,), 0, 1 << 20) % (room + 1)
    sizes = sizes.at[1:1 + 2 * couples:2].set(giver - passed).at[2:2 + 2 * couples:2].set(sink + passed)
    return sizes[jax.random.permutation(jax.random.fold_in(stream_key, 2), number_of)]


def scatter_about(stream_key, extent, width, bound, shards=(), held_as=jnp.bfloat16):
    array = jax.random.normal(stream_key, extent, jnp.float32) * width
    if len(shards) > 0:
        array = levels(stream_key, extent, shards, -0.22, 0.18) * array
    return jnp.clip(array, min=-bound, max=bound).astype(held_as)


def setup_inputs(seed: int = 0) -> dict:
    streams_of = jax.random.split(jax.random.key(seed), 10)
    hidden_in = scatter_about(streams_of[0], (ROWS, SEQ, D), 1.0, 6.0, ((0, 4), (1, 2)))
    segments = jax.vmap(lambda own: jnp.searchsorted(jnp.cumsum(uneven_parts(own, SEGS, SEQ, MOST, 2)), jnp.arange(SEQ), side="right"))(jax.random.split(streams_of[1], ROWS)).reshape((ROWS, SEQ)).astype(jnp.int32)
    partners = draw_partners(jax.random.fold_in(streams_of[9], 71), 0)
    queue = scatter_about(streams_of[3], (QUEUE, D), 1.0, 6.0, ((0, 32),))
    first_weight = draw_first_weight(jax.random.fold_in(streams_of[9], 71), 0)
    second_weight = scatter_about(streams_of[5], (2, N_SECTION, 2, D, D), FF ** -0.5, 0.109375, ((1, 4), (3, 2)))
    out_bias = scatter_about(streams_of[6], (2, N_SECTION, D), 0.5, 3.0, ((1, 4),), jnp.float32)
    ln_gain = jnp.clip(1.0 + 0.1 * jax.random.normal(streams_of[7], (2, N_SECTION, D), jnp.float32), 0.5, 1.5)
    ln_bias = scatter_about(streams_of[8], (2, N_SECTION, D), 0.5, 3.0, ((1, 4),), jnp.float32)
    return {"hidden_in": hidden_in, "segments": segments, "partners": partners, "queue": queue, "first_weight": first_weight, "second_weight": second_weight, "out_bias": out_bias, "ln_gain": ln_gain, "ln_bias": ln_bias}


@jax.custom_vjp
def low(v):
    return lax.optimization_barrier(v.astype(jnp.bfloat16)).astype(jnp.float32)

@jax.custom_vjp
def low_back(v):
    return v

def low_keep(v):
    return (low(v), None)

def low_pass(kept, grad):
    return (grad,)

def back_keep(v):
    return (v, None)

def back_low(kept, grad):
    return (low(grad),)
low.defvjp(low_keep, low_pass)
low_back.defvjp(back_keep, back_low)
inv_tau = 20.0
layer_eps = 1e-12
unit_eps = 1e-06
neg_fill = -1e+30

def precise(spec, left, right):
    return jnp.einsum(spec, left, right, precision=lax.Precision.HIGHEST)

def layer_norm(residual, norm_gain, norm_shift):
    centre = residual - lax.optimization_barrier(jnp.mean(residual, axis=-1, keepdims=True))
    spread = lax.optimization_barrier(jnp.mean(centre * centre, axis=-1, keepdims=True))
    return centre * lax.rsqrt(spread + layer_eps) * norm_gain + norm_shift

def unit_rows(vectors):
    return vectors * lax.rsqrt(lax.optimization_barrier(jnp.sum(vectors * vectors, axis=-1, keepdims=True)) + unit_eps)

def gelu_exact(values):
    return jax.nn.gelu(values, approximate=False)

def attention(hidden, segment, w_first, out_bias, norm_gain, norm_shift):
    score_scale = HD ** (-0.5)
    proj_qkv = w_first[:, :3].reshape(D, 3, HEADS, HD)
    qkv_low = low_back(low(precise('sd,djhe->jhse', hidden, proj_qkv)))
    scores = low_back(precise('hqe,hke->hqk', qkv_low[0], qkv_low[1]) * score_scale)
    same_crop = segment[:, None] == segment[None, :]
    scores = jnp.where(same_crop[None], scores, neg_fill)
    row_max = lax.optimization_barrier(jnp.max(scores, axis=-1, keepdims=True))
    weights = jnp.exp(scores - row_max)
    attn_prob = weights / lax.optimization_barrier(jnp.sum(weights, axis=-1, keepdims=True))
    mixed_out = low_back(low(precise('hqk,hke->hqe', low(attn_prob), qkv_low[2])))
    proj_out = w_first[:, 3].reshape(D, HEADS, HD)
    branch = low_back(precise('hse,dhe->sd', mixed_out, proj_out))
    return layer_norm(hidden + branch + out_bias, norm_gain, norm_shift)

def feed_forward(hidden, w_first, w_down, out_bias, norm_gain, norm_shift):
    up_proj = low_back(precise('sd,djc->sjc', hidden, w_first))
    activated = low(gelu_exact(up_proj))
    branch = low_back(precise('sjc,jcd->sd', activated, w_down))
    return layer_norm(hidden + branch + out_bias, norm_gain, norm_shift)

def encode(hidden, segment, params):
    first_w, second_w, out_bias, norm_gain, norm_shift = params
    for section_id in range(N_SECTION):
        if section_id > 0:
            hidden = low_back(low(hidden))
        if section_id % 2 == 0:
            hidden = attention(hidden, segment, first_w[section_id], out_bias[section_id], norm_gain[section_id], norm_shift[section_id])
        else:
            w_down = jnp.concatenate([second_w[section_id - 1], second_w[section_id]], axis=0)
            hidden = feed_forward(hidden, first_w[section_id], w_down, out_bias[section_id], norm_gain[section_id], norm_shift[section_id])
    return hidden

def pool_crops(hidden, segment):
    member = (segment[:, None] == jnp.arange(SEGS, dtype=jnp.int32)[None, :]).astype(jnp.float32)
    counts = lax.optimization_barrier(jnp.sum(member, axis=0))
    return precise('sc,sd->cd', member, hidden) / counts[:, None]

def reference(hidden_in, segments, partners, queue, first_weight, second_weight, out_bias, ln_gain, ln_bias):
    first_w = first_weight.astype(jnp.float32)
    second_w = second_weight.astype(jnp.float32)
    query_params = (first_w[0], second_w[0], out_bias[0], ln_gain[0], ln_bias[0])
    key_params = (first_w[1], second_w[1], out_bias[1], ln_gain[1], ln_bias[1])
    inputs = hidden_in.astype(jnp.float32)
    queue_low = low(unit_rows(queue.astype(jnp.float32)))

    def key_row(row_data):
        hidden, segment, partner_ids = row_data
        key_units = low(unit_rows(pool_crops(encode(hidden, segment, key_params), segment)))
        pick_table = (partner_ids[:, None] == jnp.arange(SEGS, dtype=jnp.int32)[None, :]).astype(jnp.float32)
        return precise('cp,pd->cd', pick_table, key_units)
    positives = lax.map(key_row, (inputs, segments, partners))

    def row_loss(hidden, params, segment, positive):
        queries = low(unit_rows(pool_crops(encode(hidden, segment, params), segment)))
        pos_logit = lax.optimization_barrier(jnp.sum(queries * positive, axis=-1)) * inv_tau
        neg_logit = precise('cd,jd->cj', queries, queue_low) * inv_tau
        queue_total = lax.optimization_barrier(jnp.sum(jnp.exp(neg_logit - inv_tau), axis=-1))
        log_total = inv_tau + jnp.log(jnp.exp(pos_logit - inv_tau) + queue_total)
        return jnp.sum(log_total - pos_logit) / CROPS
    zero_grads = jax.tree.map(jnp.zeros_like, query_params)

    def row_step(carry, row_data):
        hidden, segment, positive = row_data
        row_value, pull_back = jax.vjp(lambda hidden_v, param_v: row_loss(hidden_v, param_v, segment, positive), hidden, query_params)
        grad_hidden, grad_tree = pull_back(jnp.ones_like(row_value))
        loss_sum, grad_sum = carry
        return ((loss_sum + row_value, jax.tree.map(jnp.add, grad_sum, grad_tree)), grad_hidden)
    (loss_value, grad_tree), grad_rows = lax.scan(row_step, (jnp.zeros((), jnp.float32), zero_grads), (inputs, segments, positives))
    grad_first, grad_second, grad_bias, grad_gain, grad_shift = grad_tree
    return (loss_value, grad_rows.astype(jnp.bfloat16), grad_first, grad_second, grad_bias, grad_gain, grad_shift)
```

```python
import functools
import jax
import jax.numpy as jnp
from jax import lax
from jax.experimental import pallas as pl
from jax.experimental.pallas import tpu as pltpu

F32 = jnp.float32
BF = jnp.bfloat16
HD = 64
NEG = -1e30
LN_EPS = 1e-12


def mm(a, b, ca=1, cb=0):
    return lax.dot_general(a, b, (((ca,), (cb,)), ((), ())), preferred_element_type=F32)


def norm_rows(resid, gain, shift):
    centre = resid - jnp.mean(resid, axis=-1, keepdims=True)
    spread = jnp.mean(centre * centre, axis=-1, keepdims=True)
    rstd = lax.rsqrt(spread + LN_EPS)
    xhat = centre * rstd
    return xhat * gain + shift, xhat, rstd


def norm_back(g, xhat, rstd, gain):
    gg = g * gain
    m1 = jnp.mean(gg, axis=-1, keepdims=True)
    m2 = jnp.mean(gg * xhat, axis=-1, keepdims=True)
    return rstd * (gg - m1 - xhat * m2)


def lane_low(shape):
    return lax.broadcasted_iota(jnp.int32, shape, len(shape) - 1) < HD


def qkv_rows(x, w_ref, qkv_ref, row0, rows):
    for h in range(2):
        n = qkv_ref.shape[2]
        qkv_ref[h, pl.ds(row0, rows), :] = mm(x, w_ref[h, :, :n]).astype(BF)


def attend_rows(qkv_ref, seg_col, seg_row, p_ref, mixed_ref, row0, rows):
    half = qkv_ref.shape[2] // 3
    pairs = half // 128
    same = seg_col == seg_row
    low = lane_low((rows, 128))
    for h in range(2):
        for pp in range(pairs):
            q = qkv_ref[h, pl.ds(row0, rows), pl.ds(pp * 128, 128)]
            k = qkv_ref[h, :, pl.ds(half + pp * 128, 128)]
            v = qkv_ref[h, :, pl.ds(2 * half + pp * 128, 128)]
            outs = []
            for a in range(2):
                qa = jnp.where(low if a == 0 else ~low, q, jnp.zeros_like(q))
                s = mm(qa, k, 1, 1) * (HD ** -0.5)
                s = jnp.where(same, s, NEG)
                mx = jnp.max(s, axis=-1, keepdims=True)
                e = jnp.exp(s - mx)
                p = (e * (1.0 / jnp.sum(e, axis=-1, keepdims=True))).astype(BF)
                if p_ref is not None:
                    p_ref[(h * pairs + pp) * 2 + a, pl.ds(row0, rows), :] = p
                outs.append(mm(p, v))
            mixed_ref[pl.ds(row0, rows), pl.ds(h * half + pp * 128, 128)] = jnp.where(
                low, outs[0], outs[1]
            ).astype(BF)


def attn_out(mixed, w_ref, n_qkv):
    half = mixed.shape[1] // 2
    return mm(mixed[:, :half], w_ref[0, :, n_qkv:], 1, 1) + mm(
        mixed[:, half:], w_ref[1, :, n_qkv:], 1, 1
    )


def gelu_parts(up, want_slope):
    cdf = 0.5 * (1.0 + lax.erf(up * (0.5 ** 0.5)))
    act = up * cdf
    if not want_slope:
        return act, None
    slope = cdf + up * (jnp.exp(-0.5 * up * up) * 0.3989422804014327)
    return act, slope


def ffn_rows(x, w_ref, v_ref, act_ref, slope_ref, row0, rows, tile=512):
    acc = None
    for h in range(2):
        n = w_ref.shape[2]
        for c in range(0, n, tile):
            up = mm(x, w_ref[h, :, c : c + tile])
            act, slope = gelu_parts(up, slope_ref is not None)
            act = act.astype(BF)
            if slope_ref is not None:
                act_ref[h, pl.ds(row0, rows), c : c + tile] = act
                slope_ref[h, pl.ds(row0, rows), c : c + tile] = slope.astype(BF)
            part = mm(act, v_ref[h, c : c + tile, :])
            acc = part if acc is None else acc + part
    return acc


def ffn_back_rows(low, w_ref, v_ref, slope_ref, gup_ref, row0, rows, tile=512):
    acc = None
    for h in range(2):
        n = w_ref.shape[2]
        for c in range(0, n, tile):
            dact = mm(low, v_ref[h, c : c + tile, :], 1, 1)
            gup = (dact * slope_ref[h, pl.ds(row0, rows), c : c + tile].astype(F32)).astype(BF)
            gup_ref[h, pl.ds(row0, rows), c : c + tile] = gup
            part = mm(gup, w_ref[h, :, c : c + tile], 1, 1)
            acc = part if acc is None else acc + part
    return acc


def attn_back_core(low_ref, w_ref, qkv_ref, p_ref, dqkv_ref, n_qkv):
    half = n_qkv // 3
    pairs = half // 128
    seq = low_ref.shape[0]
    low = lane_low((seq, 128))
    for h in range(2):
        for pp in range(pairs):
            gm = mm(low_ref[...], w_ref[h, :, n_qkv + pp * 128 : n_qkv + pp * 128 + 128]).astype(BF)
            q = qkv_ref[h, :, pl.ds(pp * 128, 128)]
            k = qkv_ref[h, :, pl.ds(half + pp * 128, 128)]
            v = qkv_ref[h, :, pl.ds(2 * half + pp * 128, 128)]
            dq, dk, dv = [], [], []
            for a in range(2):
                keep = low if a == 0 else ~low
                gma = jnp.where(keep, gm, jnp.zeros_like(gm))
                pb = p_ref[(h * pairs + pp) * 2 + a, :, :]
                g = mm(gma, v, 1, 1)
                pf = pb.astype(F32)
                rs = jnp.sum(pf * g, axis=-1, keepdims=True)
                ds = (pf * (g - rs)).astype(BF)
                dq.append(mm(ds, k))
                dk.append(mm(ds, q, 0, 0))
                dv.append(mm(pb, gm, 0, 0))
            sc = HD ** -0.5
            dqkv_ref[h, :, pl.ds(pp * 128, 128)] = (jnp.where(low, dq[0], dq[1]) * sc).astype(BF)
            dqkv_ref[h, :, pl.ds(half + pp * 128, 128)] = (jnp.where(low, dk[0], dk[1]) * sc).astype(BF)
            dqkv_ref[h, :, pl.ds(2 * half + pp * 128, 128)] = jnp.where(low, dv[0], dv[1]).astype(BF)


from jax.sharding import PartitionSpec as P

MESH = pl.DeviceIdType.MESH
inv_tau = 20.0
unit_eps = 1e-06
ROWS = 256
VMEM_BYTES = 62 * 2**20


def member_rows(seg_row, count):
    return (lax.broadcasted_iota(jnp.int32, (count, seg_row.shape[1]), 0) == seg_row).astype(F32)


def split_mm(member, value):
    high = value.astype(BF)
    rest = (value - high.astype(F32)).astype(BF)
    return mm(member, high) + mm(member, rest)


def forward_kernel(
    hid, w1, w2, segc, segr, small,
    o_qkv, o_p, o_mixed, o_act, o_slope, o_xhat, o_rstd, o_x, o_w, o_v, o_pool,
    W, V, X, Y, qkv, prob, mixed, act, slope, yf, xhat, rstd,
    l_sem, ws, wr, vbs, vbr, vas, var, vfs, vfr, hs, hr, acs, acr, o_sem,
):
    s, m = lax.axis_index("section"), lax.axis_index("mp")
    last = lax.axis_size("section") - 1
    other = 1 - m
    seq = X.shape[1]
    chunks = seq // ROWS
    n_qkv = qkv.shape[3]
    va_rows = w2.shape[1]
    even = lax.rem(s, 2) == 0
    odd = lax.rem(s, 2) == 1

    barrier = pltpu.get_barrier_semaphore()
    pl.semaphore_signal(barrier, inc=1, device_id={"mp": other}, device_id_type=MESH)

    @pl.when(s > 0)
    def _():
        pl.semaphore_signal(barrier, inc=1, device_id={"section": s - 1}, device_id_type=MESH)

    @pl.when(s < last)
    def _():
        pl.semaphore_signal(barrier, inc=1, device_id={"section": s + 1}, device_id_type=MESH)

    pl.semaphore_wait(barrier, 1 + jnp.where(s > 0, 1, 0) + jnp.where(s < last, 1, 0))

    def to_core(src, dst, ss, rs):
        return pltpu.make_async_remote_copy(
            src_ref=src, dst_ref=dst, send_sem=ss, recv_sem=rs,
            device_id={"mp": other}, device_id_type=MESH,
        )

    def to_next(src, dst, ss, rs):
        return pltpu.make_async_remote_copy(
            src_ref=src, dst_ref=dst, send_sem=ss, recv_sem=rs,
            device_id={"section": s + 1}, device_id_type=MESH,
        )

    def w_far(e):
        return to_core(w1.at[e], W.at[e, m], ws.at[e], wr.at[e])

    def w_near(e):
        return pltpu.make_async_copy(w1.at[e], W.at[e, m], l_sem.at[e])

    def vb_far(e):
        return to_core(w2.at[e], V.at[e, m, pl.ds(va_rows, va_rows)], vbs.at[e], vbr.at[e])

    def vb_near(e):
        return pltpu.make_async_copy(w2.at[e], V.at[e, m, pl.ds(va_rows, va_rows)], l_sem.at[2 + e])

    def va_next(e):
        return to_next(w2.at[e], V.at[e, m, pl.ds(0, va_rows)], vas.at[e], var.at[e])

    def va_core(e):
        part = V.at[e, m, pl.ds(0, va_rows)]
        return to_core(part, part, vfs.at[e], vfr.at[e])

    def hid_far(e):
        return to_core(hid.at[other], X.at[e, pl.ds(pl.multiple_of(m * ROWS, ROWS), ROWS)], hs.at[e], hr.at[e])

    def hid_near(e):
        return pltpu.make_async_copy(
            hid.at[m], X.at[e, pl.ds(pl.multiple_of(m * ROWS, ROWS), ROWS)], l_sem.at[4 + e]
        )

    def act_next(e, c):
        rows = pl.ds(pl.multiple_of(c * ROWS, ROWS), ROWS)
        return to_next(Y.at[e, rows], X.at[e, rows], acs.at[e, c], acr.at[e, c])

    @pl.when(s == 0)
    def _():
        for e in range(2):
            hid_far(e).start()
            hid_near(e).start()

    w_far(0).start()
    w_near(0).start()

    @pl.when(odd)
    def _():
        vb_far(0).start()
        vb_near(0).start()

    @pl.when(even)
    def _():
        va_next(0).start()

    w_far(1).start()
    w_near(1).start()

    @pl.when(odd)
    def _():
        vb_far(1).start()
        vb_near(1).start()

    @pl.when(s == 0)
    def _():
        for e in range(2):
            hid_far(e).wait_recv()
            hid_near(e).wait()

    def saves(e):
        pairs = [
            (qkv.at[0], o_qkv), (prob, o_p), (mixed.at[0], o_mixed), (act, o_act), (slope, o_slope),
            (xhat, o_xhat), (rstd, o_rstd), (X.at[0], o_x), (W.at[0], o_w), (V.at[0], o_v),
        ]
        return [pltpu.make_async_copy(a, b, o_sem.at[i]) for i, (a, b) in enumerate(pairs)]

    def finish(e, rows, resid):
        y, xh, rs = norm_rows(resid, small[e, 1:2, :], small[e, 2:3, :])
        if e == 0:
            xhat[rows, :] = xh
            rstd[rows, :] = jnp.broadcast_to(rs, (ROWS, 128))
        return y

    def wait_w(e):
        w_near(e).wait()
        w_far(e).wait_recv()

    def attention(e):
        wait_w(e)

        def project(c, carry):
            @pl.when(s > 0)
            def _():
                act_next(e, c).wait_recv()

            r = pl.multiple_of(c * ROWS, ROWS)
            qkv_rows(X[e, pl.ds(r, ROWS), :], W.at[e], qkv.at[e], r, ROWS)
            return carry

        lax.fori_loop(0, chunks, project, 0)

        def attend(c, carry):
            r = pl.multiple_of(c * ROWS, ROWS)
            rows = pl.ds(r, ROWS)
            attend_rows(qkv.at[e], segc[rows, :1], segr[:1, :], prob if e == 0 else None, mixed.at[e], r, ROWS)
            branch = attn_out(mixed[e, rows, :], W.at[e], n_qkv)
            y = finish(e, rows, X[e, rows, :].astype(F32) + branch + small[e, 0:1, :])
            Y[e, rows, :] = y.astype(BF)
            act_next(e, c).start()
            return carry

        lax.fori_loop(0, chunks, attend, 0)

    def feed(e):
        wait_w(e)
        va_next(e).wait_recv()
        va_core(e).start()
        vb_near(e).wait()
        vb_far(e).wait_recv()
        va_core(e).wait_recv()

        def one(c, carry):
            act_next(e, c).wait_recv()
            r = pl.multiple_of(c * ROWS, ROWS)
            rows = pl.ds(r, ROWS)
            x = X[e, rows, :]
            if e == 0:
                branch = ffn_rows(x, W.at[e], V.at[e], act, slope, r, ROWS)
            else:
                branch = ffn_rows(x, W.at[e], V.at[e], None, None, r, ROWS)
            y = finish(e, rows, x.astype(F32) + branch + small[e, 0:1, :])

            @pl.when(s < last)
            def _():
                Y[e, rows, :] = y.astype(BF)
                act_next(e, c).start()

            @pl.when(s == last)
            def _():
                yf[rows, :] = y

            return carry

        lax.fori_loop(0, chunks, one, 0)

        @pl.when(s == last)
        def _():
            member = member_rows(segr[:1, :], 8)
            counts = jnp.sum(member, axis=-1, keepdims=True)
            o_pool[e] = split_mm(member.astype(BF), yf[...]) / jnp.maximum(counts, 1.0)

    for e in range(2):
        @pl.when(even)
        def _():
            attention(e)
            if e == 0:
                va_next(1).start()

        @pl.when(odd)
        def _():
            feed(e)

        if e == 0:
            for copy in saves(0):
                copy.start()

    for copy in saves(0):
        copy.wait()
    for e in range(2):
        w_far(e).wait_send()

        @pl.when(odd)
        def _():
            vb_far(e).wait_send()
            va_core(e).wait_send()

        @pl.when(even)
        def _():
            va_next(e).wait_send()

        @pl.when(s == 0)
        def _():
            hid_far(e).wait_send()

        @pl.when(s < last)
        def _():
            for c in range(chunks):
                act_next(e, c).wait_send()


def backward_kernel(
    i_qkv, i_p, i_mixed, i_act, i_slope, i_xhat, i_rstd, i_x, i_w, i_v, gpool, segc, small,
    o_gin, o_dw, o_dv, o_sum,
    qkv, prob, mixed, act, slope, xhat, rstd, X, W, V, G, gout, low, resid, gup, dqkv, gsplit,
    i_sem, gs, gr, is_, ir,
):
    s, m = lax.axis_index("section"), lax.axis_index("mp")
    sections = lax.axis_size("section")
    last = sections - 1
    seq = X.shape[0]
    chunks = seq // ROWS
    n_qkv = qkv.shape[2]
    even = lax.rem(s, 2) == 0
    odd = lax.rem(s, 2) == 1
    loads = [
        pltpu.make_async_copy(a, b, i_sem.at[i])
        for i, (a, b) in enumerate(
            [(i_qkv, qkv), (i_p, prob), (i_mixed, mixed), (i_act, act), (i_slope, slope),
             (i_xhat, xhat), (i_rstd, rstd), (i_x, X), (i_w, W), (i_v, V)]
        )
    ]
    for copy in loads:
        copy.start()

    barrier = pltpu.get_barrier_semaphore()
    for t in range(sections):
        for c in range(2):
            @pl.when((s != t) | (m != c))
            def _():
                pl.semaphore_signal(barrier, inc=1, device_id={"section": t, "mp": c}, device_id_type=MESH)

    pl.semaphore_wait(barrier, 2 * sections - 1)

    def grad_prev(c):
        rows = pl.ds(pl.multiple_of(c * ROWS, ROWS), ROWS)
        return pltpu.make_async_remote_copy(
            src_ref=gout.at[rows], dst_ref=G.at[rows], send_sem=gs.at[c], recv_sem=gr.at[c],
            device_id={"section": s - 1}, device_id_type=MESH,
        )

    def spread(t, c):
        return pltpu.make_async_remote_copy(
            src_ref=gsplit.at[t, pl.ds(c * ROWS, ROWS)], dst_ref=o_gin.at[m],
            send_sem=is_.at[t * 2 + c], recv_sem=ir.at[m],
            device_id={"section": t, "mp": c}, device_id_type=MESH,
        )

    for copy in loads:
        copy.wait()

    o_sum[...] = jnp.zeros_like(o_sum)

    def through_norm(c, g):
        rows = pl.ds(pl.multiple_of(c * ROWS, ROWS), ROWS)
        xh = xhat[rows, :]
        grad = norm_back(g, xh, rstd[rows, :1], small[1:2, :])
        o_sum[0:1, :] += jnp.sum(grad, axis=0, keepdims=True)
        o_sum[1:2, :] += jnp.sum(g * xh, axis=0, keepdims=True)
        o_sum[2:3, :] += jnp.sum(g, axis=0, keepdims=True)
        resid[rows, :] = grad
        low[rows, :] = grad.astype(BF)

    @pl.when(odd)
    def _():
        def one(c, carry):
            r = pl.multiple_of(c * ROWS, ROWS)
            rows = pl.ds(r, ROWS)

            @pl.when(s == last)
            def _():
                own = (lax.broadcasted_iota(jnp.int32, (ROWS, 8), 1) == segc[rows, :8]).astype(BF)
                through_norm(c, split_mm(own, gpool[...]))

            @pl.when(s < last)
            def _():
                grad_prev(c).wait_recv()
                through_norm(c, G[rows, :].astype(F32))

            dx = ffn_back_rows(low[rows, :], W, V, slope, gup, r, ROWS)
            gout[rows, :] = (resid[rows, :] + dx).astype(BF)
            grad_prev(c).start()
            return carry

        lax.fori_loop(0, chunks, one, 0)
        for h in range(2):
            o_dw[h] = mm(X[...], gup[h], 0, 0).astype(BF)
            o_dv[h] = mm(act[h], low[...], 0, 0).astype(BF)
        for c in range(chunks):
            grad_prev(c).wait_send()

    @pl.when(even)
    def _():
        def one(c, carry):
            rows = pl.ds(pl.multiple_of(c * ROWS, ROWS), ROWS)
            grad_prev(c).wait_recv()
            through_norm(c, G[rows, :].astype(F32))
            return carry

        lax.fori_loop(0, chunks, one, 0)
        attn_back_core(low, W, qkv, prob, dqkv, n_qkv)

        def back(c, carry):
            rows = pl.ds(pl.multiple_of(c * ROWS, ROWS), ROWS)
            dx = mm(dqkv[0, rows, :], W[0, :, :n_qkv], 1, 1) + mm(dqkv[1, rows, :], W[1, :, :n_qkv], 1, 1)
            grad = (resid[rows, :] + dx).astype(BF)

            @pl.when(s > 0)
            def _():
                gout[rows, :] = grad
                grad_prev(c).start()

            @pl.when(s == 0)
            def _():
                width = gsplit.shape[2]
                for t in range(sections):
                    gsplit[t, rows, :] = grad[:, t * width : (t + 1) * width]

            return carry

        lax.fori_loop(0, chunks, back, 0)

        @pl.when(s == 0)
        def _():
            for t in range(sections):
                for c in range(2):
                    if t > 0:
                        spread(t, c).start()
                    else:
                        @pl.when(m != c)
                        def _():
                            spread(t, c).start()

                        @pl.when(m == c)
                        def _():
                            pltpu.make_async_copy(
                                gsplit.at[t, pl.ds(c * ROWS, ROWS)], o_gin.at[m], is_.at[t * 2 + c]
                            ).start()

        half = n_qkv // 3
        for h in range(2):
            o_dw[h, :, :n_qkv] = mm(X[...], dqkv[h], 0, 0).astype(BF)
            o_dw[h, :, n_qkv:] = mm(low[...], mixed[:, h * half : (h + 1) * half], 0, 0).astype(BF)
            o_dv[h] = jnp.zeros_like(o_dv[h])

        @pl.when(s > 0)
        def _():
            for c in range(chunks):
                grad_prev(c).wait_send()

        @pl.when(s == 0)
        def _():
            for t in range(sections):
                for c in range(2):
                    if t > 0:
                        spread(t, c).wait_send()
                    else:
                        @pl.when(m != c)
                        def _():
                            spread(t, c).wait_send()

                        @pl.when(m == c)
                        def _():
                            pltpu.make_async_copy(
                                gsplit.at[t, pl.ds(c * ROWS, ROWS)], o_gin.at[m], is_.at[t * 2 + c]
                            ).wait()

    def arrival(r):
        return pltpu.make_async_remote_copy(
            src_ref=gsplit.at[0, pl.ds(0, ROWS)], dst_ref=o_gin.at[r],
            send_sem=is_.at[0], recv_sem=ir.at[r],
            device_id={"section": 0, "mp": r}, device_id_type=MESH,
        )

    for r in range(2):
        @pl.when((s != 0) | (m != r))
        def _():
            arrival(r).wait_recv()


def unit_rows(vectors):
    return vectors * lax.rsqrt(jnp.sum(vectors * vectors, axis=-1, keepdims=True) + unit_eps)


AXES = ("section", "dp", "mp")


def crop_head(pooled, own_partners, own_segments, queue):
    sections = lax.axis_size("section")
    rows_all = lax.axis_size("dp") * lax.axis_size("mp")
    crops = own_partners.shape[0]
    width = pooled.shape[-1]
    query = pooled[0, :crops]
    pick = (own_partners[:, None] == jnp.arange(crops, dtype=jnp.int32)[None, :]).astype(F32)
    query_own = unit_rows(query).astype(BF)
    key_low = unit_rows(pooled[1, :crops]).astype(BF)
    partner_own = jnp.dot(pick, key_low.astype(F32), precision=lax.Precision.HIGHEST).astype(BF)
    pair = lax.all_gather(jnp.stack([query_own, partner_own]), AXES, axis=0, tiled=False)
    pair = pair[(sections - 1) * rows_all :]
    query_low = pair[:, 0].reshape(-1, width)
    partner_low = pair[:, 1].reshape(-1, width)
    pos_logit = jnp.sum(query_low.astype(F32) * partner_low.astype(F32), axis=-1) * inv_tau
    queue_low = unit_rows(queue.astype(F32)).astype(BF)
    neg_logit = jnp.einsum("cd,jd->cj", query_low, queue_low, preferred_element_type=F32) * inv_tau
    neg_weight = jnp.exp(neg_logit - inv_tau)
    partial_total = jnp.sum(neg_weight, axis=-1)
    partial_pull = split_right(neg_weight, queue_low)
    both = jnp.concatenate(
        [partial_pull, jnp.broadcast_to(partial_total[:, None], (partial_total.shape[0], 128))], axis=1
    )
    both = lax.psum(both, AXES)
    queue_total, queue_pull = both[:, width], both[:, :width]
    denominator = jnp.exp(pos_logit - inv_tau) + queue_total
    log_total = inv_tau + jnp.log(denominator)
    loss_value = jnp.mean(log_total - pos_logit)
    start = (lax.axis_index("dp") * lax.axis_size("mp") + lax.axis_index("mp")) * crops

    def own(value):
        return lax.dynamic_slice_in_dim(value, start, crops, 0)

    own_denominator = own(denominator)
    pos_weight = own(jnp.exp(pos_logit - inv_tau)) / own_denominator
    grad_query = (
        own(queue_pull) / own_denominator[:, None]
        + (pos_weight - 1.0)[:, None] * own(partner_low).astype(F32)
    ) * (inv_tau / query_low.shape[0])
    grad_pooled = jax.vjp(unit_rows, query)[1](grad_query)[0]
    counts = jnp.sum((own_segments[:, None] == jnp.arange(crops, dtype=jnp.int32)).astype(F32), axis=0)
    return loss_value, jnp.pad(grad_pooled / counts[:, None], ((0, 8 - crops), (0, 0)))


def split_right(weights, values):
    high = weights.astype(BF)
    rest = (weights - high.astype(F32)).astype(BF)
    return jnp.dot(high, values, preferred_element_type=F32) + jnp.dot(
        rest, values, preferred_element_type=F32
    )


def local(
    hidden_in, segments, partners, queue, first_weight, second_weight, out_bias, ln_gain, ln_bias
):
    m = lax.axis_index("mp")
    width = hidden_in.shape[-1]
    seq = segments.shape[1]
    w1 = first_weight.reshape(2, width, -1)
    w2 = second_weight.reshape(2, -1, width)
    cols = w1.shape[2]
    n_qkv = cols // 4 * 3
    heads = 2 * (cols // 4) // HD
    own_segments = lax.dynamic_index_in_dim(segments, m, 0, keepdims=False)
    own_partners = lax.dynamic_index_in_dim(partners, m, 0, keepdims=False)
    segc = jnp.broadcast_to(own_segments[:, None], (seq, 128))
    segr = jnp.broadcast_to(own_segments[None, :], (8, seq))
    small = jnp.stack([out_bias[:, 0], ln_gain[:, 0], ln_bias[:, 0]], axis=1)
    small = jnp.pad(small, ((0, 0), (0, 5), (0, 0)))
    anyspace = pl.BlockSpec(memory_space=pl.ANY)
    vmem = pl.BlockSpec(memory_space=pltpu.VMEM)
    shape = jax.ShapeDtypeStruct
    dma = pltpu.SemaphoreType.DMA
    saved = [
        shape((2, seq, n_qkv), BF), shape((heads, seq, seq), BF), shape((seq, width), BF),
        shape((2, seq, cols), BF), shape((2, seq, cols), BF), shape((seq, width), F32),
        shape((seq, 128), F32), shape((seq, width), BF), shape((2, width, cols), BF),
        shape((2, cols, width), BF),
    ]
    *kept, pooled = pl.pallas_call(
        forward_kernel,
        out_shape=saved + [shape((2, 8, width), F32)],
        in_specs=[anyspace] * 3 + [vmem] * 3,
        out_specs=[anyspace] * 10 + [vmem],
        scratch_shapes=[
            pltpu.VMEM((2, 2, width, cols), BF), pltpu.VMEM((2, 2, cols, width), BF),
            pltpu.VMEM((2, seq, width), BF), pltpu.VMEM((2, seq, width), BF),
            pltpu.VMEM((2, 2, seq, n_qkv), BF), pltpu.VMEM((heads, seq, seq), BF),
            pltpu.VMEM((2, seq, width), BF), pltpu.VMEM((2, seq, cols), BF),
            pltpu.VMEM((2, seq, cols), BF), pltpu.VMEM((seq, width), F32),
            pltpu.VMEM((seq, width), F32), pltpu.VMEM((seq, 128), F32),
            dma((6,)), dma((2,)), dma((2,)), dma((2,)), dma((2,)), dma((2,)), dma((2,)), dma((2,)), dma((2,)),
            dma((2,)), dma((2,)), dma((2, seq // ROWS)), dma((2, seq // ROWS)), dma((10,)),
        ],
        compiler_params=pltpu.CompilerParams(
            collective_id=0, has_side_effects=True, vmem_limit_bytes=VMEM_BYTES
        ),
        name="forward",
    )(hidden_in, w1, w2, segc, segr, small)
    loss_value, grad_pooled = crop_head(pooled, own_partners, own_segments, queue)
    half_width = width // lax.axis_size("section")
    gin, dw, dv, sums = pl.pallas_call(
        backward_kernel,
        out_shape=[
            shape((2, seq // 2, half_width), BF), shape((2, width, cols), BF),
            shape((2, cols, width), BF), shape((8, width), F32),
        ],
        in_specs=[anyspace] * 10 + [vmem] * 3,
        out_specs=[vmem] * 4,
        scratch_shapes=[pltpu.VMEM(a.shape, a.dtype) for a in saved]
        + [
            pltpu.VMEM((seq, width), BF), pltpu.VMEM((seq, width), BF), pltpu.VMEM((seq, width), BF),
            pltpu.VMEM((seq, width), F32), pltpu.VMEM((2, seq, cols), BF), pltpu.VMEM((2, seq, n_qkv), BF),
            pltpu.VMEM((lax.axis_size("section"), seq, half_width), BF),
            dma((10,)), dma((seq // ROWS,)), dma((seq // ROWS,)), dma((2 * lax.axis_size("section"),)), dma((2,)),
        ],
        compiler_params=pltpu.CompilerParams(
            collective_id=1, has_side_effects=True, vmem_limit_bytes=VMEM_BYTES
        ),
        name="backward",
    )(*kept, grad_pooled, segc, small[0])
    va_rows = w2.shape[1]
    returned = lax.ppermute(
        dv[:, :va_rows], "section", [(i + 1, i) for i in range(lax.axis_size("section") - 1)]
    )
    section_kind = lax.axis_index("section") % 2
    grad_second = jnp.where(section_kind == 0, returned, dv[:, va_rows:])
    flat = jnp.concatenate([dw.reshape(2, -1), grad_second.reshape(2, -1)], axis=1)
    mine = lax.psum_scatter(flat, "mp", scatter_dimension=0, tiled=False)
    total = lax.psum(mine, "dp").astype(F32)
    grad_first = total[: width * cols].reshape(width, 4, -1)
    grad_second = total[width * cols :].reshape(second_weight.shape[2:])
    sums = lax.psum(sums, ("dp", "mp"))
    return (
        loss_value, gin, grad_first[None], grad_second[None], sums[0:1], sums[1:2], sums[2:3],
    )


def solution(mesh):
    in_specs = (
        P("dp", "mp", None), P("dp", None), P("dp", None), P(("section", "dp", "mp"), None),
        P(None, "section", None, None, "mp"), P(None, "section", None, "mp", None),
        P(None, "section", None), P(None, "section", None), P(None, "section", None),
    )
    out_specs = (
        P(), P("dp", "mp", "section"), P("section", None, None, "mp"), P("section", None, "mp", None),
        P("section", None), P("section", None), P("section", None),
    )
    return jax.shard_map(local, mesh=mesh, in_specs=in_specs, out_specs=out_specs, check_vma=False)
```

```python
import functools
import jax
import jax.numpy as jnp
from jax import lax
from jax.experimental import pallas as pl
from jax.experimental.pallas import tpu as pltpu

F32 = jnp.float32
BF = jnp.bfloat16
HD = 64
NEG = -1e30
LN_EPS = 1e-12


def mm(a, b, ca=1, cb=0):
    return lax.dot_general(a, b, (((ca,), (cb,)), ((), ())), preferred_element_type=F32)


def norm_rows(resid, gain, shift):
    centre = resid - jnp.mean(resid, axis=-1, keepdims=True)
    spread = jnp.mean(centre * centre, axis=-1, keepdims=True)
    rstd = lax.rsqrt(spread + LN_EPS)
    xhat = centre * rstd
    return xhat * gain + shift, xhat, rstd


def norm_back(g, xhat, rstd, gain):
    gg = g * gain
    m1 = jnp.mean(gg, axis=-1, keepdims=True)
    m2 = jnp.mean(gg * xhat, axis=-1, keepdims=True)
    return rstd * (gg - m1 - xhat * m2)


def lane_low(shape):
    return lax.broadcasted_iota(jnp.int32, shape, len(shape) - 1) < HD


def qkv_rows(x, w_ref, qkv_ref, row0, rows):
    for h in range(2):
        n = qkv_ref.shape[2]
        qkv_ref[h, pl.ds(row0, rows), :] = mm(x, w_ref[h, :, :n]).astype(BF)


def attend_rows(qkv_ref, seg_col, seg_row, p_ref, mixed_ref, row0, rows):
    half = qkv_ref.shape[2] // 3
    pairs = half // 128
    same = seg_col == seg_row
    low = lane_low((rows, 128))
    for h in range(2):
        for pp in range(pairs):
            q = qkv_ref[h, pl.ds(row0, rows), pl.ds(pp * 128, 128)]
            k = qkv_ref[h, :, pl.ds(half + pp * 128, 128)]
            v = qkv_ref[h, :, pl.ds(2 * half + pp * 128, 128)]
            outs = []
            for a in range(2):
                qa = jnp.where(low if a == 0 else ~low, q, jnp.zeros_like(q))
                s = mm(qa, k, 1, 1) * (HD ** -0.5)
                s = jnp.where(same, s, NEG)
                mx = jnp.max(s, axis=-1, keepdims=True)
                e = jnp.exp(s - mx)
                p = (e * (1.0 / jnp.sum(e, axis=-1, keepdims=True))).astype(BF)
                if p_ref is not None:
                    p_ref[(h * pairs + pp) * 2 + a, pl.ds(row0, rows), :] = p
                outs.append(mm(p, v))
            mixed_ref[pl.ds(row0, rows), pl.ds(h * half + pp * 128, 128)] = jnp.where(
                low, outs[0], outs[1]
            ).astype(BF)


def attn_out(mixed, w_ref, n_qkv):
    half = mixed.shape[1] // 2
    return mm(mixed[:, :half], w_ref[0, :, n_qkv:], 1, 1) + mm(
        mixed[:, half:], w_ref[1, :, n_qkv:], 1, 1
    )


def gelu_parts(up, want_slope):
    cdf = 0.5 * (1.0 + lax.erf(up * (0.5 ** 0.5)))
    act = up * cdf
    if not want_slope:
        return act, None
    slope = cdf + up * (jnp.exp(-0.5 * up * up) * 0.3989422804014327)
    return act, slope


def ffn_rows(x, w_ref, v_ref, keep_ref, row0, rows, tile=512):
    acc = None
    for h in range(2):
        n = w_ref.shape[2]
        for c in range(0, n, tile):
            up = mm(x, w_ref[h, :, c : c + tile])
            act, slope = gelu_parts(up, keep_ref is not None)
            act = act.astype(BF)
            if keep_ref is not None:
                at = (h * n + c) // tile
                keep_ref[at, pl.ds(row0, rows), :] = act
                keep_ref[keep_ref.shape[0] // 2 + at, pl.ds(row0, rows), :] = slope.astype(BF)
            part = mm(act, v_ref[h, c : c + tile, :])
            acc = part if acc is None else acc + part
    return acc


def ffn_back_rows(low, w_ref, v_ref, keep_ref, gup_ref, row0, rows, tile=512):
    acc = None
    for h in range(2):
        n = w_ref.shape[2]
        for c in range(0, n, tile):
            dact = mm(low, v_ref[h, c : c + tile, :], 1, 1)
            at = keep_ref.shape[0] // 2 + (h * n + c) // tile
            gup = (dact * keep_ref[at, pl.ds(row0, rows), :].astype(F32)).astype(BF)
            gup_ref[h, pl.ds(row0, rows), c : c + tile] = gup
            part = mm(gup, w_ref[h, :, c : c + tile], 1, 1)
            acc = part if acc is None else acc + part
    return acc


def attn_back_core(low_ref, w_ref, qkv_ref, p_ref, dqkv_ref, n_qkv):
    half = n_qkv // 3
    pairs = half // 128
    seq = low_ref.shape[0]
    low = lane_low((seq, 128))
    for h in range(2):
        for pp in range(pairs):
            gm = mm(low_ref[...], w_ref[h, :, n_qkv + pp * 128 : n_qkv + pp * 128 + 128]).astype(BF)
            q = qkv_ref[h, :, pl.ds(pp * 128, 128)]
            k = qkv_ref[h, :, pl.ds(half + pp * 128, 128)]
            v = qkv_ref[h, :, pl.ds(2 * half + pp * 128, 128)]
            dq, dk, dv = [], [], []
            for a in range(2):
                keep = low if a == 0 else ~low
                gma = jnp.where(keep, gm, jnp.zeros_like(gm))
                pb = p_ref[(h * pairs + pp) * 2 + a, :, :]
                g = mm(gma, v, 1, 1)
                pf = pb.astype(F32)
                rs = jnp.sum(pf * g, axis=-1, keepdims=True)
                ds = (pf * (g - rs)).astype(BF)
                dq.append(mm(ds, k))
                dk.append(mm(ds, q, 0, 0))
                dv.append(mm(pb, gm, 0, 0))
            sc = HD ** -0.5
            dqkv_ref[h, :, pl.ds(pp * 128, 128)] = (jnp.where(low, dq[0], dq[1]) * sc).astype(BF)
            dqkv_ref[h, :, pl.ds(half + pp * 128, 128)] = (jnp.where(low, dk[0], dk[1]) * sc).astype(BF)
            dqkv_ref[h, :, pl.ds(2 * half + pp * 128, 128)] = jnp.where(low, dv[0], dv[1]).astype(BF)


from jax.sharding import PartitionSpec as P

MESH = pl.DeviceIdType.MESH
inv_tau = 20.0
unit_eps = 1e-06
ROWS = 256
VMEM_BYTES = 62 * 2**20


def member_rows(seg_row, count):
    return (lax.broadcasted_iota(jnp.int32, (count, seg_row.shape[1]), 0) == seg_row).astype(F32)


def split_mm(member, value):
    high = value.astype(BF)
    rest = (value - high.astype(F32)).astype(BF)
    return mm(member, high) + mm(member, rest)


def forward_kernel(
    hid, w1, w2, segc, segr, small,
    o_qkv, o_p, o_mixed, o_xhat, o_rstd, o_x, o_w, o_v, o_pool,
    W, V, X, Y, qkv, prob, mixed, yf, xhat, rstd,
    l_sem, ws, wr, vbs, vbr, vas, var, vfs, vfr, hs, hr, acs, acr, o_sem,
):
    s, m = lax.axis_index("section"), lax.axis_index("mp")
    last = lax.axis_size("section") - 1
    other = 1 - m
    seq = X.shape[1]
    chunks = seq // ROWS
    n_qkv = qkv.shape[3]
    va_rows = w2.shape[1]
    even = lax.rem(s, 2) == 0
    odd = lax.rem(s, 2) == 1

    barrier = pltpu.get_barrier_semaphore()
    pl.semaphore_signal(barrier, inc=1, device_id={"mp": other}, device_id_type=MESH)

    @pl.when(s > 0)
    def _():
        pl.semaphore_signal(barrier, inc=1, device_id={"section": s - 1}, device_id_type=MESH)

    @pl.when(s < last)
    def _():
        pl.semaphore_signal(barrier, inc=1, device_id={"section": s + 1}, device_id_type=MESH)

    pl.semaphore_wait(barrier, 1 + jnp.where(s > 0, 1, 0) + jnp.where(s < last, 1, 0))

    def to_core(src, dst, ss, rs):
        return pltpu.make_async_remote_copy(
            src_ref=src, dst_ref=dst, send_sem=ss, recv_sem=rs,
            device_id={"mp": other}, device_id_type=MESH,
        )

    def to_next(src, dst, ss, rs):
        return pltpu.make_async_remote_copy(
            src_ref=src, dst_ref=dst, send_sem=ss, recv_sem=rs,
            device_id={"section": s + 1}, device_id_type=MESH,
        )

    def w_far(e):
        return to_core(w1.at[e], W.at[e, m], ws.at[e], wr.at[e])

    def w_near(e):
        return pltpu.make_async_copy(w1.at[e], W.at[e, m], l_sem.at[e])

    def vb_far(e):
        return to_core(w2.at[e], V.at[e, m, pl.ds(va_rows, va_rows)], vbs.at[e], vbr.at[e])

    def vb_near(e):
        return pltpu.make_async_copy(w2.at[e], V.at[e, m, pl.ds(va_rows, va_rows)], l_sem.at[2 + e])

    def va_next(e):
        return to_next(w2.at[e], V.at[e, m, pl.ds(0, va_rows)], vas.at[e], var.at[e])

    def va_core(e):
        part = V.at[e, m, pl.ds(0, va_rows)]
        return to_core(part, part, vfs.at[e], vfr.at[e])

    def hid_far(e):
        return to_core(hid.at[other], X.at[e, pl.ds(pl.multiple_of(m * ROWS, ROWS), ROWS)], hs.at[e], hr.at[e])

    def hid_near(e):
        return pltpu.make_async_copy(
            hid.at[m], X.at[e, pl.ds(pl.multiple_of(m * ROWS, ROWS), ROWS)], l_sem.at[4 + e]
        )

    def act_next(e, c):
        rows = pl.ds(pl.multiple_of(c * ROWS, ROWS), ROWS)
        return to_next(Y.at[e, rows], X.at[e, rows], acs.at[e, c], acr.at[e, c])

    @pl.when(s == 0)
    def _():
        for e in range(2):
            hid_far(e).start()
            hid_near(e).start()

    w_far(0).start()
    w_near(0).start()

    @pl.when(odd)
    def _():
        vb_far(0).start()
        vb_near(0).start()

    @pl.when(even)
    def _():
        va_next(0).start()

    w_far(1).start()
    w_near(1).start()

    @pl.when(odd)
    def _():
        vb_far(1).start()
        vb_near(1).start()

    @pl.when(s == 0)
    def _():
        for e in range(2):
            hid_far(e).wait_recv()
            hid_near(e).wait()

    def saves(e):
        pairs = [
            (qkv.at[0], o_qkv), (prob, o_p), (mixed.at[0], o_mixed),
            (xhat, o_xhat), (rstd, o_rstd), (X.at[0], o_x), (W.at[0], o_w), (V.at[0], o_v),
        ]
        return [pltpu.make_async_copy(a, b, o_sem.at[i]) for i, (a, b) in enumerate(pairs)]

    def finish(e, rows, resid):
        y, xh, rs = norm_rows(resid, small[e, 1:2, :], small[e, 2:3, :])
        if e == 0:
            xhat[rows, :] = xh
            rstd[rows, :] = jnp.broadcast_to(rs, (ROWS, 128))
        return y

    def wait_w(e):
        w_near(e).wait()
        w_far(e).wait_recv()

    def attention(e):
        wait_w(e)

        def project(c, carry):
            @pl.when(s > 0)
            def _():
                act_next(e, c).wait_recv()

            r = pl.multiple_of(c * ROWS, ROWS)
            qkv_rows(X[e, pl.ds(r, ROWS), :], W.at[e], qkv.at[e], r, ROWS)
            return carry

        lax.fori_loop(0, chunks, project, 0)

        def attend(c, carry):
            r = pl.multiple_of(c * ROWS, ROWS)
            rows = pl.ds(r, ROWS)
            attend_rows(qkv.at[e], segc[rows, :1], segr[:1, :], prob if e == 0 else None, mixed.at[e], r, ROWS)
            branch = attn_out(mixed[e, rows, :], W.at[e], n_qkv)
            y = finish(e, rows, X[e, rows, :].astype(F32) + branch + small[e, 0:1, :])
            Y[e, rows, :] = y.astype(BF)
            act_next(e, c).start()
            return carry

        lax.fori_loop(0, chunks, attend, 0)

    def feed(e):
        wait_w(e)
        va_next(e).wait_recv()
        va_core(e).start()
        vb_near(e).wait()
        vb_far(e).wait_recv()
        va_core(e).wait_recv()

        def one(c, carry):
            act_next(e, c).wait_recv()
            r = pl.multiple_of(c * ROWS, ROWS)
            rows = pl.ds(r, ROWS)
            x = X[e, rows, :]
            branch = ffn_rows(x, W.at[e], V.at[e], prob if e == 0 else None, r, ROWS)
            y = finish(e, rows, x.astype(F32) + branch + small[e, 0:1, :])

            @pl.when(s < last)
            def _():
                Y[e, rows, :] = y.astype(BF)
                act_next(e, c).start()

            @pl.when(s == last)
            def _():
                yf[rows, :] = y

            return carry

        lax.fori_loop(0, chunks, one, 0)

        @pl.when(s == last)
        def _():
            member = member_rows(segr[:1, :], 8)
            counts = jnp.sum(member, axis=-1, keepdims=True)
            o_pool[e] = split_mm(member.astype(BF), yf[...]) / jnp.maximum(counts, 1.0)

    for e in range(2):
        @pl.when(even)
        def _():
            attention(e)
            if e == 0:
                va_next(1).start()

        @pl.when(odd)
        def _():
            feed(e)

        if e == 0:
            for copy in saves(0):
                copy.start()

    for copy in saves(0):
        copy.wait()
    for e in range(2):
        w_far(e).wait_send()

        @pl.when(odd)
        def _():
            vb_far(e).wait_send()
            va_core(e).wait_send()

        @pl.when(even)
        def _():
            va_next(e).wait_send()

        @pl.when(s == 0)
        def _():
            hid_far(e).wait_send()

        @pl.when(s < last)
        def _():
            for c in range(chunks):
                act_next(e, c).wait_send()


PIECES = 16
WAIT_ROOT = 2
LAG = 3


def backward_kernel(
    i_qkv, i_p, i_mixed, i_xhat, i_rstd, i_x, i_w, i_v, gpool, segc, small,
    o_gin, o_red, o_sum,
    qkv, prob, mixed, xhat, rstd, X, W, V, G, gout, low, resid, gup, gsplit,
    mine, give, taken, part, sums,
    i_sem, gs, gr, is_, ir, xs, xr, ps, pr, fs, fr, vs, vr, ss, sr,
):
    s, d, m = lax.axis_index("section"), lax.axis_index("dp"), lax.axis_index("mp")
    sections, planes = lax.axis_size("section"), lax.axis_size("dp")
    last = sections - 1
    other = 1 - m
    seq, width = X.shape
    chunks = seq // ROWS
    n_qkv = qkv.shape[2]
    cols = W.shape[2]
    even = lax.rem(s, 2) == 0
    odd = lax.rem(s, 2) == 1
    loads = [
        pltpu.make_async_copy(a, b, i_sem.at[i])
        for i, (a, b) in enumerate(
            [(i_xhat, xhat), (i_rstd, rstd), (i_v, V), (i_p, prob), (i_w, W), (i_x, X),
             (i_qkv, qkv), (i_mixed, mixed)]
        )
    ]
    for copy in loads:
        copy.start()

    barrier = pltpu.get_barrier_semaphore()
    for t in range(sections):
        for c in range(2):
            @pl.when((s != t) | (m != c))
            def _():
                pl.semaphore_signal(barrier, inc=1, device_id={"section": t, "mp": c}, device_id_type=MESH)

    def greet(i, carry):
        to = lax.rem(d + 1 + i, planes)
        for c in range(2):
            pl.semaphore_signal(barrier, inc=1, device_id={"dp": to, "mp": c}, device_id_type=MESH)
        return carry

    lax.fori_loop(0, planes - 1, greet, 0)
    pl.semaphore_wait(barrier, 2 * sections - 1 + 2 * (planes - 1))

    def remote(src, dst, send, recv, **to):
        return pltpu.make_async_remote_copy(
            src_ref=src, dst_ref=dst, send_sem=send, recv_sem=recv, device_id=to, device_id_type=MESH
        )

    def grad_prev(c):
        rows = pl.ds(pl.multiple_of(c * ROWS, ROWS), ROWS)
        return remote(gout.at[rows], G.at[rows], gs.at[c], gr.at[c], section=s - 1)

    def spread(t, c):
        return remote(
            gsplit.at[t, pl.ds(c * ROWS, ROWS)], o_gin.at[m], is_.at[t * 2 + c], ir.at[m], section=t, mp=c
        )

    for copy in loads:
        copy.wait()

    own_slot = d * 2 + m
    sums[own_slot] = jnp.zeros_like(sums[own_slot])

    def through_norm(c, g):
        rows = pl.ds(pl.multiple_of(c * ROWS, ROWS), ROWS)
        xh = xhat[rows, :]
        grad = norm_back(g, xh, rstd[rows, :1], small[1:2, :])
        sums[own_slot, 0:1, :] += jnp.sum(grad, axis=0, keepdims=True)
        sums[own_slot, 1:2, :] += jnp.sum(g * xh, axis=0, keepdims=True)
        sums[own_slot, 2:3, :] += jnp.sum(g, axis=0, keepdims=True)
        resid[rows, :] = grad
        low[rows, :] = grad.astype(BF)

    def exchange(kind):
        return remote(give.at[kind], taken.at[kind], xs.at[kind], xr.at[kind], mp=other)

    def sum_to(i):
        to = lax.rem(own_slot + 1 + i, 2 * planes)
        return remote(
            sums.at[own_slot], sums.at[own_slot], ss.at[i], sr.at[own_slot], dp=to // 2, mp=lax.rem(to, 2)
        )

    def sum_from(i):
        slot = lax.rem(own_slot + 1 + i, 2 * planes)
        return remote(sums.at[slot], sums.at[slot], ss.at[i], sr.at[slot], dp=slot // 2, mp=lax.rem(slot, 2))

    def start_sums():
        def one(i, carry):
            sum_to(i).start()
            return carry

        lax.fori_loop(0, 2 * planes - 1, one, 0)

    @pl.when(odd)
    def _():
        def one(c, carry):
            r = pl.multiple_of(c * ROWS, ROWS)
            rows = pl.ds(r, ROWS)

            @pl.when(s == last)
            def _():
                own = (lax.broadcasted_iota(jnp.int32, (ROWS, 8), 1) == segc[rows, :8]).astype(BF)
                through_norm(c, split_mm(own, gpool[...]))

            @pl.when(s < last)
            def _():
                grad_prev(c).wait_recv()
                through_norm(c, G[rows, :].astype(F32))

            dx = ffn_back_rows(low[rows, :], W, V, prob, gup, r, ROWS)
            gout[rows, :] = (resid[rows, :] + dx).astype(BF)
            grad_prev(c).start()
            return carry

        lax.fori_loop(0, chunks, one, 0)
        start_sums()
        unit = 256
        for h, out in ((other, give), (m, mine)):
            for c in range(cols // unit):
                act = prob[h * (cols // 512) + c * unit // 512, :, c * unit % 512 : c * unit % 512 + unit]
                r, q = c * unit % width, c * unit // width * width
                out[0, r : r + unit, q : q + width] = mm(act, low[...], 0, 0).astype(BF)
            if out is give:
                exchange(0).start()
        for h, out in ((other, give), (m, mine)):
            for c in range(0, cols, 512):
                out[1, :, c : c + 512] = mm(X[...], gup[h, :, c : c + 512], 0, 0).astype(BF)
            if out is give:
                exchange(1).start()
        exchange(0).wait_recv()

    @pl.when(even)
    def _():
        def one(c, carry):
            rows = pl.ds(pl.multiple_of(c * ROWS, ROWS), ROWS)
            grad_prev(c).wait_recv()
            through_norm(c, G[rows, :].astype(F32))
            return carry

        lax.fori_loop(0, chunks, one, 0)
        start_sums()
        attn_back_core(low, W, qkv, prob, gup, n_qkv)

        def back(c, carry):
            rows = pl.ds(pl.multiple_of(c * ROWS, ROWS), ROWS)
            dx = mm(gup[0, rows, :n_qkv], W[0, :, :n_qkv], 1, 1) + mm(
                gup[1, rows, :n_qkv], W[1, :, :n_qkv], 1, 1
            )
            grad = (resid[rows, :] + dx).astype(BF)

            @pl.when(s > 0)
            def _():
                gout[rows, :] = grad
                grad_prev(c).start()

            @pl.when(s == 0)
            def _():
                part_width = gsplit.shape[2]
                for t in range(sections):
                    gsplit[t, rows, :] = grad[:, t * part_width : (t + 1) * part_width]

            return carry

        lax.fori_loop(0, chunks, back, 0)

        @pl.when(s == 0)
        def _():
            for t in range(sections):
                for c in range(2):
                    if t > 0:
                        spread(t, c).start()
                    else:
                        @pl.when(m != c)
                        def _():
                            spread(t, c).start()

                        @pl.when(m == c)
                        def _():
                            pltpu.make_async_copy(
                                gsplit.at[t, pl.ds(c * ROWS, ROWS)], o_gin.at[m], is_.at[t * 2 + c]
                            ).start()

        half = n_qkv // 3
        for h, out in ((other, give), (m, mine)):
            for c in range(0, n_qkv, half):
                out[1, :, c : c + half] = mm(X[...], gup[h, :, c : c + half], 0, 0).astype(BF)
            for k in range(2):
                @pl.when(h == k)
                def _():
                    out[1, :, n_qkv:] = mm(low[...], mixed[:, k * half : (k + 1) * half], 0, 0).astype(BF)
            if out is give:
                exchange(1).start()

    exchange(1).wait_recv()

    step_rows = width // PIECES
    root_a, root_b = (planes - 1) // 2, planes // 2
    first = jnp.where(odd, 0, PIECES)
    total = 2 * PIECES
    lag = WAIT_ROOT + LAG * jnp.maximum(root_b - d, d - root_a)

    def place(i):
        kind = i // PIECES
        rows = pl.ds(pl.multiple_of(lax.rem(i, PIECES) * step_rows, step_rows), step_rows)
        root = jnp.where(lax.rem(i, 2) == 0, root_a, root_b)
        return kind, rows, root

    def part_right(i):
        kind, rows, _ = place(i)
        return remote(mine.at[kind, rows], part.at[0, kind, rows], ps.at[i], pr.at[0, i], dp=d + 1)

    def part_left(i):
        kind, rows, _ = place(i)
        return remote(mine.at[kind, rows], part.at[1, kind, rows], ps.at[i], pr.at[1, i], dp=d - 1)

    def whole(i, side, src):
        kind, rows, _ = place(i)
        return remote(src.at[kind, rows], o_red.at[kind, rows], fs.at[side, i], fr.at[i], dp=d + (1 if side else -1))

    def keep_root(i):
        kind, rows, _ = place(i)
        return pltpu.make_async_copy(mine.at[kind, rows], o_red.at[kind, rows], fr.at[i])

    def down_prev(i):
        _, rows, _ = place(i)
        return remote(
            o_red.at[0, rows, pl.ds(0, width)], o_red.at[0, rows, pl.ds(width, width)],
            vs.at[i], vr.at[i], section=s - 1,
        )

    def add(i, *sides):
        kind, rows, _ = place(i)
        value = mine[kind, rows, :].astype(F32) + taken[kind, rows, :].astype(F32)
        for side in sides:
            value = value + part[side, kind, rows, :].astype(F32)
        mine[kind, rows, :] = value.astype(BF)

    def pieces(i, carry):
        root = place(i)[2]

        @pl.when((i < total) & (d < root))
        def _():
            @pl.when(d > 0)
            def _():
                part_right(i).wait_recv()
                add(i, 0)

            @pl.when(d == 0)
            def _():
                add(i)

            part_right(i).start()

        @pl.when((i < total) & (d > root))
        def _():
            @pl.when(d < planes - 1)
            def _():
                part_left(i).wait_recv()
                add(i, 1)

            @pl.when(d == planes - 1)
            def _():
                add(i)

            part_left(i).start()

        k = i - WAIT_ROOT

        @pl.when((k >= first) & (k < total) & (d == place(k)[2]))
        def _():
            part_right(k).wait_recv()
            part_left(k).wait_recv()
            add(k, 0, 1)
            keep_root(k).start()
            whole(k, 0, mine).start()
            whole(k, 1, mine).start()

        @pl.when(i >= first + lag)
        def _():
            j = i - lag
            kind, _, root = place(j)
            keep_root(j).wait()

            @pl.when((d < root) & (d > 0))
            def _():
                whole(j, 0, o_red).start()

            @pl.when((d > root) & (d < planes - 1))
            def _():
                whole(j, 1, o_red).start()

            @pl.when(kind == 0)
            def _():
                down_prev(j).start()

        return carry

    lax.fori_loop(first, total + lag, pieces, 0)

    def settle(i, carry):
        kind, rows, root = place(i)

        @pl.when(d != root)
        def _():
            part_right(i).wait_send()

        @pl.when((d <= root) & (d > 0))
        def _():
            whole(i, 0, mine).wait_send()

        @pl.when((d >= root) & (d < planes - 1))
        def _():
            whole(i, 1, mine).wait_send()

        @pl.when(kind == 0)
        def _():
            down_prev(i).wait_send()

        return carry

    lax.fori_loop(first, total, settle, 0)

    @pl.when(even)
    def _():
        def arrive(i, carry):
            down_prev(i).wait_recv()
            return carry

        lax.fori_loop(0, PIECES, arrive, 0)

    @pl.when(odd)
    def _():
        exchange(0).wait_send()

    exchange(1).wait_send()

    @pl.when(s > 0)
    def _():
        for c in range(chunks):
            grad_prev(c).wait_send()

    @pl.when(s == 0)
    def _():
        for t in range(sections):
            for c in range(2):
                if t > 0:
                    spread(t, c).wait_send()
                else:
                    @pl.when(m != c)
                    def _():
                        spread(t, c).wait_send()

                    @pl.when(m == c)
                    def _():
                        pltpu.make_async_copy(
                            gsplit.at[t, pl.ds(c * ROWS, ROWS)], o_gin.at[m], is_.at[t * 2 + c]
                        ).wait()

    def arrival(r):
        return remote(gsplit.at[0, pl.ds(0, ROWS)], o_gin.at[r], is_.at[0], ir.at[r], section=0, mp=r)

    for r in range(2):
        @pl.when((s != 0) | (m != r))
        def _():
            arrival(r).wait_recv()

    def sums_in(i, carry):
        sum_from(i).wait_recv()
        sum_to(i).wait_send()
        return carry

    lax.fori_loop(0, 2 * planes - 1, sums_in, 0)
    o_sum[...] = jnp.sum(sums[...], axis=0)


def unit_rows(vectors):
    return vectors * lax.rsqrt(jnp.sum(vectors * vectors, axis=-1, keepdims=True) + unit_eps)


AXES = ("section", "dp", "mp")


def crop_head(pooled, own_partners, own_segments, queue):
    sections = lax.axis_size("section")
    rows_all = lax.axis_size("dp") * lax.axis_size("mp")
    crops = own_partners.shape[0]
    width = pooled.shape[-1]
    query = pooled[0, :crops]
    pick = (own_partners[:, None] == jnp.arange(crops, dtype=jnp.int32)[None, :]).astype(F32)
    query_own = unit_rows(query).astype(BF)
    key_low = unit_rows(pooled[1, :crops]).astype(BF)
    partner_own = jnp.dot(pick, key_low.astype(F32), precision=lax.Precision.HIGHEST).astype(BF)
    pair = lax.all_gather(jnp.stack([query_own, partner_own]), AXES, axis=0, tiled=False)
    pair = pair[(sections - 1) * rows_all :]
    query_low = pair[:, 0].reshape(-1, width)
    partner_low = pair[:, 1].reshape(-1, width)
    pos_logit = jnp.sum(query_low.astype(F32) * partner_low.astype(F32), axis=-1) * inv_tau
    queue_low = unit_rows(queue.astype(F32)).astype(BF)
    neg_logit = jnp.einsum("cd,jd->cj", query_low, queue_low, preferred_element_type=F32) * inv_tau
    neg_weight = jnp.exp(neg_logit - inv_tau)
    partial_total = jnp.sum(neg_weight, axis=-1)
    partial_pull = split_right(neg_weight, queue_low)
    both = jnp.concatenate(
        [partial_pull, jnp.broadcast_to(partial_total[:, None], (partial_total.shape[0], 128))], axis=1
    )
    both = lax.psum(both, AXES)
    queue_total, queue_pull = both[:, width], both[:, :width]
    denominator = jnp.exp(pos_logit - inv_tau) + queue_total
    log_total = inv_tau + jnp.log(denominator)
    loss_value = jnp.mean(log_total - pos_logit)
    start = (lax.axis_index("dp") * lax.axis_size("mp") + lax.axis_index("mp")) * crops

    def own(value):
        return lax.dynamic_slice_in_dim(value, start, crops, 0)

    own_denominator = own(denominator)
    pos_weight = own(jnp.exp(pos_logit - inv_tau)) / own_denominator
    grad_query = (
        own(queue_pull) / own_denominator[:, None]
        + (pos_weight - 1.0)[:, None] * own(partner_low).astype(F32)
    ) * (inv_tau / query_low.shape[0])
    grad_pooled = jax.vjp(unit_rows, query)[1](grad_query)[0]
    counts = jnp.sum((own_segments[:, None] == jnp.arange(crops, dtype=jnp.int32)).astype(F32), axis=0)
    return loss_value, jnp.pad(grad_pooled / counts[:, None], ((0, 8 - crops), (0, 0)))


def split_right(weights, values):
    high = weights.astype(BF)
    rest = (weights - high.astype(F32)).astype(BF)
    return jnp.dot(high, values, preferred_element_type=F32) + jnp.dot(
        rest, values, preferred_element_type=F32
    )


def local(
    hidden_in, segments, partners, queue, first_weight, second_weight, out_bias, ln_gain, ln_bias
):
    m = lax.axis_index("mp")
    width = hidden_in.shape[-1]
    seq = segments.shape[1]
    w1 = first_weight.reshape(2, width, -1)
    w2 = second_weight.reshape(2, -1, width)
    cols = w1.shape[2]
    n_qkv = cols // 4 * 3
    heads = 2 * (cols // 4) // HD
    own_segments = lax.dynamic_index_in_dim(segments, m, 0, keepdims=False)
    own_partners = lax.dynamic_index_in_dim(partners, m, 0, keepdims=False)
    segc = jnp.broadcast_to(own_segments[:, None], (seq, 128))
    segr = jnp.broadcast_to(own_segments[None, :], (8, seq))
    small = jnp.stack([out_bias[:, 0], ln_gain[:, 0], ln_bias[:, 0]], axis=1)
    small = jnp.pad(small, ((0, 0), (0, 5), (0, 0)))
    anyspace = pl.BlockSpec(memory_space=pl.ANY)
    vmem = pl.BlockSpec(memory_space=pltpu.VMEM)
    shape = jax.ShapeDtypeStruct
    dma = pltpu.SemaphoreType.DMA
    saved = [
        shape((2, seq, n_qkv), BF), shape((heads, seq, seq), BF), shape((seq, width), BF),
        shape((seq, width), F32), shape((seq, 128), F32), shape((seq, width), BF), shape((2, width, cols), BF),
        shape((2, cols, width), BF),
    ]
    *kept, pooled = pl.pallas_call(
        forward_kernel,
        out_shape=saved + [shape((2, 8, width), F32)],
        in_specs=[anyspace] * 3 + [vmem] * 3,
        out_specs=[anyspace] * 8 + [vmem],
        scratch_shapes=[
            pltpu.VMEM((2, 2, width, cols), BF), pltpu.VMEM((2, 2, cols, width), BF),
            pltpu.VMEM((2, seq, width), BF), pltpu.VMEM((2, seq, width), BF),
            pltpu.VMEM((2, 2, seq, n_qkv), BF), pltpu.VMEM((heads, seq, seq), BF),
            pltpu.VMEM((2, seq, width), BF), pltpu.VMEM((seq, width), F32),
            pltpu.VMEM((seq, width), F32), pltpu.VMEM((seq, 128), F32),
            dma((6,)), dma((2,)), dma((2,)), dma((2,)), dma((2,)), dma((2,)), dma((2,)), dma((2,)), dma((2,)),
            dma((2,)), dma((2,)), dma((2, seq // ROWS)), dma((2, seq // ROWS)), dma((8,)),
        ],
        compiler_params=pltpu.CompilerParams(
            collective_id=0, has_side_effects=True, vmem_limit_bytes=VMEM_BYTES
        ),
        name="forward",
    )(hidden_in, w1, w2, segc, segr, small)
    loss_value, grad_pooled = crop_head(pooled, own_partners, own_segments, queue)
    half_width = width // lax.axis_size("section")
    sections, planes = lax.axis_size("section"), lax.axis_size("dp")
    gin, red, sums = pl.pallas_call(
        backward_kernel,
        out_shape=[
            shape((2, seq // 2, half_width), BF), shape((2, width, cols), BF), shape((8, width), F32),
        ],
        in_specs=[anyspace] * 8 + [vmem] * 3,
        out_specs=[vmem, anyspace, vmem],
        scratch_shapes=[pltpu.VMEM(a.shape, a.dtype) for a in saved]
        + [
            pltpu.VMEM((seq, width), BF), pltpu.VMEM((seq, width), BF), pltpu.VMEM((seq, width), BF),
            pltpu.VMEM((seq, width), F32), pltpu.VMEM((2, seq, cols), BF),
            pltpu.VMEM((sections, seq, half_width), BF),
            pltpu.VMEM((2, width, cols), BF), pltpu.VMEM((2, width, cols), BF),
            pltpu.VMEM((2, width, cols), BF), pltpu.VMEM((2, 2, width, cols), BF),
            pltpu.VMEM((2 * planes, 8, width), F32),
            dma((8,)), dma((seq // ROWS,)), dma((seq // ROWS,)), dma((2 * sections,)), dma((2,)),
            dma((2,)), dma((2,)), dma((2 * PIECES,)), dma((2, 2 * PIECES)), dma((2, 2 * PIECES)),
            dma((2 * PIECES,)), dma((PIECES,)), dma((PIECES,)), dma((2 * planes,)), dma((2 * planes,)),
        ],
        compiler_params=pltpu.CompilerParams(
            collective_id=1, has_side_effects=True, vmem_limit_bytes=VMEM_BYTES
        ),
        name="backward",
    )(*kept, grad_pooled, segc, small[0])
    grad_first = red[1].astype(F32).reshape(width, 4, -1)
    grad_second = red[0, :, width:].astype(F32).reshape(second_weight.shape[2:])
    return (
        loss_value, gin, grad_first[None], grad_second[None], sums[0:1], sums[1:2], sums[2:3],
    )


def solution(mesh):
    in_specs = (
        P("dp", "mp", None), P("dp", None), P("dp", None), P(("section", "dp", "mp"), None),
        P(None, "section", None, None, "mp"), P(None, "section", None, "mp", None),
        P(None, "section", None), P(None, "section", None), P(None, "section", None),
    )
    out_specs = (
        P(), P("dp", "mp", "section"), P("section", None, None, "mp"), P("section", None, "mp", None),
        P("section", None), P("section", None), P("section", None),
    )
    return jax.shard_map(local, mesh=mesh, in_specs=in_specs, out_specs=out_specs, check_vma=False)
```

```python
import functools
import jax
import jax.numpy as jnp
from jax import lax
from jax.experimental import pallas as pl
from jax.experimental.pallas import tpu as pltpu

F32 = jnp.float32
BF = jnp.bfloat16
HD = 64
NEG = -1e30
LN_EPS = 1e-12


def mm(a, b, ca=1, cb=0):
    return lax.dot_general(a, b, (((ca,), (cb,)), ((), ())), preferred_element_type=F32)


def norm_rows(resid, gain, shift):
    centre = resid - jnp.mean(resid, axis=-1, keepdims=True)
    spread = jnp.mean(centre * centre, axis=-1, keepdims=True)
    rstd = lax.rsqrt(spread + LN_EPS)
    xhat = centre * rstd
    return xhat * gain + shift, xhat, rstd


def norm_back(g, xhat, rstd, gain):
    gg = g * gain
    m1 = jnp.mean(gg, axis=-1, keepdims=True)
    m2 = jnp.mean(gg * xhat, axis=-1, keepdims=True)
    return rstd * (gg - m1 - xhat * m2)


def lane_low(shape):
    return lax.broadcasted_iota(jnp.int32, shape, len(shape) - 1) < HD


def qkv_rows(x, w_ref, qkv_ref, row0, rows):
    for h in range(2):
        n = qkv_ref.shape[2]
        qkv_ref[h, pl.ds(row0, rows), :] = mm(x, w_ref[h, :, :n]).astype(BF)


def attend_rows(qkv_ref, seg_col, seg_row, p_ref, mixed_ref, row0, rows):
    half = qkv_ref.shape[2] // 3
    pairs = half // 128
    same = seg_col == seg_row
    low = lane_low((rows, 128))
    for h in range(2):
        for pp in range(pairs):
            q = qkv_ref[h, pl.ds(row0, rows), pl.ds(pp * 128, 128)]
            k = qkv_ref[h, :, pl.ds(half + pp * 128, 128)]
            v = qkv_ref[h, :, pl.ds(2 * half + pp * 128, 128)]
            outs = []
            for a in range(2):
                qa = jnp.where(low if a == 0 else ~low, q, jnp.zeros_like(q))
                s = mm(qa, k, 1, 1) * (HD ** -0.5)
                s = jnp.where(same, s, NEG)
                mx = jnp.max(s, axis=-1, keepdims=True)
                e = jnp.exp(s - mx)
                p = (e * (1.0 / jnp.sum(e, axis=-1, keepdims=True))).astype(BF)
                if p_ref is not None:
                    p_ref[(h * pairs + pp) * 2 + a, pl.ds(row0, rows), :] = p
                outs.append(mm(p, v))
            mixed_ref[pl.ds(row0, rows), pl.ds(h * half + pp * 128, 128)] = jnp.where(
                low, outs[0], outs[1]
            ).astype(BF)


def attn_out(mixed, w_ref, n_qkv):
    half = mixed.shape[1] // 2
    return mm(mixed[:, :half], w_ref[0, :, n_qkv:], 1, 1) + mm(
        mixed[:, half:], w_ref[1, :, n_qkv:], 1, 1
    )


def gelu_parts(up, want_slope):
    cdf = 0.5 * (1.0 + lax.erf(up * (0.5 ** 0.5)))
    act = up * cdf
    if not want_slope:
        return act, None
    slope = cdf + up * (jnp.exp(-0.5 * up * up) * 0.3989422804014327)
    return act, slope


def ffn_rows(x, w_ref, v_ref, keep_ref, row0, rows, tile=512):
    acc = None
    for h in range(2):
        n = w_ref.shape[2]
        for c in range(0, n, tile):
            up = mm(x, w_ref[h, :, c : c + tile])
            act, slope = gelu_parts(up, keep_ref is not None)
            act = act.astype(BF)
            if keep_ref is not None:
                at = (h * n + c) // tile
                keep_ref[at, pl.ds(row0, rows), :] = act
                keep_ref[keep_ref.shape[0] // 2 + at, pl.ds(row0, rows), :] = slope.astype(BF)
            part = mm(act, v_ref[h, c : c + tile, :])
            acc = part if acc is None else acc + part
    return acc


def ffn_back_rows(low, w_ref, v_ref, keep_ref, gup_ref, row0, rows, tile=512):
    acc = None
    for h in range(2):
        n = w_ref.shape[2]
        for c in range(0, n, tile):
            dact = mm(low, v_ref[h, c : c + tile, :], 1, 1)
            at = keep_ref.shape[0] // 2 + (h * n + c) // tile
            gup = (dact * keep_ref[at, pl.ds(row0, rows), :].astype(F32)).astype(BF)
            gup_ref[h, pl.ds(row0, rows), c : c + tile] = gup
            part = mm(gup, w_ref[h, :, c : c + tile], 1, 1)
            acc = part if acc is None else acc + part
    return acc


def attn_back_core(low_ref, w_ref, qkv_ref, p_ref, dqkv_ref, n_qkv):
    half = n_qkv // 3
    pairs = half // 128
    seq = low_ref.shape[0]
    low = lane_low((seq, 128))
    for h in range(2):
        for pp in range(pairs):
            gm = mm(low_ref[...], w_ref[h, :, n_qkv + pp * 128 : n_qkv + pp * 128 + 128]).astype(BF)
            q = qkv_ref[h, :, pl.ds(pp * 128, 128)]
            k = qkv_ref[h, :, pl.ds(half + pp * 128, 128)]
            v = qkv_ref[h, :, pl.ds(2 * half + pp * 128, 128)]
            dq, dk, dv = [], [], []
            for a in range(2):
                keep = low if a == 0 else ~low
                gma = jnp.where(keep, gm, jnp.zeros_like(gm))
                pb = p_ref[(h * pairs + pp) * 2 + a, :, :]
                g = mm(gma, v, 1, 1)
                pf = pb.astype(F32)
                rs = jnp.sum(pf * g, axis=-1, keepdims=True)
                ds = (pf * (g - rs)).astype(BF)
                dq.append(mm(ds, k))
                dk.append(mm(ds, q, 0, 0))
                dv.append(mm(pb, gm, 0, 0))
            sc = HD ** -0.5
            dqkv_ref[h, :, pl.ds(pp * 128, 128)] = (jnp.where(low, dq[0], dq[1]) * sc).astype(BF)
            dqkv_ref[h, :, pl.ds(half + pp * 128, 128)] = (jnp.where(low, dk[0], dk[1]) * sc).astype(BF)
            dqkv_ref[h, :, pl.ds(2 * half + pp * 128, 128)] = jnp.where(low, dv[0], dv[1]).astype(BF)


from jax.sharding import PartitionSpec as P

MESH = pl.DeviceIdType.MESH
inv_tau = 20.0
unit_eps = 1e-06
ROWS = 256
VMEM_BYTES = 62 * 2**20


CROPS_OF_ROW = 6


def unit_rows(vectors):
    return vectors * lax.rsqrt(jnp.sum(vectors * vectors, axis=-1, keepdims=True) + unit_eps)


def member_rows(seg_row, count):
    return (lax.broadcasted_iota(jnp.int32, (count, seg_row.shape[1]), 0) == seg_row).astype(F32)


def split_mm(member, value):
    high = value.astype(BF)
    rest = (value - high.astype(F32)).astype(BF)
    return mm(member, high) + mm(member, rest)


def forward_kernel(
    hid, w1, w2, queue, segc, segr, small, partner,
    o_qkv, o_p, o_mixed, o_xhat, o_rstd, o_x, o_w, o_v, o_head,
    W, V, X, Y, qkv, prob, mixed, yf, xhat, rstd, pool, rows_q, queue_low, part, parts, blocks,
    l_sem, ws, wr, vbs, vbr, vas, var, vfs, vfr, hs, hr, acs, acr, o_sem,
    qs, qr, ds, dr, us, ur, bs, br,
):
    s, d, m = lax.axis_index("section"), lax.axis_index("dp"), lax.axis_index("mp")
    last, planes = lax.axis_size("section") - 1, lax.axis_size("dp")
    own_slot, slots = d * 2 + m, 2 * planes
    other = 1 - m
    seq = X.shape[1]
    chunks = seq // ROWS
    n_qkv = qkv.shape[3]
    va_rows = w2.shape[1]
    even = lax.rem(s, 2) == 0
    odd = lax.rem(s, 2) == 1

    barrier = pltpu.get_barrier_semaphore()
    pl.semaphore_signal(barrier, inc=1, device_id={"mp": other}, device_id_type=MESH)

    @pl.when(s > 0)
    def _():
        pl.semaphore_signal(barrier, inc=1, device_id={"section": s - 1}, device_id_type=MESH)

    @pl.when(s < last)
    def _():
        pl.semaphore_signal(barrier, inc=1, device_id={"section": s + 1}, device_id_type=MESH)

    @pl.when(s < last - 1)
    def _():
        pl.semaphore_signal(barrier, inc=1, device_id={"section": last}, device_id_type=MESH)

    @pl.when(s == last)
    def _():
        for t in range(last - 1):
            pl.semaphore_signal(barrier, inc=1, device_id={"section": t}, device_id_type=MESH)

        def greet(i, carry):
            for c in range(2):
                pl.semaphore_signal(
                    barrier, inc=1, device_id={"dp": lax.rem(d + 1 + i, planes), "mp": c}, device_id_type=MESH
                )
            return carry

        lax.fori_loop(0, planes - 1, greet, 0)

    pl.semaphore_wait(
        barrier,
        1
        + jnp.where(s > 0, 1, 0)
        + jnp.where(s < last, 1, 0)
        + jnp.where(s < last - 1, 1, 0)
        + jnp.where(s == last, last - 1 + 2 * (planes - 1), 0),
    )

    def to_core(src, dst, ss, rs):
        return pltpu.make_async_remote_copy(
            src_ref=src, dst_ref=dst, send_sem=ss, recv_sem=rs,
            device_id={"mp": other}, device_id_type=MESH,
        )

    def to_next(src, dst, ss, rs):
        return pltpu.make_async_remote_copy(
            src_ref=src, dst_ref=dst, send_sem=ss, recv_sem=rs,
            device_id={"section": s + 1}, device_id_type=MESH,
        )

    def w_far(e):
        return to_core(w1.at[e], W.at[e, m], ws.at[e], wr.at[e])

    def w_near(e):
        return pltpu.make_async_copy(w1.at[e], W.at[e, m], l_sem.at[e])

    def vb_far(e):
        return to_core(w2.at[e], V.at[e, m, pl.ds(va_rows, va_rows)], vbs.at[e], vbr.at[e])

    def vb_near(e):
        return pltpu.make_async_copy(w2.at[e], V.at[e, m, pl.ds(va_rows, va_rows)], l_sem.at[2 + e])

    def va_next(e):
        return to_next(w2.at[e], V.at[e, m, pl.ds(0, va_rows)], vas.at[e], var.at[e])

    def va_core(e):
        part = V.at[e, m, pl.ds(0, va_rows)]
        return to_core(part, part, vfs.at[e], vfr.at[e])

    def hid_far(e):
        return to_core(hid.at[other], X.at[e, pl.ds(pl.multiple_of(m * ROWS, ROWS), ROWS)], hs.at[e], hr.at[e])

    def hid_near(e):
        return pltpu.make_async_copy(
            hid.at[m], X.at[e, pl.ds(pl.multiple_of(m * ROWS, ROWS), ROWS)], l_sem.at[4 + e]
        )

    def act_next(e, c):
        rows = pl.ds(pl.multiple_of(c * ROWS, ROWS), ROWS)
        return to_next(Y.at[e, rows], X.at[e, rows], acs.at[e, c], acr.at[e, c])

    @pl.when(s == 0)
    def _():
        for e in range(2):
            hid_far(e).start()
            hid_near(e).start()

    w_far(0).start()
    w_near(0).start()

    @pl.when(odd)
    def _():
        vb_far(0).start()
        vb_near(0).start()

    @pl.when(even)
    def _():
        va_next(0).start()

    w_far(1).start()
    w_near(1).start()

    @pl.when(odd)
    def _():
        vb_far(1).start()
        vb_near(1).start()

    @pl.when(s == 0)
    def _():
        for e in range(2):
            hid_far(e).wait_recv()
            hid_near(e).wait()


    def saves(e):
        pairs = [
            (qkv.at[0], o_qkv), (prob, o_p), (mixed.at[0], o_mixed),
            (xhat, o_xhat), (rstd, o_rstd), (X.at[0], o_x), (W.at[0], o_w), (V.at[0], o_v),
        ]
        return [pltpu.make_async_copy(a, b, o_sem.at[i]) for i, (a, b) in enumerate(pairs)]

    def finish(e, rows, resid):
        y, xh, rs = norm_rows(resid, small[e, 1:2, :], small[e, 2:3, :])
        if e == 0:
            xhat[rows, :] = xh
            rstd[rows, :] = jnp.broadcast_to(rs, (ROWS, 128))
        return y

    def wait_w(e):
        w_near(e).wait()
        w_far(e).wait_recv()

    def remote(src, dst, send, recv, **to):
        return pltpu.make_async_remote_copy(
            src_ref=src, dst_ref=dst, send_sem=send, recv_sem=recv, device_id=to, device_id_type=MESH
        )

    def peer(i):
        return lax.rem(own_slot + 1 + i, slots)

    def query_to(i):
        to = peer(i)
        return remote(
            rows_q.at[own_slot], rows_q.at[own_slot], qs.at[i], qr.at[own_slot], dp=to // 2, mp=lax.rem(to, 2)
        )

    def query_from(i):
        slot = peer(i)
        return remote(rows_q.at[slot], rows_q.at[slot], qs.at[i], qr.at[slot], dp=slot // 2, mp=lax.rem(slot, 2))

    def query_down(t):
        return remote(rows_q, rows_q, ds.at[t], dr.at[0], section=t)

    def part_up():
        return remote(part, parts.at[s], us.at[0], ur.at[s], section=last)

    def part_in(t):
        return remote(part, parts.at[t], us.at[0], ur.at[t], section=last)

    def block_to(i):
        to = peer(i)
        return remote(part.at[to], blocks.at[own_slot], bs.at[i], br.at[own_slot], dp=to // 2, mp=lax.rem(to, 2))

    def block_from(i):
        slot = peer(i)
        return remote(part.at[slot], blocks.at[slot], bs.at[i], br.at[slot], dp=slot // 2, mp=lax.rem(slot, 2))

    def each(count, what):
        def one(i, carry):
            what(i)
            return carry

        lax.fori_loop(0, count, one, 0)

    def queue_copy():
        return pltpu.make_async_copy(queue, queue_low, l_sem.at[6])

    def low_queue():
        queue_copy().wait()
        raw = queue_low[...].astype(F32)
        queue_low[...] = unit_rows(raw).astype(BF)

    def queue_share():
        width = queue_low.shape[1]
        query = rows_q[...].reshape(-1, width).astype(BF)
        weight = jnp.exp(mm(query, queue_low[...], 1, 1) * inv_tau - inv_tau)
        high = weight.astype(BF)
        rest = (weight - high.astype(F32)).astype(BF)
        pull = mm(high, queue_low[...]) + mm(rest, queue_low[...])
        sums = jnp.sum(weight, axis=-1, keepdims=True)
        part[:, :, :width] = pull.reshape(slots, 8, width)
        part[:, :, width:] = jnp.broadcast_to(sums, (sums.shape[0], 128)).reshape(slots, 8, 128)

    def share_below():
        query_down(0).wait_recv()
        queue_share()
        part_up().start()

    def share_last():
        rows_q[own_slot] = unit_rows(pool[0]).astype(BF).astype(F32)
        each(slots - 1, lambda i: query_to(i).start())
        each(slots - 1, lambda i: query_from(i).wait_recv())
        for t in range(last):
            query_down(t).start()
        queue_share()
        for t in range(last):
            part_in(t).wait_recv()
        part[...] = part[...] + jnp.sum(parts[...], axis=0)
        blocks[own_slot] = part[own_slot]
        each(slots - 1, lambda i: block_to(i).start())

    def head_end():
        width = queue_low.shape[1]
        pick = (lax.broadcasted_iota(jnp.int32, (8, 8), 1) == partner[:, :8]).astype(F32)
        key_low = unit_rows(pool[1]).astype(BF).astype(F32)
        partner_low = jnp.dot(pick, key_low, preferred_element_type=F32)
        query_low = rows_q[own_slot]
        pos = jnp.sum(query_low * partner_low, axis=-1, keepdims=True) * inv_tau
        each(slots - 1, lambda i: block_from(i).wait_recv())
        total = jnp.sum(blocks[...], axis=0)
        pos_weight = jnp.exp(pos - inv_tau)
        denominator = pos_weight + total[:, width : width + 1]
        log_total = inv_tau + jnp.log(denominator)
        member = member_rows(segr[:1, :], 8)
        counts = jnp.sum(member, axis=-1, keepdims=True)
        crops = slots * CROPS_OF_ROW
        real = lax.broadcasted_iota(jnp.int32, (8, 1), 0) < CROPS_OF_ROW
        loss = jnp.sum(jnp.where(real, log_total - pos, 0.0), axis=0, keepdims=True) * (1.0 / crops)
        grad = (total[:, :width] / denominator + (pos_weight / denominator - 1.0) * partner_low) * (
            inv_tau / crops
        )
        vectors = pool[0]
        scale = lax.rsqrt(jnp.sum(vectors * vectors, axis=-1, keepdims=True) + unit_eps)
        inner = jnp.sum(vectors * grad, axis=-1, keepdims=True)
        grad = scale * grad - vectors * (scale * scale * scale * inner)
        o_head[:8, :] = grad / jnp.maximum(counts, 1.0)
        o_head[8:, :] = jnp.broadcast_to(loss, (8, width))

    def attention(e):
        wait_w(e)

        def project(c, carry):
            @pl.when(s > 0)
            def _():
                act_next(e, c).wait_recv()

            r = pl.multiple_of(c * ROWS, ROWS)
            qkv_rows(X[e, pl.ds(r, ROWS), :], W.at[e], qkv.at[e], r, ROWS)
            return carry

        lax.fori_loop(0, chunks, project, 0)
        if e == 1:
            pl.when(s > 0)(share_below)

        def attend(c, carry):
            r = pl.multiple_of(c * ROWS, ROWS)
            rows = pl.ds(r, ROWS)
            attend_rows(qkv.at[e], segc[rows, :1], segr[:1, :], prob if e == 0 else None, mixed.at[e], r, ROWS)
            branch = attn_out(mixed[e, rows, :], W.at[e], n_qkv)
            y = finish(e, rows, X[e, rows, :].astype(F32) + branch + small[e, 0:1, :])
            Y[e, rows, :] = y.astype(BF)
            act_next(e, c).start()
            return carry

        lax.fori_loop(0, chunks, attend, 0)

    def feed(e):
        wait_w(e)
        va_next(e).wait_recv()
        va_core(e).start()
        vb_near(e).wait()
        vb_far(e).wait_recv()
        va_core(e).wait_recv()

        def one(c, carry):
            act_next(e, c).wait_recv()
            r = pl.multiple_of(c * ROWS, ROWS)
            rows = pl.ds(r, ROWS)
            x = X[e, rows, :]
            branch = ffn_rows(x, W.at[e], V.at[e], prob if e == 0 else None, r, ROWS)
            y = finish(e, rows, x.astype(F32) + branch + small[e, 0:1, :])

            @pl.when(s < last)
            def _():
                Y[e, rows, :] = y.astype(BF)
                act_next(e, c).start()

            @pl.when(s == last)
            def _():
                yf[rows, :] = y

            return carry

        lax.fori_loop(0, chunks, one, 0)

        @pl.when(s == last)
        def _():
            member = member_rows(segr[:1, :], 8)
            counts = jnp.sum(member, axis=-1, keepdims=True)
            pool[e] = split_mm(member.astype(BF), yf[...]) / jnp.maximum(counts, 1.0)

    queue_copy().start()

    @pl.when(s > 0)
    def _():
        low_queue()

    for e in range(2):
        @pl.when(even)
        def _():
            attention(e)
            if e == 0:
                va_next(1).start()

        @pl.when(odd)
        def _():
            feed(e)

        if e == 0:
            pl.when(s == last)(share_last)
            for copy in saves(0):
                copy.start()

    @pl.when(s == 0)
    def _():
        low_queue()

    pl.when(s < last - 1)(share_below)
    pl.when(s == last)(head_end)
    for copy in saves(0):
        copy.wait()

    @pl.when(s < last)
    def _():
        part_up().wait_send()

    @pl.when(s == last)
    def _():
        for t in range(last):
            query_down(t).wait_send()
        each(slots - 1, lambda i: query_to(i).wait_send())
        each(slots - 1, lambda i: block_to(i).wait_send())

    for e in range(2):
        w_far(e).wait_send()

        @pl.when(odd)
        def _():
            vb_far(e).wait_send()
            va_core(e).wait_send()

        @pl.when(even)
        def _():
            va_next(e).wait_send()

        @pl.when(s == 0)
        def _():
            hid_far(e).wait_send()

        @pl.when(s < last)
        def _():
            for c in range(chunks):
                act_next(e, c).wait_send()


PIECES = 16
WAIT_ROOT = 2
LAG = 3


def backward_kernel(
    i_qkv, i_p, i_mixed, i_xhat, i_rstd, i_x, i_w, i_v, head, segc, small,
    o_gin, o_red, o_sum,
    qkv, prob, mixed, xhat, rstd, X, W, V, G, gout, low, resid, gup, gsplit,
    mine, give, taken, part, sums, loss,
    i_sem, gs, gr, is_, ir, xs, xr, ps, pr, fs, fr, vs, vr, ss, sr, ls, lr,
):
    s, d, m = lax.axis_index("section"), lax.axis_index("dp"), lax.axis_index("mp")
    sections, planes = lax.axis_size("section"), lax.axis_size("dp")
    last = sections - 1
    other = 1 - m
    seq, width = X.shape
    chunks = seq // ROWS
    n_qkv = qkv.shape[2]
    cols = W.shape[2]
    even = lax.rem(s, 2) == 0
    odd = lax.rem(s, 2) == 1
    loads = [
        pltpu.make_async_copy(a, b, i_sem.at[i])
        for i, (a, b) in enumerate(
            [(i_xhat, xhat), (i_rstd, rstd), (i_v, V), (i_p, prob), (i_w, W), (i_x, X),
             (i_qkv, qkv), (i_mixed, mixed)]
        )
    ]
    for copy in loads:
        copy.start()

    barrier = pltpu.get_barrier_semaphore()
    for t in range(sections):
        for c in range(2):
            @pl.when((s != t) | (m != c))
            def _():
                pl.semaphore_signal(barrier, inc=1, device_id={"section": t, "mp": c}, device_id_type=MESH)

    def greet(i, carry):
        to = lax.rem(d + 1 + i, planes)
        for c in range(2):
            pl.semaphore_signal(barrier, inc=1, device_id={"dp": to, "mp": c}, device_id_type=MESH)
        return carry

    lax.fori_loop(0, planes - 1, greet, 0)
    pl.semaphore_wait(barrier, 2 * sections - 1 + 2 * (planes - 1))

    def remote(src, dst, send, recv, **to):
        return pltpu.make_async_remote_copy(
            src_ref=src, dst_ref=dst, send_sem=send, recv_sem=recv, device_id=to, device_id_type=MESH
        )

    def grad_prev(c):
        rows = pl.ds(pl.multiple_of(c * ROWS, ROWS), ROWS)
        return remote(gout.at[rows], G.at[rows], gs.at[c], gr.at[c], section=s - 1)

    def spread(t, c):
        return remote(
            gsplit.at[t, pl.ds(c * ROWS, ROWS)], o_gin.at[m], is_.at[t * 2 + c], ir.at[m], section=t, mp=c
        )

    for copy in loads:
        copy.wait()

    own_slot = d * 2 + m
    sums[own_slot] = jnp.zeros_like(sums[own_slot])

    @pl.when(s == last)
    def _():
        sums[own_slot, 3:4, :] = head[8:9, :]

    def through_norm(c, g):
        rows = pl.ds(pl.multiple_of(c * ROWS, ROWS), ROWS)
        xh = xhat[rows, :]
        grad = norm_back(g, xh, rstd[rows, :1], small[1:2, :])
        sums[own_slot, 0:1, :] += jnp.sum(grad, axis=0, keepdims=True)
        sums[own_slot, 1:2, :] += jnp.sum(g * xh, axis=0, keepdims=True)
        sums[own_slot, 2:3, :] += jnp.sum(g, axis=0, keepdims=True)
        resid[rows, :] = grad
        low[rows, :] = grad.astype(BF)

    def exchange(kind):
        return remote(give.at[kind], taken.at[kind], xs.at[kind], xr.at[kind], mp=other)

    def sum_to(i):
        to = lax.rem(own_slot + 1 + i, 2 * planes)
        return remote(
            sums.at[own_slot], sums.at[own_slot], ss.at[i], sr.at[own_slot], dp=to // 2, mp=lax.rem(to, 2)
        )

    def sum_from(i):
        slot = lax.rem(own_slot + 1 + i, 2 * planes)
        return remote(sums.at[slot], sums.at[slot], ss.at[i], sr.at[slot], dp=slot // 2, mp=lax.rem(slot, 2))

    def start_sums():
        def one(i, carry):
            sum_to(i).start()
            return carry

        lax.fori_loop(0, 2 * planes - 1, one, 0)

    @pl.when(odd)
    def _():
        def one(c, carry):
            r = pl.multiple_of(c * ROWS, ROWS)
            rows = pl.ds(r, ROWS)

            @pl.when(s == last)
            def _():
                own = (lax.broadcasted_iota(jnp.int32, (ROWS, 8), 1) == segc[rows, :8]).astype(BF)
                through_norm(c, split_mm(own, head[:8, :]))

            @pl.when(s < last)
            def _():
                grad_prev(c).wait_recv()
                through_norm(c, G[rows, :].astype(F32))

            dx = ffn_back_rows(low[rows, :], W, V, prob, gup, r, ROWS)
            gout[rows, :] = (resid[rows, :] + dx).astype(BF)
            grad_prev(c).start()
            return carry

        lax.fori_loop(0, chunks, one, 0)
        start_sums()
        unit = 256
        for h, out in ((other, give), (m, mine)):
            for c in range(cols // unit):
                act = prob[h * (cols // 512) + c * unit // 512, :, c * unit % 512 : c * unit % 512 + unit]
                r, q = c * unit % width, c * unit // width * width
                out[0, r : r + unit, q : q + width] = mm(act, low[...], 0, 0).astype(BF)
            if out is give:
                exchange(0).start()
        for h, out in ((other, give), (m, mine)):
            for c in range(0, cols, 512):
                out[1, :, c : c + 512] = mm(X[...], gup[h, :, c : c + 512], 0, 0).astype(BF)
            if out is give:
                exchange(1).start()
        exchange(0).wait_recv()

    @pl.when(even)
    def _():
        def one(c, carry):
            rows = pl.ds(pl.multiple_of(c * ROWS, ROWS), ROWS)
            grad_prev(c).wait_recv()
            through_norm(c, G[rows, :].astype(F32))
            return carry

        lax.fori_loop(0, chunks, one, 0)
        start_sums()
        attn_back_core(low, W, qkv, prob, gup, n_qkv)

        def back(c, carry):
            rows = pl.ds(pl.multiple_of(c * ROWS, ROWS), ROWS)
            dx = mm(gup[0, rows, :n_qkv], W[0, :, :n_qkv], 1, 1) + mm(
                gup[1, rows, :n_qkv], W[1, :, :n_qkv], 1, 1
            )
            grad = (resid[rows, :] + dx).astype(BF)

            @pl.when(s > 0)
            def _():
                gout[rows, :] = grad
                grad_prev(c).start()

            @pl.when(s == 0)
            def _():
                part_width = gsplit.shape[2]
                for t in range(sections):
                    gsplit[t, rows, :] = grad[:, t * part_width : (t + 1) * part_width]

            return carry

        lax.fori_loop(0, chunks, back, 0)

        @pl.when(s == 0)
        def _():
            for t in range(sections):
                for c in range(2):
                    if t > 0:
                        spread(t, c).start()
                    else:
                        @pl.when(m != c)
                        def _():
                            spread(t, c).start()

                        @pl.when(m == c)
                        def _():
                            pltpu.make_async_copy(
                                gsplit.at[t, pl.ds(c * ROWS, ROWS)], o_gin.at[m], is_.at[t * 2 + c]
                            ).start()

        half = n_qkv // 3
        for h, out in ((other, give), (m, mine)):
            for c in range(0, n_qkv, half):
                out[1, :, c : c + half] = mm(X[...], gup[h, :, c : c + half], 0, 0).astype(BF)
            for k in range(2):
                @pl.when(h == k)
                def _():
                    out[1, :, n_qkv:] = mm(low[...], mixed[:, k * half : (k + 1) * half], 0, 0).astype(BF)
            if out is give:
                exchange(1).start()

    exchange(1).wait_recv()

    step_rows = width // PIECES
    root_a, root_b = (planes - 1) // 2, planes // 2
    first = jnp.where(odd, 0, PIECES)
    total = 2 * PIECES
    lag = WAIT_ROOT + LAG * jnp.maximum(root_b - d, d - root_a)

    def place(i):
        kind = i // PIECES
        rows = pl.ds(pl.multiple_of(lax.rem(i, PIECES) * step_rows, step_rows), step_rows)
        root = jnp.where(lax.rem(i, 2) == 0, root_a, root_b)
        return kind, rows, root

    def part_right(i):
        kind, rows, _ = place(i)
        return remote(mine.at[kind, rows], part.at[0, kind, rows], ps.at[i], pr.at[0, i], dp=d + 1)

    def part_left(i):
        kind, rows, _ = place(i)
        return remote(mine.at[kind, rows], part.at[1, kind, rows], ps.at[i], pr.at[1, i], dp=d - 1)

    def whole(i, side, src):
        kind, rows, _ = place(i)
        return remote(src.at[kind, rows], o_red.at[kind, rows], fs.at[side, i], fr.at[i], dp=d + (1 if side else -1))

    def keep_root(i):
        kind, rows, _ = place(i)
        return pltpu.make_async_copy(mine.at[kind, rows], o_red.at[kind, rows], fr.at[i])

    def down_prev(i):
        _, rows, _ = place(i)
        return remote(
            o_red.at[0, rows, pl.ds(0, width)], o_red.at[0, rows, pl.ds(width, width)],
            vs.at[i], vr.at[i], section=s - 1,
        )

    def add(i, *sides):
        kind, rows, _ = place(i)
        value = mine[kind, rows, :].astype(F32) + taken[kind, rows, :].astype(F32)
        for side in sides:
            value = value + part[side, kind, rows, :].astype(F32)
        mine[kind, rows, :] = value.astype(BF)

    def pieces(i, carry):
        root = place(i)[2]

        @pl.when((i < total) & (d < root))
        def _():
            @pl.when(d > 0)
            def _():
                part_right(i).wait_recv()
                add(i, 0)

            @pl.when(d == 0)
            def _():
                add(i)

            part_right(i).start()

        @pl.when((i < total) & (d > root))
        def _():
            @pl.when(d < planes - 1)
            def _():
                part_left(i).wait_recv()
                add(i, 1)

            @pl.when(d == planes - 1)
            def _():
                add(i)

            part_left(i).start()

        k = i - WAIT_ROOT

        @pl.when((k >= first) & (k < total) & (d == place(k)[2]))
        def _():
            part_right(k).wait_recv()
            part_left(k).wait_recv()
            add(k, 0, 1)
            keep_root(k).start()
            whole(k, 0, mine).start()
            whole(k, 1, mine).start()

        @pl.when(i >= first + lag)
        def _():
            j = i - lag
            kind, _, root = place(j)
            keep_root(j).wait()

            @pl.when((d < root) & (d > 0))
            def _():
                whole(j, 0, o_red).start()

            @pl.when((d > root) & (d < planes - 1))
            def _():
                whole(j, 1, o_red).start()

            @pl.when(kind == 0)
            def _():
                down_prev(j).start()

        return carry

    lax.fori_loop(first, total + lag, pieces, 0)

    def settle(i, carry):
        kind, rows, root = place(i)

        @pl.when(d != root)
        def _():
            part_right(i).wait_send()

        @pl.when((d <= root) & (d > 0))
        def _():
            whole(i, 0, mine).wait_send()

        @pl.when((d >= root) & (d < planes - 1))
        def _():
            whole(i, 1, mine).wait_send()

        @pl.when(kind == 0)
        def _():
            down_prev(i).wait_send()

        return carry

    lax.fori_loop(first, total, settle, 0)

    @pl.when(even)
    def _():
        def arrive(i, carry):
            down_prev(i).wait_recv()
            return carry

        lax.fori_loop(0, PIECES, arrive, 0)

    @pl.when(odd)
    def _():
        exchange(0).wait_send()

    exchange(1).wait_send()

    @pl.when(s > 0)
    def _():
        for c in range(chunks):
            grad_prev(c).wait_send()

    @pl.when(s == 0)
    def _():
        for t in range(sections):
            for c in range(2):
                if t > 0:
                    spread(t, c).wait_send()
                else:
                    @pl.when(m != c)
                    def _():
                        spread(t, c).wait_send()

                    @pl.when(m == c)
                    def _():
                        pltpu.make_async_copy(
                            gsplit.at[t, pl.ds(c * ROWS, ROWS)], o_gin.at[m], is_.at[t * 2 + c]
                        ).wait()

    def arrival(r):
        return remote(gsplit.at[0, pl.ds(0, ROWS)], o_gin.at[r], is_.at[0], ir.at[r], section=0, mp=r)

    for r in range(2):
        @pl.when((s != 0) | (m != r))
        def _():
            arrival(r).wait_recv()

    def sums_in(i, carry):
        sum_from(i).wait_recv()
        sum_to(i).wait_send()
        return carry

    def loss_down(t):
        return remote(loss, loss, ls.at[t], lr.at[0], section=t)

    lax.fori_loop(0, 2 * planes - 1, sums_in, 0)
    total_sums = jnp.sum(sums[...], axis=0)

    @pl.when(s == last)
    def _():
        loss[...] = total_sums
        for t in range(last):
            loss_down(t).start()
        for t in range(last):
            loss_down(t).wait_send()

    @pl.when(s < last)
    def _():
        loss_down(0).wait_recv()

    o_sum[...] = total_sums
    o_sum[3:4, :] = loss[3:4, :]


def local(
    hidden_in, segments, partners, queue, first_weight, second_weight, out_bias, ln_gain, ln_bias
):
    m = lax.axis_index("mp")
    width = hidden_in.shape[-1]
    seq = segments.shape[1]
    w1 = first_weight.reshape(2, width, -1)
    w2 = second_weight.reshape(2, -1, width)
    cols = w1.shape[2]
    n_qkv = cols // 4 * 3
    heads = 2 * (cols // 4) // HD
    own_segments = lax.dynamic_index_in_dim(segments, m, 0, keepdims=False)
    own_partners = lax.dynamic_index_in_dim(partners, m, 0, keepdims=False)
    segc = jnp.broadcast_to(own_segments[:, None], (seq, 128))
    segr = jnp.broadcast_to(own_segments[None, :], (8, seq))
    small = jnp.stack([out_bias[:, 0], ln_gain[:, 0], ln_bias[:, 0]], axis=1)
    small = jnp.pad(small, ((0, 0), (0, 5), (0, 0)))
    anyspace = pl.BlockSpec(memory_space=pl.ANY)
    vmem = pl.BlockSpec(memory_space=pltpu.VMEM)
    shape = jax.ShapeDtypeStruct
    dma = pltpu.SemaphoreType.DMA
    saved = [
        shape((2, seq, n_qkv), BF), shape((heads, seq, seq), BF), shape((seq, width), BF),
        shape((seq, width), F32), shape((seq, 128), F32), shape((seq, width), BF), shape((2, width, cols), BF),
        shape((2, cols, width), BF),
    ]
    sections, planes = lax.axis_size("section"), lax.axis_size("dp")
    crops = partners.shape[1]
    partner = jnp.broadcast_to(jnp.pad(own_partners, (0, 8 - crops), constant_values=-1)[:, None], (8, 128))
    *kept, head = pl.pallas_call(
        forward_kernel,
        out_shape=saved + [shape((16, width), F32)],
        in_specs=[anyspace] * 4 + [vmem] * 4,
        out_specs=[anyspace] * 8 + [vmem],
        scratch_shapes=[
            pltpu.VMEM((2, 2, width, cols), BF), pltpu.VMEM((2, 2, cols, width), BF),
            pltpu.VMEM((2, seq, width), BF), pltpu.VMEM((2, seq, width), BF),
            pltpu.VMEM((2, 2, seq, n_qkv), BF), pltpu.VMEM((heads, seq, seq), BF),
            pltpu.VMEM((2, seq, width), BF), pltpu.VMEM((seq, width), F32),
            pltpu.VMEM((seq, width), F32), pltpu.VMEM((seq, 128), F32),
            pltpu.VMEM((2, 8, width), F32), pltpu.VMEM((2 * planes, 8, width), F32),
            pltpu.VMEM(queue.shape, BF), pltpu.VMEM((2 * planes, 8, width + 128), F32),
            pltpu.VMEM((sections - 1, 2 * planes, 8, width + 128), F32),
            pltpu.VMEM((2 * planes, 8, width + 128), F32),
            dma((7,)), dma((2,)), dma((2,)), dma((2,)), dma((2,)), dma((2,)), dma((2,)), dma((2,)), dma((2,)),
            dma((2,)), dma((2,)), dma((2, seq // ROWS)), dma((2, seq // ROWS)), dma((8,)),
            dma((2 * planes,)), dma((2 * planes,)), dma((sections - 1,)), dma((1,)), dma((1,)),
            dma((sections - 1,)), dma((2 * planes,)), dma((2 * planes,)),
        ],
        compiler_params=pltpu.CompilerParams(
            collective_id=0, has_side_effects=True, vmem_limit_bytes=VMEM_BYTES
        ),
        name="forward",
    )(hidden_in, w1, w2, queue, segc, segr, small, partner)
    half_width = width // lax.axis_size("section")
    gin, red, sums = pl.pallas_call(
        backward_kernel,
        out_shape=[
            shape((2, seq // 2, half_width), BF), shape((2, width, cols), BF), shape((8, width), F32),
        ],
        in_specs=[anyspace] * 8 + [vmem] * 3,
        out_specs=[vmem, anyspace, vmem],
        scratch_shapes=[pltpu.VMEM(a.shape, a.dtype) for a in saved]
        + [
            pltpu.VMEM((seq, width), BF), pltpu.VMEM((seq, width), BF), pltpu.VMEM((seq, width), BF),
            pltpu.VMEM((seq, width), F32), pltpu.VMEM((2, seq, cols), BF),
            pltpu.VMEM((sections, seq, half_width), BF),
            pltpu.VMEM((2, width, cols), BF), pltpu.VMEM((2, width, cols), BF),
            pltpu.VMEM((2, width, cols), BF), pltpu.VMEM((2, 2, width, cols), BF),
            pltpu.VMEM((2 * planes, 8, width), F32), pltpu.VMEM((8, width), F32),
            dma((8,)), dma((seq // ROWS,)), dma((seq // ROWS,)), dma((2 * sections,)), dma((2,)),
            dma((2,)), dma((2,)), dma((2 * PIECES,)), dma((2, 2 * PIECES)), dma((2, 2 * PIECES)),
            dma((2 * PIECES,)), dma((PIECES,)), dma((PIECES,)), dma((2 * planes,)), dma((2 * planes,)),
            dma((sections - 1,)), dma((1,)),
        ],
        compiler_params=pltpu.CompilerParams(
            collective_id=1, has_side_effects=True, vmem_limit_bytes=VMEM_BYTES
        ),
        name="backward",
    )(*kept, head, segc, small[0])
    grad_first = red[1].astype(F32).reshape(width, 4, -1)
    grad_second = red[0, :, width:].astype(F32).reshape(second_weight.shape[2:])
    return (
        sums[3, 0], gin, grad_first[None], grad_second[None], sums[0:1], sums[1:2], sums[2:3],
    )


def solution(mesh):
    in_specs = (
        P("dp", "mp", None), P("dp", None), P("dp", None), P(("section", "dp", "mp"), None),
        P(None, "section", None, None, "mp"), P(None, "section", None, "mp", None),
        P(None, "section", None), P(None, "section", None), P(None, "section", None),
    )
    out_specs = (
        P(), P("dp", "mp", "section"), P("section", None, None, "mp"), P("section", None, "mp", None),
        P("section", None), P("section", None), P("section", None),
    )
    return jax.shard_map(local, mesh=mesh, in_specs=in_specs, out_specs=out_specs, check_vma=False)
```

```python
import functools
import jax
import jax.numpy as jnp
from jax import lax
from jax.experimental import pallas as pl
from jax.experimental.pallas import tpu as pltpu

F32 = jnp.float32
BF = jnp.bfloat16
HD = 64
NEG = -1e30
LN_EPS = 1e-12


def mm(a, b, ca=1, cb=0):
    return lax.dot_general(a, b, (((ca,), (cb,)), ((), ())), preferred_element_type=F32)


def norm_rows(resid, gain, shift):
    centre = resid - jnp.mean(resid, axis=-1, keepdims=True)
    spread = jnp.mean(centre * centre, axis=-1, keepdims=True)
    rstd = lax.rsqrt(spread + LN_EPS)
    xhat = centre * rstd
    return xhat * gain + shift, xhat, rstd


def norm_back(g, xhat, rstd, gain):
    gg = g * gain
    m1 = jnp.mean(gg, axis=-1, keepdims=True)
    m2 = jnp.mean(gg * xhat, axis=-1, keepdims=True)
    return rstd * (gg - m1 - xhat * m2)


def lane_low(shape):
    return lax.broadcasted_iota(jnp.int32, shape, len(shape) - 1) < HD


def qkv_rows(x, w_ref, qkv_ref, row0, rows):
    for h in range(2):
        n = qkv_ref.shape[2]
        qkv_ref[h, pl.ds(row0, rows), :] = mm(x, w_ref[h, :, :n]).astype(BF)


def crop_features(seg_col):
    lane = lax.broadcasted_iota(jnp.int32, seg_col.shape, 1)
    hit = lane == seg_col
    as_query = jnp.where(hit, NEG, 0.0).astype(BF)
    as_key = jnp.where(hit | (lane >= 8), 0.0, 1.0).astype(BF)
    return as_query, as_key


def attend_rows(qkv_ref, fq_ref, fk_ref, p_ref, inv_ref, mixed_ref, row0, rows):
    half = qkv_ref.shape[2] // 3
    pairs = half // 128
    low = lane_low((rows, 128))
    fq = fq_ref[pl.ds(row0, rows), :]
    fk = fk_ref[...]
    ones = jnp.ones((fk.shape[0], 128), BF)
    for h in range(2):
        for pp in range(pairs):
            q = qkv_ref[h, pl.ds(row0, rows), pl.ds(pp * 128, 128)] * jnp.asarray(HD ** -0.5, BF)
            k = jnp.concatenate([qkv_ref[h, :, pl.ds(half + pp * 128, 128)], fk], axis=1)
            v = jnp.concatenate([qkv_ref[h, :, pl.ds(2 * half + pp * 128, 128)], ones], axis=1)
            outs, invs = [], []
            for a in range(2):
                qa = jnp.where(low if a == 0 else ~low, q, jnp.zeros_like(q))
                s = mm(jnp.concatenate([qa, fq], axis=1), k, 1, 1)
                p = jnp.exp(s - jnp.max(s, axis=-1, keepdims=True)).astype(BF)
                if p_ref is not None:
                    p_ref[(h * pairs + pp) * 2 + a, pl.ds(row0, rows), :] = p
                o = mm(p, v)
                inv = 1.0 / o[:, 128:]
                outs.append(o[:, :128] * inv)
                invs.append(inv)
            if inv_ref is not None:
                inv_ref[h * pairs + pp, pl.ds(row0, rows), :] = jnp.where(low, invs[0], invs[1])
            mixed_ref[pl.ds(row0, rows), pl.ds(h * half + pp * 128, 128)] = jnp.where(
                low, outs[0], outs[1]
            ).astype(BF)


def attn_out(mixed, w_ref, n_qkv):
    half = mixed.shape[1] // 2
    return mm(mixed[:, :half], w_ref[0, :, n_qkv:], 1, 1) + mm(
        mixed[:, half:], w_ref[1, :, n_qkv:], 1, 1
    )


def gelu_parts(up, want_slope):
    cdf = 0.5 * (1.0 + lax.erf(up * (0.5 ** 0.5)))
    act = up * cdf
    if not want_slope:
        return act, None
    slope = cdf + up * (jnp.exp(-0.5 * up * up) * 0.3989422804014327)
    return act, slope


def ffn_rows(x, w_ref, v_ref, keep_ref, row0, rows, tile=512):
    acc = None
    for h in range(2):
        n = w_ref.shape[2]
        for c in range(0, n, tile):
            up = mm(x, w_ref[h, :, c : c + tile])
            act, slope = gelu_parts(up, keep_ref is not None)
            act = act.astype(BF)
            if keep_ref is not None:
                at = (h * n + c) // tile
                keep_ref[at, pl.ds(row0, rows), :] = act
                keep_ref[keep_ref.shape[0] // 2 + at, pl.ds(row0, rows), :] = slope.astype(BF)
            part = mm(act, v_ref[h, c : c + tile, :])
            acc = part if acc is None else acc + part
    return acc


def ffn_back_rows(low, w_ref, v_ref, keep_ref, gup_ref, row0, rows, tile=512):
    acc = None
    for h in range(2):
        n = w_ref.shape[2]
        for c in range(0, n, tile):
            dact = mm(low, v_ref[h, c : c + tile, :], 1, 1)
            at = keep_ref.shape[0] // 2 + (h * n + c) // tile
            gup = (dact * keep_ref[at, pl.ds(row0, rows), :].astype(F32)).astype(BF)
            gup_ref[h, pl.ds(row0, rows), c : c + tile] = gup
            part = mm(gup, w_ref[h, :, c : c + tile], 1, 1)
            acc = part if acc is None else acc + part
    return acc


def attn_back_core(low_ref, w_ref, qkv_ref, p_ref, inv_ref, mixed_ref, dqkv_ref, n_qkv):
    half = n_qkv // 3
    pairs = half // 128
    seq = low_ref.shape[0]
    low = lane_low((seq, 128))
    ones = jnp.ones((seq, 128), BF)
    scale = HD ** -0.5
    for h in range(2):
        for pp in range(pairs):
            at = pp * 128
            gm = mm(low_ref[...], w_ref[h, :, n_qkv + at : n_qkv + at + 128]).astype(BF)
            gs = gm.astype(F32) * inv_ref[h * pairs + pp]
            ts = -(gs * mixed_ref[:, h * half + at : h * half + at + 128].astype(F32))
            gs, ts = gs.astype(BF), ts.astype(BF)
            q = qkv_ref[h, :, pl.ds(at, 128)]
            k = qkv_ref[h, :, pl.ds(half + at, 128)]
            v = jnp.concatenate([qkv_ref[h, :, pl.ds(2 * half + at, 128)], ones], axis=1)
            none = jnp.zeros_like(q)
            dq = dk = dv = 0.0
            for a in range(2):
                keep = low if a == 0 else ~low
                ga = jnp.where(keep, gs, none)
                pb = p_ref[(h * pairs + pp) * 2 + a, :, :]
                g = mm(jnp.concatenate([ga, jnp.where(keep, ts, none)], axis=1), v, 1, 1)
                ds = (pb.astype(F32) * g).astype(BF)
                dq = dq + mm(ds, jnp.where(keep, k, none))
                dk = dk + mm(ds, jnp.where(keep, q, none), 0, 0)
                dv = dv + mm(pb, ga, 0, 0)
            dqkv_ref[h, :, pl.ds(at, 128)] = (dq * scale).astype(BF)
            dqkv_ref[h, :, pl.ds(half + at, 128)] = (dk * scale).astype(BF)
            dqkv_ref[h, :, pl.ds(2 * half + at, 128)] = dv.astype(BF)


from jax.sharding import PartitionSpec as P

MESH = pl.DeviceIdType.MESH
inv_tau = 20.0
unit_eps = 1e-06
ROWS = 256
SEND = 128
V_PARTS = 4
VMEM_BYTES = 62 * 2**20


CROPS_OF_ROW = 6


def unit_rows(vectors):
    return vectors * lax.rsqrt(jnp.sum(vectors * vectors, axis=-1, keepdims=True) + unit_eps)


def member_rows(seg_row, count):
    return (lax.broadcasted_iota(jnp.int32, (count, seg_row.shape[1]), 0) == seg_row).astype(F32)


def split_mm(member, value):
    high = value.astype(BF)
    rest = (value - high.astype(F32)).astype(BF)
    return mm(member, high) + mm(member, rest)


def forward_kernel(
    hid, w1, w2, queue, segc, segr, small, partner,
    o_qkv, o_p, o_mixed, o_inv, o_xhat, o_rstd, o_x, o_w, o_v, o_head,
    W, V, X, Y, qkv, prob, mixed, inv, yf, xhat, rstd, fq, fk, pool, rows_q, queue_low, part, parts, blocks,
    l_sem, ws, wr, vbs, vbr, vas, var, vzs, vzr, vfs, vfr, hs, hr, acs, acr, o_sem,
    qs, qr, ds, dr, us, ur, bs, br,
):
    s, d, m = lax.axis_index("section"), lax.axis_index("dp"), lax.axis_index("mp")
    last, planes = lax.axis_size("section") - 1, lax.axis_size("dp")
    own_slot, slots = d * 2 + m, 2 * planes
    lane_d = lax.rem(d, 2)
    beside = d + 1 - 2 * lane_d
    other = 1 - m
    seq = X.shape[1]
    chunks = seq // ROWS
    sends = seq // SEND
    n_qkv = qkv.shape[3]
    va_rows = w2.shape[1]
    even = lax.rem(s, 2) == 0
    odd = lax.rem(s, 2) == 1

    barrier = pltpu.get_barrier_semaphore()
    pl.semaphore_signal(barrier, inc=1, device_id={"mp": other}, device_id_type=MESH)

    @pl.when(s > 0)
    def _():
        pl.semaphore_signal(barrier, inc=1, device_id={"section": s - 1}, device_id_type=MESH)

    @pl.when(s < last)
    def _():
        pl.semaphore_signal(barrier, inc=1, device_id={"section": s + 1}, device_id_type=MESH)

    @pl.when(s < last - 1)
    def _():
        pl.semaphore_signal(barrier, inc=1, device_id={"section": last}, device_id_type=MESH)

    @pl.when(s == last)
    def _():
        for t in range(last - 1):
            pl.semaphore_signal(barrier, inc=1, device_id={"section": t}, device_id_type=MESH)

        def greet(i, carry):
            for c in range(2):
                pl.semaphore_signal(
                    barrier, inc=1, device_id={"dp": lax.rem(d + 1 + i, planes), "mp": c}, device_id_type=MESH
                )
            return carry

        lax.fori_loop(0, planes - 1, greet, 0)

    @pl.when(odd & (s < last))
    def _():
        pl.semaphore_signal(barrier, inc=1, device_id={"dp": beside}, device_id_type=MESH)

    pl.semaphore_wait(
        barrier,
        1
        + jnp.where(odd & (s < last), 1, 0)
        + jnp.where(s > 0, 1, 0)
        + jnp.where(s < last, 1, 0)
        + jnp.where(s < last - 1, 1, 0)
        + jnp.where(s == last, last - 1 + 2 * (planes - 1), 0),
    )

    def to_core(src, dst, ss, rs):
        return pltpu.make_async_remote_copy(
            src_ref=src, dst_ref=dst, send_sem=ss, recv_sem=rs,
            device_id={"mp": other}, device_id_type=MESH,
        )

    def to_next(src, dst, ss, rs):
        return pltpu.make_async_remote_copy(
            src_ref=src, dst_ref=dst, send_sem=ss, recv_sem=rs,
            device_id={"section": s + 1}, device_id_type=MESH,
        )

    def w_far(e):
        return to_core(w1.at[e], W.at[e, m], ws.at[e], wr.at[e])

    def w_near(e):
        return pltpu.make_async_copy(w1.at[e], W.at[e, m], l_sem.at[e])

    def vb_far(e):
        return to_core(w2.at[e], V.at[e, m, pl.ds(va_rows, va_rows)], vbs.at[e], vbr.at[e])

    def vb_near(e):
        return pltpu.make_async_copy(w2.at[e], V.at[e, m, pl.ds(va_rows, va_rows)], l_sem.at[2 + e])

    def va_part(e, i, side):
        half = va_rows // 2
        start = jnp.where(lane_d == side, 0, half) + i * (half // V_PARTS)
        return pl.ds(pl.multiple_of(start, half // V_PARTS), half // V_PARTS)

    def va_next(e, i):
        rows = va_part(e, i, 0)
        return to_next(w2.at[e, rows], V.at[e, m, rows], vas.at[e, i], var.at[e, i])

    def va_beside(e, i):
        rows = va_part(e, i, 0)
        return pltpu.make_async_remote_copy(
            src_ref=V.at[e, m, rows], dst_ref=V.at[e, m, rows], send_sem=vzs.at[e, i], recv_sem=vzr.at[e, i],
            device_id={"dp": beside}, device_id_type=MESH,
        )

    def va_core(e, i, side):
        part = V.at[e, m, va_part(e, i, side)]
        return to_core(part, part, vfs.at[e, side, i], vfr.at[e, side, i])

    def hid_far(e):
        return to_core(hid.at[other], X.at[e, pl.ds(pl.multiple_of(m * ROWS, ROWS), ROWS)], hs.at[e], hr.at[e])

    def hid_near(e):
        return pltpu.make_async_copy(
            hid.at[m], X.at[e, pl.ds(pl.multiple_of(m * ROWS, ROWS), ROWS)], l_sem.at[4 + e]
        )

    def act_next(e, c):
        rows = pl.ds(pl.multiple_of(c * SEND, SEND), SEND)
        return to_next(Y.at[e, rows], X.at[e, rows], acs.at[e, c], acr.at[e, c])

    @pl.when(s == 0)
    def _():
        for e in range(2):
            hid_far(e).start()
            hid_near(e).start()

    w_far(0).start()
    w_near(0).start()

    @pl.when(odd)
    def _():
        vb_far(0).start()
        vb_near(0).start()

    @pl.when(even)
    def _():
        for i in range(V_PARTS):
            va_next(0, i).start()

    w_far(1).start()
    w_near(1).start()

    @pl.when(odd)
    def _():
        vb_far(1).start()
        vb_near(1).start()

    @pl.when(s == 0)
    def _():
        for e in range(2):
            hid_far(e).wait_recv()
            hid_near(e).wait()


    def saves(e):
        pairs = [
            (qkv.at[0], o_qkv), (prob, o_p), (mixed.at[0], o_mixed), (inv, o_inv),
            (xhat, o_xhat), (rstd, o_rstd), (X.at[0], o_x), (W.at[0], o_w), (V.at[0], o_v),
        ]
        return [pltpu.make_async_copy(a, b, o_sem.at[i]) for i, (a, b) in enumerate(pairs)]

    def finish(e, rows, resid):
        y, xh, rs = norm_rows(resid, small[e, 1:2, :], small[e, 2:3, :])
        if e == 0:
            xhat[rows, :] = xh
            rstd[rows, :] = jnp.broadcast_to(rs, (rs.shape[0], 128))
        return y

    def wait_w(e):
        w_near(e).wait()
        w_far(e).wait_recv()

    def remote(src, dst, send, recv, **to):
        return pltpu.make_async_remote_copy(
            src_ref=src, dst_ref=dst, send_sem=send, recv_sem=recv, device_id=to, device_id_type=MESH
        )

    def peer(i):
        return lax.rem(own_slot + 1 + i, slots)

    def query_to(i):
        to = peer(i)
        return remote(
            rows_q.at[own_slot], rows_q.at[own_slot], qs.at[i], qr.at[own_slot], dp=to // 2, mp=lax.rem(to, 2)
        )

    def query_from(i):
        slot = peer(i)
        return remote(rows_q.at[slot], rows_q.at[slot], qs.at[i], qr.at[slot], dp=slot // 2, mp=lax.rem(slot, 2))

    def query_down(t):
        return remote(rows_q, rows_q, ds.at[t], dr.at[0], section=t)

    def part_up():
        return remote(part, parts.at[s], us.at[0], ur.at[s], section=last)

    def part_in(t):
        return remote(part, parts.at[t], us.at[0], ur.at[t], section=last)

    def block_to(i):
        to = peer(i)
        return remote(part.at[to], blocks.at[own_slot], bs.at[i], br.at[own_slot], dp=to // 2, mp=lax.rem(to, 2))

    def block_from(i):
        slot = peer(i)
        return remote(part.at[slot], blocks.at[slot], bs.at[i], br.at[slot], dp=slot // 2, mp=lax.rem(slot, 2))

    def each(count, what):
        def one(i, carry):
            what(i)
            return carry

        lax.fori_loop(0, count, one, 0)

    def queue_copy():
        return pltpu.make_async_copy(queue, queue_low, l_sem.at[6])

    def low_queue():
        queue_copy().wait()
        raw = queue_low[...].astype(F32)
        queue_low[...] = unit_rows(raw).astype(BF)

    def queue_share():
        width = queue_low.shape[1]
        query = rows_q[...].reshape(-1, width).astype(BF)
        weight = jnp.exp(mm(query, queue_low[...], 1, 1) * inv_tau - inv_tau)
        high = weight.astype(BF)
        rest = (weight - high.astype(F32)).astype(BF)
        pull = mm(high, queue_low[...]) + mm(rest, queue_low[...])
        sums = jnp.sum(weight, axis=-1, keepdims=True)
        part[:, :, :width] = pull.reshape(slots, 8, width)
        part[:, :, width:] = jnp.broadcast_to(sums, (sums.shape[0], 128)).reshape(slots, 8, 128)

    def share_below():
        query_down(0).wait_recv()
        queue_share()
        part_up().start()

    def share_last():
        rows_q[own_slot] = unit_rows(pool[0]).astype(BF).astype(F32)
        each(slots - 1, lambda i: query_to(i).start())
        each(slots - 1, lambda i: query_from(i).wait_recv())
        for t in range(last):
            query_down(t).start()
        queue_share()

    def share_sum():
        for t in range(last):
            part_in(t).wait_recv()
        part[...] = part[...] + jnp.sum(parts[...], axis=0)
        blocks[own_slot] = part[own_slot]
        each(slots - 1, lambda i: block_to(i).start())

    def head_end():
        width = queue_low.shape[1]
        pick = (lax.broadcasted_iota(jnp.int32, (8, 8), 1) == partner[:, :8]).astype(F32)
        key_low = unit_rows(pool[1]).astype(BF).astype(F32)
        partner_low = jnp.dot(pick, key_low, preferred_element_type=F32)
        query_low = rows_q[own_slot]
        pos = jnp.sum(query_low * partner_low, axis=-1, keepdims=True) * inv_tau
        each(slots - 1, lambda i: block_from(i).wait_recv())
        total = jnp.sum(blocks[...], axis=0)
        pos_weight = jnp.exp(pos - inv_tau)
        denominator = pos_weight + total[:, width : width + 1]
        log_total = inv_tau + jnp.log(denominator)
        member = member_rows(segr[:1, :], 8)
        counts = jnp.sum(member, axis=-1, keepdims=True)
        crops = slots * CROPS_OF_ROW
        real = lax.broadcasted_iota(jnp.int32, (8, 1), 0) < CROPS_OF_ROW
        loss = jnp.sum(jnp.where(real, log_total - pos, 0.0), axis=0, keepdims=True) * (1.0 / crops)
        grad = (total[:, :width] / denominator + (pos_weight / denominator - 1.0) * partner_low) * (
            inv_tau / crops
        )
        vectors = pool[0]
        scale = lax.rsqrt(jnp.sum(vectors * vectors, axis=-1, keepdims=True) + unit_eps)
        inner = jnp.sum(vectors * grad, axis=-1, keepdims=True)
        grad = scale * grad - vectors * (scale * scale * scale * inner)
        o_head[:8, :] = grad / jnp.maximum(counts, 1.0)
        o_head[8:, :] = jnp.broadcast_to(loss, (8, width))

    def attention(e):
        wait_w(e)

        def project(c, carry):
            @pl.when(s > 0)
            def _():
                for i in range(ROWS // SEND):
                    act_next(e, c * (ROWS // SEND) + i).wait_recv()

            r = pl.multiple_of(c * ROWS, ROWS)
            qkv_rows(X[e, pl.ds(r, ROWS), :], W.at[e], qkv.at[e], r, ROWS)
            return carry

        lax.fori_loop(0, chunks, project, 0)

        def attend(c, carry):
            r = pl.multiple_of(c * ROWS, ROWS)
            rows = pl.ds(r, ROWS)
            attend_rows(
                qkv.at[e], fq, fk, prob if e == 0 else None, inv if e == 0 else None, mixed.at[e], r, ROWS
            )
            branch = attn_out(mixed[e, rows, :], W.at[e], n_qkv)
            y = finish(e, rows, X[e, rows, :].astype(F32) + branch + small[e, 0:1, :])
            Y[e, rows, :] = y.astype(BF)
            for i in range(ROWS // SEND):
                act_next(e, c * (ROWS // SEND) + i).start()
            if e == 1:
                pl.when((s > 0) & (c == 0))(share_below)
            return carry

        lax.fori_loop(0, chunks, attend, 0)

    def feed(e):
        for i in range(V_PARTS):
            va_next(e, i).wait_recv()
            va_beside(e, i).start()
            va_core(e, i, 0).start()
        for i in range(V_PARTS):
            va_beside(e, i).wait_recv()
            va_core(e, i, 1).start()
        wait_w(e)
        vb_near(e).wait()
        vb_far(e).wait_recv()
        for i in range(V_PARTS):
            va_core(e, i, 0).wait_recv()
            va_core(e, i, 1).wait_recv()

        def one(c, carry):
            act_next(e, c).wait_recv()
            r = pl.multiple_of(c * SEND, SEND)
            rows = pl.ds(r, SEND)
            x = X[e, rows, :]
            branch = ffn_rows(x, W.at[e], V.at[e], prob if e == 0 else None, r, SEND)
            y = finish(e, rows, x.astype(F32) + branch + small[e, 0:1, :])

            @pl.when(s < last)
            def _():
                Y[e, rows, :] = y.astype(BF)
                act_next(e, c).start()

            @pl.when(s == last)
            def _():
                yf[rows, :] = y

            if e == 1:
                pl.when((s == last) & (c == sends // 2 - 1))(share_sum)
            return carry

        lax.fori_loop(0, sends, one, 0)

        @pl.when(s == last)
        def _():
            member = member_rows(segr[:1, :], 8)
            counts = jnp.sum(member, axis=-1, keepdims=True)
            pool[e] = split_mm(member.astype(BF), yf[...]) / jnp.maximum(counts, 1.0)

    queue_copy().start()

    @pl.when(even)
    def _():
        fq[...], fk[...] = crop_features(segc[...])

    @pl.when(s > 0)
    def _():
        low_queue()

    for e in range(2):
        @pl.when(even)
        def _():
            attention(e)
            if e == 0:
                for i in range(V_PARTS):
                    va_next(1, i).start()

        @pl.when(odd)
        def _():
            feed(e)

        if e == 0:
            pl.when(s == last)(share_last)
            for copy in saves(0):
                copy.start()

    @pl.when(s == 0)
    def _():
        low_queue()

    pl.when(s < last - 1)(share_below)
    pl.when(s == last)(head_end)
    for copy in saves(0):
        copy.wait()

    @pl.when(s < last)
    def _():
        part_up().wait_send()

    @pl.when(s == last)
    def _():
        for t in range(last):
            query_down(t).wait_send()
        each(slots - 1, lambda i: query_to(i).wait_send())
        each(slots - 1, lambda i: block_to(i).wait_send())

    for e in range(2):
        w_far(e).wait_send()

        @pl.when(odd)
        def _():
            vb_far(e).wait_send()
            for i in range(V_PARTS):
                va_beside(e, i).wait_send()
                va_core(e, i, 0).wait_send()
                va_core(e, i, 1).wait_send()

        @pl.when(even)
        def _():
            for i in range(V_PARTS):
                va_next(e, i).wait_send()

        @pl.when(s == 0)
        def _():
            hid_far(e).wait_send()

        @pl.when(s < last)
        def _():
            for c in range(sends):
                act_next(e, c).wait_send()


PIECES = 16
WAIT_ROOT = 2
LAG = 3


def backward_kernel(
    i_qkv, i_p, i_mixed, i_inv, i_xhat, i_rstd, i_x, i_w, i_v, head, segc, small,
    o_gin, o_red, o_sum,
    qkv, prob, mixed, inv, xhat, rstd, X, W, V, G, gout, low, resid, gup, gsplit,
    mine, give, taken, part, sums, loss,
    i_sem, gs, gr, is_, ir, xs, xr, ps, pr, fs, fr, vs, vr, ss, sr, ls, lr,
):
    s, d, m = lax.axis_index("section"), lax.axis_index("dp"), lax.axis_index("mp")
    sections, planes = lax.axis_size("section"), lax.axis_size("dp")
    last = sections - 1
    other = 1 - m
    seq, width = X.shape
    chunks = seq // ROWS
    sends = seq // SEND
    n_qkv = qkv.shape[2]
    cols = W.shape[2]
    even = lax.rem(s, 2) == 0
    odd = lax.rem(s, 2) == 1
    load = {
        name: pltpu.make_async_copy(a, b, i_sem.at[i])
        for i, (name, a, b) in enumerate(
            [("xhat", i_xhat, xhat), ("rstd", i_rstd, rstd), ("v", i_v, V), ("p", i_p, prob), ("w", i_w, W),
             ("x", i_x, X), ("qkv", i_qkv, qkv), ("mixed", i_mixed, mixed), ("inv", i_inv, inv)]
        )
    }
    for name in ("xhat", "rstd"):
        load[name].start()
    pl.when(odd)(load["v"].start)
    for name in ("p", "w", "x"):
        load[name].start()

    @pl.when(even)
    def _():
        for name in ("qkv", "mixed", "inv"):
            load[name].start()

    barrier = pltpu.get_barrier_semaphore()
    for t in range(sections):
        for c in range(2):
            @pl.when((s != t) | (m != c))
            def _():
                pl.semaphore_signal(barrier, inc=1, device_id={"section": t, "mp": c}, device_id_type=MESH)

    def greet(i, carry):
        to = lax.rem(d + 1 + i, planes)
        for c in range(2):
            pl.semaphore_signal(barrier, inc=1, device_id={"dp": to, "mp": c}, device_id_type=MESH)
        return carry

    lax.fori_loop(0, planes - 1, greet, 0)
    pl.semaphore_wait(barrier, 2 * sections - 1 + 2 * (planes - 1))

    def remote(src, dst, send, recv, **to):
        return pltpu.make_async_remote_copy(
            src_ref=src, dst_ref=dst, send_sem=send, recv_sem=recv, device_id=to, device_id_type=MESH
        )

    def grad_prev(c):
        rows = pl.ds(pl.multiple_of(c * SEND, SEND), SEND)
        return remote(gout.at[rows], G.at[rows], gs.at[c], gr.at[c], section=s - 1)

    def spread(t, c):
        return remote(
            gsplit.at[t, pl.ds(c * ROWS, ROWS)], o_gin.at[m], is_.at[t * 2 + c], ir.at[m], section=t, mp=c
        )

    load["xhat"].wait()
    load["rstd"].wait()

    own_slot = d * 2 + m
    sums[own_slot] = jnp.zeros_like(sums[own_slot])

    @pl.when(s == last)
    def _():
        sums[own_slot, 3:4, :] = head[8:9, :]

    def through_norm(rows, g):
        xh = xhat[rows, :]
        grad = norm_back(g, xh, rstd[rows, :1], small[1:2, :])
        sums[own_slot, 0:1, :] += jnp.sum(grad, axis=0, keepdims=True)
        sums[own_slot, 1:2, :] += jnp.sum(g * xh, axis=0, keepdims=True)
        sums[own_slot, 2:3, :] += jnp.sum(g, axis=0, keepdims=True)
        resid[rows, :] = grad
        low[rows, :] = grad.astype(BF)

    def exchange(kind):
        return remote(give.at[kind], taken.at[kind], xs.at[kind], xr.at[kind], mp=other)

    def sum_to(i):
        to = lax.rem(own_slot + 1 + i, 2 * planes)
        return remote(
            sums.at[own_slot], sums.at[own_slot], ss.at[i], sr.at[own_slot], dp=to // 2, mp=lax.rem(to, 2)
        )

    def sum_from(i):
        slot = lax.rem(own_slot + 1 + i, 2 * planes)
        return remote(sums.at[slot], sums.at[slot], ss.at[i], sr.at[slot], dp=slot // 2, mp=lax.rem(slot, 2))

    def start_sums():
        def one(i, carry):
            sum_to(i).start()
            return carry

        lax.fori_loop(0, 2 * planes - 1, one, 0)

    @pl.when(odd)
    def _():
        for name in ("v", "p", "w", "x"):
            load[name].wait()

        def one(c, carry):
            r = pl.multiple_of(c * SEND, SEND)
            rows = pl.ds(r, SEND)

            @pl.when(s == last)
            def _():
                own = (lax.broadcasted_iota(jnp.int32, (SEND, 8), 1) == segc[rows, :8]).astype(BF)
                through_norm(rows, split_mm(own, head[:8, :]))

            @pl.when(s < last)
            def _():
                grad_prev(c).wait_recv()
                through_norm(rows, G[rows, :].astype(F32))

            dx = ffn_back_rows(low[rows, :], W, V, prob, gup, r, SEND)
            gout[rows, :] = (resid[rows, :] + dx).astype(BF)
            grad_prev(c).start()
            return carry

        lax.fori_loop(0, sends, one, 0)
        start_sums()
        unit = 256
        for h, out in ((other, give), (m, mine)):
            for c in range(cols // unit):
                act = prob[h * (cols // 512) + c * unit // 512, :, c * unit % 512 : c * unit % 512 + unit]
                r, q = c * unit % width, c * unit // width * width
                out[0, r : r + unit, q : q + width] = mm(act, low[...], 0, 0).astype(BF)
            if out is give:
                exchange(0).start()
        for h, out in ((other, give), (m, mine)):
            for c in range(0, cols, 512):
                out[1, :, c : c + 512] = mm(X[...], gup[h, :, c : c + 512], 0, 0).astype(BF)
            if out is give:
                exchange(1).start()
        exchange(0).wait_recv()

    @pl.when(even)
    def _():
        for name in ("p", "w", "x", "qkv", "mixed", "inv"):
            load[name].wait()

        def one(c, carry):
            rows = pl.ds(pl.multiple_of(c * SEND, SEND), SEND)
            grad_prev(c).wait_recv()
            through_norm(rows, G[rows, :].astype(F32))
            return carry

        lax.fori_loop(0, sends, one, 0)
        start_sums()
        attn_back_core(low, W, qkv, prob, inv, mixed, gup, n_qkv)

        def back(c, carry):
            rows = pl.ds(pl.multiple_of(c * ROWS, ROWS), ROWS)
            dx = mm(gup[0, rows, :n_qkv], W[0, :, :n_qkv], 1, 1) + mm(
                gup[1, rows, :n_qkv], W[1, :, :n_qkv], 1, 1
            )
            grad = (resid[rows, :] + dx).astype(BF)

            @pl.when(s > 0)
            def _():
                gout[rows, :] = grad
                for i in range(ROWS // SEND):
                    grad_prev(c * (ROWS // SEND) + i).start()

            @pl.when(s == 0)
            def _():
                part_width = gsplit.shape[2]
                for t in range(sections):
                    gsplit[t, rows, :] = grad[:, t * part_width : (t + 1) * part_width]

            return carry

        lax.fori_loop(0, chunks, back, 0)

        @pl.when(s == 0)
        def _():
            for t in range(sections):
                for c in range(2):
                    if t > 0:
                        spread(t, c).start()
                    else:
                        @pl.when(m != c)
                        def _():
                            spread(t, c).start()

                        @pl.when(m == c)
                        def _():
                            pltpu.make_async_copy(
                                gsplit.at[t, pl.ds(c * ROWS, ROWS)], o_gin.at[m], is_.at[t * 2 + c]
                            ).start()

        half = n_qkv // 3
        for h, out in ((other, give), (m, mine)):
            for c in range(0, n_qkv, half):
                out[1, :, c : c + half] = mm(X[...], gup[h, :, c : c + half], 0, 0).astype(BF)
            for k in range(2):
                @pl.when(h == k)
                def _():
                    out[1, :, n_qkv:] = mm(low[...], mixed[:, k * half : (k + 1) * half], 0, 0).astype(BF)
            if out is give:
                exchange(1).start()

    exchange(1).wait_recv()

    step_rows = width // PIECES
    root_a, root_b = (planes - 1) // 2, planes // 2
    first = jnp.where(odd, 0, PIECES)
    total = 2 * PIECES
    lag = WAIT_ROOT + LAG * jnp.maximum(root_b - d, d - root_a)

    def place(i):
        kind = i // PIECES
        rows = pl.ds(pl.multiple_of(lax.rem(i, PIECES) * step_rows, step_rows), step_rows)
        root = jnp.where(lax.rem(i, 2) == 0, root_a, root_b)
        return kind, rows, root

    def part_right(i):
        kind, rows, _ = place(i)
        return remote(mine.at[kind, rows], part.at[0, kind, rows], ps.at[i], pr.at[0, i], dp=d + 1)

    def part_left(i):
        kind, rows, _ = place(i)
        return remote(mine.at[kind, rows], part.at[1, kind, rows], ps.at[i], pr.at[1, i], dp=d - 1)

    def whole(i, side, src):
        kind, rows, _ = place(i)
        return remote(src.at[kind, rows], o_red.at[kind, rows], fs.at[side, i], fr.at[i], dp=d + (1 if side else -1))

    def keep_root(i):
        kind, rows, _ = place(i)
        return pltpu.make_async_copy(mine.at[kind, rows], o_red.at[kind, rows], fr.at[i])

    def down_prev(i):
        _, rows, _ = place(i)
        return remote(
            o_red.at[0, rows, pl.ds(0, width)], o_red.at[0, rows, pl.ds(width, width)],
            vs.at[i], vr.at[i], section=s - 1,
        )

    def add(i, *sides):
        kind, rows, _ = place(i)
        value = mine[kind, rows, :].astype(F32) + taken[kind, rows, :].astype(F32)
        for side in sides:
            value = value + part[side, kind, rows, :].astype(F32)
        mine[kind, rows, :] = value.astype(BF)

    def pieces(i, carry):
        root = place(i)[2]

        @pl.when((i < total) & (d < root))
        def _():
            @pl.when(d > 0)
            def _():
                part_right(i).wait_recv()
                add(i, 0)

            @pl.when(d == 0)
            def _():
                add(i)

            part_right(i).start()

        @pl.when((i < total) & (d > root))
        def _():
            @pl.when(d < planes - 1)
            def _():
                part_left(i).wait_recv()
                add(i, 1)

            @pl.when(d == planes - 1)
            def _():
                add(i)

            part_left(i).start()

        k = i - WAIT_ROOT

        @pl.when((k >= first) & (k < total) & (d == place(k)[2]))
        def _():
            part_right(k).wait_recv()
            part_left(k).wait_recv()
            add(k, 0, 1)
            keep_root(k).start()
            whole(k, 0, mine).start()
            whole(k, 1, mine).start()

        @pl.when(i >= first + lag)
        def _():
            j = i - lag
            kind, _, root = place(j)
            keep_root(j).wait()

            @pl.when((d < root) & (d > 0))
            def _():
                whole(j, 0, o_red).start()

            @pl.when((d > root) & (d < planes - 1))
            def _():
                whole(j, 1, o_red).start()

            @pl.when(kind == 0)
            def _():
                down_prev(j).start()

        return carry

    lax.fori_loop(first, total + lag, pieces, 0)

    def settle(i, carry):
        kind, rows, root = place(i)

        @pl.when(d != root)
        def _():
            part_right(i).wait_send()

        @pl.when((d <= root) & (d > 0))
        def _():
            whole(i, 0, mine).wait_send()

        @pl.when((d >= root) & (d < planes - 1))
        def _():
            whole(i, 1, mine).wait_send()

        @pl.when(kind == 0)
        def _():
            down_prev(i).wait_send()

        return carry

    lax.fori_loop(first, total, settle, 0)

    @pl.when(even)
    def _():
        def arrive(i, carry):
            down_prev(i).wait_recv()
            return carry

        lax.fori_loop(0, PIECES, arrive, 0)

    @pl.when(odd)
    def _():
        exchange(0).wait_send()

    exchange(1).wait_send()

    @pl.when(s > 0)
    def _():
        for c in range(sends):
            grad_prev(c).wait_send()

    @pl.when(s == 0)
    def _():
        for t in range(sections):
            for c in range(2):
                if t > 0:
                    spread(t, c).wait_send()
                else:
                    @pl.when(m != c)
                    def _():
                        spread(t, c).wait_send()

                    @pl.when(m == c)
                    def _():
                        pltpu.make_async_copy(
                            gsplit.at[t, pl.ds(c * ROWS, ROWS)], o_gin.at[m], is_.at[t * 2 + c]
                        ).wait()

    def arrival(r):
        return remote(gsplit.at[0, pl.ds(0, ROWS)], o_gin.at[r], is_.at[0], ir.at[r], section=0, mp=r)

    for r in range(2):
        @pl.when((s != 0) | (m != r))
        def _():
            arrival(r).wait_recv()

    def sums_in(i, carry):
        sum_from(i).wait_recv()
        sum_to(i).wait_send()
        return carry

    def loss_down(t):
        return remote(loss, loss, ls.at[t], lr.at[0], section=t)

    lax.fori_loop(0, 2 * planes - 1, sums_in, 0)
    total_sums = jnp.sum(sums[...], axis=0)

    @pl.when(s == last)
    def _():
        loss[...] = total_sums
        for t in range(last):
            loss_down(t).start()
        for t in range(last):
            loss_down(t).wait_send()

    @pl.when(s < last)
    def _():
        loss_down(0).wait_recv()

    o_sum[...] = total_sums
    o_sum[3:4, :] = loss[3:4, :]


def local(
    hidden_in, segments, partners, queue, first_weight, second_weight, out_bias, ln_gain, ln_bias
):
    m = lax.axis_index("mp")
    width = hidden_in.shape[-1]
    seq = segments.shape[1]
    w1 = first_weight.reshape(2, width, -1)
    w2 = second_weight.reshape(2, -1, width)
    cols = w1.shape[2]
    n_qkv = cols // 4 * 3
    heads = 2 * (cols // 4) // HD
    own_segments = lax.dynamic_index_in_dim(segments, m, 0, keepdims=False)
    own_partners = lax.dynamic_index_in_dim(partners, m, 0, keepdims=False)
    segc = jnp.broadcast_to(own_segments[:, None], (seq, 128))
    segr = jnp.broadcast_to(own_segments[None, :], (8, seq))
    small = jnp.stack([out_bias[:, 0], ln_gain[:, 0], ln_bias[:, 0]], axis=1)
    small = jnp.pad(small, ((0, 0), (0, 5), (0, 0)))
    anyspace = pl.BlockSpec(memory_space=pl.ANY)
    vmem = pl.BlockSpec(memory_space=pltpu.VMEM)
    shape = jax.ShapeDtypeStruct
    dma = pltpu.SemaphoreType.DMA
    saved = [
        shape((2, seq, n_qkv), BF), shape((heads, seq, seq), BF), shape((seq, width), BF),
        shape((heads // 2, seq, 128), F32), shape((seq, width), F32), shape((seq, 128), F32), shape((seq, width), BF), shape((2, width, cols), BF),
        shape((2, cols, width), BF),
    ]
    sections, planes = lax.axis_size("section"), lax.axis_size("dp")
    crops = partners.shape[1]
    partner = jnp.broadcast_to(jnp.pad(own_partners, (0, 8 - crops), constant_values=-1)[:, None], (8, 128))
    *kept, head = pl.pallas_call(
        forward_kernel,
        out_shape=saved + [shape((16, width), F32)],
        in_specs=[anyspace] * 4 + [vmem] * 4,
        out_specs=[anyspace] * 9 + [vmem],
        scratch_shapes=[
            pltpu.VMEM((2, 2, width, cols), BF), pltpu.VMEM((2, 2, cols, width), BF),
            pltpu.VMEM((2, seq, width), BF), pltpu.VMEM((2, seq, width), BF),
            pltpu.VMEM((2, 2, seq, n_qkv), BF), pltpu.VMEM((heads, seq, seq), BF),
            pltpu.VMEM((2, seq, width), BF), pltpu.VMEM((heads // 2, seq, 128), F32), pltpu.VMEM((seq, width), F32),
            pltpu.VMEM((seq, width), F32), pltpu.VMEM((seq, 128), F32),
            pltpu.VMEM((seq, 128), BF), pltpu.VMEM((seq, 128), BF),
            pltpu.VMEM((2, 8, width), F32), pltpu.VMEM((2 * planes, 8, width), F32),
            pltpu.VMEM(queue.shape, BF), pltpu.VMEM((2 * planes, 8, width + 128), F32),
            pltpu.VMEM((sections - 1, 2 * planes, 8, width + 128), F32),
            pltpu.VMEM((2 * planes, 8, width + 128), F32),
            dma((7,)), dma((2,)), dma((2,)), dma((2,)), dma((2,)), dma((2, V_PARTS)), dma((2, V_PARTS)),
            dma((2, V_PARTS)), dma((2, V_PARTS)), dma((2, 2, V_PARTS)), dma((2, 2, V_PARTS)),
            dma((2,)), dma((2,)), dma((2, seq // SEND)), dma((2, seq // SEND)), dma((9,)),
            dma((2 * planes,)), dma((2 * planes,)), dma((sections - 1,)), dma((1,)), dma((1,)),
            dma((sections - 1,)), dma((2 * planes,)), dma((2 * planes,)),
        ],
        compiler_params=pltpu.CompilerParams(
            collective_id=0, has_side_effects=True, vmem_limit_bytes=VMEM_BYTES
        ),
        name="forward",
    )(hidden_in, w1, w2, queue, segc, segr, small, partner)
    half_width = width // lax.axis_size("section")
    gin, red, sums = pl.pallas_call(
        backward_kernel,
        out_shape=[
            shape((2, seq // 2, half_width), BF), shape((2, width, cols), BF), shape((8, width), F32),
        ],
        in_specs=[anyspace] * 9 + [vmem] * 3,
        out_specs=[vmem, anyspace, vmem],
        scratch_shapes=[pltpu.VMEM(a.shape, a.dtype) for a in saved]
        + [
            pltpu.VMEM((seq, width), BF), pltpu.VMEM((seq, width), BF), pltpu.VMEM((seq, width), BF),
            pltpu.VMEM((seq, width), F32), pltpu.VMEM((2, seq, cols), BF),
            pltpu.VMEM((sections, seq, half_width), BF),
            pltpu.VMEM((2, width, cols), BF), pltpu.VMEM((2, width, cols), BF),
            pltpu.VMEM((2, width, cols), BF), pltpu.VMEM((2, 2, width, cols), BF),
            pltpu.VMEM((2 * planes, 8, width), F32), pltpu.VMEM((8, width), F32),
            dma((9,)), dma((seq // SEND,)), dma((seq // SEND,)), dma((2 * sections,)), dma((2,)),
            dma((2,)), dma((2,)), dma((2 * PIECES,)), dma((2, 2 * PIECES)), dma((2, 2 * PIECES)),
            dma((2 * PIECES,)), dma((PIECES,)), dma((PIECES,)), dma((2 * planes,)), dma((2 * planes,)),
            dma((sections - 1,)), dma((1,)),
        ],
        compiler_params=pltpu.CompilerParams(
            collective_id=1, has_side_effects=True, vmem_limit_bytes=VMEM_BYTES
        ),
        name="backward",
    )(*kept, head, segc, small[0])
    grad_first = red[1].astype(F32).reshape(width, 4, -1)
    grad_second = red[0, :, width:].astype(F32).reshape(second_weight.shape[2:])
    return (
        sums[3, 0], gin, grad_first[None], grad_second[None], sums[0:1], sums[1:2], sums[2:3],
    )


def solution(mesh):
    in_specs = (
        P("dp", "mp", None), P("dp", None), P("dp", None), P(("section", "dp", "mp"), None),
        P(None, "section", None, None, "mp"), P(None, "section", None, "mp", None),
        P(None, "section", None), P(None, "section", None), P(None, "section", None),
    )
    out_specs = (
        P(), P("dp", "mp", "section"), P("section", None, None, "mp"), P("section", None, "mp", None),
        P("section", None), P("section", None), P("section", None),
    )
    return jax.shard_map(local, mesh=mesh, in_specs=in_specs, out_specs=out_specs, check_vma=False)
```

```python
import functools
import jax
import jax.numpy as jnp
from jax import lax
from jax.experimental import pallas as pl
from jax.experimental.pallas import tpu as pltpu

F32 = jnp.float32
BF = jnp.bfloat16
HD = 64
NEG = -1e30
LN_EPS = 1e-12


def mm(a, b, ca=1, cb=0):
    return lax.dot_general(a, b, (((ca,), (cb,)), ((), ())), preferred_element_type=F32)


def norm_rows(resid, gain, shift):
    centre = resid - jnp.mean(resid, axis=-1, keepdims=True)
    spread = jnp.mean(centre * centre, axis=-1, keepdims=True)
    rstd = lax.rsqrt(spread + LN_EPS)
    xhat = centre * rstd
    return xhat * gain + shift, xhat, rstd


def norm_back(g, xhat, rstd, gain):
    gg = g * gain
    m1 = jnp.mean(gg, axis=-1, keepdims=True)
    m2 = jnp.mean(gg * xhat, axis=-1, keepdims=True)
    return rstd * (gg - m1 - xhat * m2)


def lane_low(shape):
    return lax.broadcasted_iota(jnp.int32, shape, len(shape) - 1) < HD


def qkv_rows(x, w_ref, qkv_ref, row0, rows):
    for h in range(2):
        n = qkv_ref.shape[2]
        qkv_ref[h, pl.ds(row0, rows), :] = mm(x, w_ref[h, :, :n]).astype(BF)


def crop_features(seg_col):
    lane = lax.broadcasted_iota(jnp.int32, seg_col.shape, 1)
    hit = lane == seg_col
    as_query = jnp.where(hit, NEG, 0.0).astype(BF)
    as_key = jnp.where(hit | (lane >= 8), 0.0, 1.0).astype(BF)
    return as_query, as_key


def attend_rows(qkv_ref, fq_ref, fk_ref, p_ref, inv_ref, mixed_ref, row0, rows):
    half = qkv_ref.shape[2] // 3
    pairs = half // 128
    low = lane_low((rows, 128))
    fq = fq_ref[pl.ds(row0, rows), :]
    fk = fk_ref[...]
    ones = jnp.ones((fk.shape[0], 128), BF)
    for h in range(2):
        for pp in range(pairs):
            q = qkv_ref[h, pl.ds(row0, rows), pl.ds(pp * 128, 128)] * jnp.asarray(HD ** -0.5, BF)
            k = jnp.concatenate([qkv_ref[h, :, pl.ds(half + pp * 128, 128)], fk], axis=1)
            v = jnp.concatenate([qkv_ref[h, :, pl.ds(2 * half + pp * 128, 128)], ones], axis=1)
            outs, invs = [], []
            for a in range(2):
                qa = jnp.where(low if a == 0 else ~low, q, jnp.zeros_like(q))
                s = mm(jnp.concatenate([qa, fq], axis=1), k, 1, 1)
                p = jnp.exp(s - jnp.max(s, axis=-1, keepdims=True)).astype(BF)
                if p_ref is not None:
                    p_ref[(h * pairs + pp) * 2 + a, pl.ds(row0, rows), :] = p
                o = mm(p, v)
                inv = 1.0 / o[:, 128:]
                outs.append(o[:, :128] * inv)
                invs.append(inv)
            if inv_ref is not None:
                inv_ref[h * pairs + pp, pl.ds(row0, rows), :] = jnp.where(low, invs[0], invs[1])
            mixed_ref[pl.ds(row0, rows), pl.ds(h * half + pp * 128, 128)] = jnp.where(
                low, outs[0], outs[1]
            ).astype(BF)


def attn_out(mixed, w_ref, n_qkv):
    half = mixed.shape[1] // 2
    return mm(mixed[:, :half], w_ref[0, :, n_qkv:], 1, 1) + mm(
        mixed[:, half:], w_ref[1, :, n_qkv:], 1, 1
    )


def gelu_parts(up, want_slope):
    cdf = 0.5 * (1.0 + lax.erf(up * (0.5 ** 0.5)))
    act = up * cdf
    if not want_slope:
        return act, None
    slope = cdf + up * (jnp.exp(-0.5 * up * up) * 0.3989422804014327)
    return act, slope


def ffn_rows(x, w_ref, v_ref, keep_ref, row0, rows, tile=512):
    acc = None
    for h in range(2):
        n = w_ref.shape[2]
        for c in range(0, n, tile):
            up = mm(x, w_ref[h, :, c : c + tile])
            act, slope = gelu_parts(up, keep_ref is not None)
            act = act.astype(BF)
            if keep_ref is not None:
                at = (h * n + c) // tile
                keep_ref[at, pl.ds(row0, rows), :] = act
                keep_ref[keep_ref.shape[0] // 2 + at, pl.ds(row0, rows), :] = slope.astype(BF)
            part = mm(act, v_ref[h, c : c + tile, :])
            acc = part if acc is None else acc + part
    return acc


def ffn_back_rows(low, w_ref, v_ref, keep_ref, gup_ref, row0, rows, tile=512):
    acc = None
    for h in range(2):
        n = w_ref.shape[2]
        for c in range(0, n, tile):
            dact = mm(low, v_ref[h, c : c + tile, :], 1, 1)
            at = keep_ref.shape[0] // 2 + (h * n + c) // tile
            gup = (dact * keep_ref[at, pl.ds(row0, rows), :].astype(F32)).astype(BF)
            gup_ref[h, pl.ds(row0, rows), c : c + tile] = gup
            part = mm(gup, w_ref[h, :, c : c + tile], 1, 1)
            acc = part if acc is None else acc + part
    return acc


def attn_back_core(low_ref, w_ref, qkv_ref, p_ref, inv_ref, mixed_ref, dqkv_ref, n_qkv):
    half = n_qkv // 3
    pairs = half // 128
    seq = low_ref.shape[0]
    low = lane_low((seq, 128))
    ones = jnp.ones((seq, 128), BF)
    scale = HD ** -0.5
    for h in range(2):
        for pp in range(pairs):
            at = pp * 128
            gm = mm(low_ref[...], w_ref[h, :, n_qkv + at : n_qkv + at + 128]).astype(BF)
            gs = gm.astype(F32) * inv_ref[h * pairs + pp]
            ts = -(gs * mixed_ref[:, h * half + at : h * half + at + 128].astype(F32))
            gs, ts = gs.astype(BF), ts.astype(BF)
            q = qkv_ref[h, :, pl.ds(at, 128)]
            k = qkv_ref[h, :, pl.ds(half + at, 128)]
            v = jnp.concatenate([qkv_ref[h, :, pl.ds(2 * half + at, 128)], ones], axis=1)
            none = jnp.zeros_like(q)
            dq = dk = dv = 0.0
            for a in range(2):
                keep = low if a == 0 else ~low
                ga = jnp.where(keep, gs, none)
                pb = p_ref[(h * pairs + pp) * 2 + a, :, :]
                g = mm(jnp.concatenate([ga, jnp.where(keep, ts, none)], axis=1), v, 1, 1)
                ds = (pb.astype(F32) * g).astype(BF)
                dq = dq + mm(ds, jnp.where(keep, k, none))
                dk = dk + mm(ds, jnp.where(keep, q, none), 0, 0)
                dv = dv + mm(pb, ga, 0, 0)
            dqkv_ref[h, :, pl.ds(at, 128)] = (dq * scale).astype(BF)
            dqkv_ref[h, :, pl.ds(half + at, 128)] = (dk * scale).astype(BF)
            dqkv_ref[h, :, pl.ds(2 * half + at, 128)] = dv.astype(BF)


from jax.sharding import PartitionSpec as P

MESH = pl.DeviceIdType.MESH
inv_tau = 20.0
unit_eps = 1e-06
ROWS = 256
SEND = 128
V_PARTS = 4
VMEM_BYTES = 62 * 2**20


CROPS_OF_ROW = 6


def unit_rows(vectors):
    return vectors * lax.rsqrt(jnp.sum(vectors * vectors, axis=-1, keepdims=True) + unit_eps)


def member_rows(seg_row, count):
    return (lax.broadcasted_iota(jnp.int32, (count, seg_row.shape[1]), 0) == seg_row).astype(F32)


def split_mm(member, value):
    high = value.astype(BF)
    rest = (value - high.astype(F32)).astype(BF)
    return mm(member, high) + mm(member, rest)


def forward_kernel(
    hid, w1, w2, queue, segments, partners, out_bias, ln_gain, ln_bias,
    o_qkv, o_p, o_mixed, o_inv, o_xhat, o_rstd, o_x, o_w, o_v, o_head,
    W, V, X, Y, qkv, prob, mixed, inv, yf, xhat, rstd, fq, fk, pick, pool, rows_q, queue_low, part, parts, blocks,
    l_sem, wl, ws, wr, vbs, vbr, vas, var, vzs, vzr, vfs, vfr, hs, hr, acs, acr, o_sem,
    qs, qr, ds, dr, us, ur, bs, br,
):
    s, d, m = lax.axis_index("section"), lax.axis_index("dp"), lax.axis_index("mp")
    last, planes = lax.axis_size("section") - 1, lax.axis_size("dp")
    own_slot, slots = d * 2 + m, 2 * planes
    lane_d = lax.rem(d, 2)
    beside = d + 1 - 2 * lane_d
    other = 1 - m
    seq = X.shape[1]
    chunks = seq // ROWS
    sends = seq // SEND
    n_qkv = qkv.shape[3]
    va_rows = w2.shape[1]
    even = lax.rem(s, 2) == 0
    odd = lax.rem(s, 2) == 1

    barrier = pltpu.get_barrier_semaphore()
    pl.semaphore_signal(barrier, inc=1, device_id={"mp": other}, device_id_type=MESH)

    @pl.when(s > 0)
    def _():
        pl.semaphore_signal(barrier, inc=1, device_id={"section": s - 1}, device_id_type=MESH)

    @pl.when(s < last)
    def _():
        pl.semaphore_signal(barrier, inc=1, device_id={"section": s + 1}, device_id_type=MESH)

    @pl.when(s < last - 1)
    def _():
        pl.semaphore_signal(barrier, inc=1, device_id={"section": last}, device_id_type=MESH)

    @pl.when(s == last)
    def _():
        for t in range(last - 1):
            pl.semaphore_signal(barrier, inc=1, device_id={"section": t}, device_id_type=MESH)

        def greet(i, carry):
            for c in range(2):
                pl.semaphore_signal(
                    barrier, inc=1, device_id={"dp": lax.rem(d + 1 + i, planes), "mp": c}, device_id_type=MESH
                )
            return carry

        lax.fori_loop(0, planes - 1, greet, 0)

    @pl.when(odd & (s < last))
    def _():
        pl.semaphore_signal(barrier, inc=1, device_id={"dp": beside}, device_id_type=MESH)

    pl.semaphore_wait(
        barrier,
        1
        + jnp.where(odd & (s < last), 1, 0)
        + jnp.where(s > 0, 1, 0)
        + jnp.where(s < last, 1, 0)
        + jnp.where(s < last - 1, 1, 0)
        + jnp.where(s == last, last - 1 + 2 * (planes - 1), 0),
    )

    def to_core(src, dst, ss, rs):
        return pltpu.make_async_remote_copy(
            src_ref=src, dst_ref=dst, send_sem=ss, recv_sem=rs,
            device_id={"mp": other}, device_id_type=MESH,
        )

    def to_next(src, dst, ss, rs):
        return pltpu.make_async_remote_copy(
            src_ref=src, dst_ref=dst, send_sem=ss, recv_sem=rs,
            device_id={"section": s + 1}, device_id_type=MESH,
        )

    def w_place(e, j):
        half = w1.shape[3]
        return W.at[e, m, :, pl.ds(j * half, half)]

    def w_far(e, j):
        return to_core(w1.at[e, j], w_place(e, j), ws.at[e, j], wr.at[e, j])

    def w_near(e, j):
        return pltpu.make_async_copy(w1.at[e, j], w_place(e, j), wl.at[e, j])

    def vb_far(e):
        return to_core(w2.at[e], V.at[e, m, pl.ds(va_rows, va_rows)], vbs.at[e], vbr.at[e])

    def vb_near(e):
        return pltpu.make_async_copy(w2.at[e], V.at[e, m, pl.ds(va_rows, va_rows)], l_sem.at[2 + e])

    seg_row = jnp.where(m == 0, segments[0:1, :], segments[1:2, :])

    def va_part(e, i, side):
        half = va_rows // 2
        start = jnp.where(lane_d == side, 0, half) + i * (half // V_PARTS)
        return pl.ds(pl.multiple_of(start, half // V_PARTS), half // V_PARTS)

    def va_next(e, i):
        rows = va_part(e, i, 0)
        return to_next(w2.at[e, rows], V.at[e, m, rows], vas.at[e, i], var.at[e, i])

    def va_beside(e, i):
        rows = va_part(e, i, 0)
        return pltpu.make_async_remote_copy(
            src_ref=V.at[e, m, rows], dst_ref=V.at[e, m, rows], send_sem=vzs.at[e, i], recv_sem=vzr.at[e, i],
            device_id={"dp": beside}, device_id_type=MESH,
        )

    def va_core(e, i, side):
        part = V.at[e, m, va_part(e, i, side)]
        return to_core(part, part, vfs.at[e, side, i], vfr.at[e, side, i])

    def hid_far(e):
        return to_core(hid.at[other], X.at[e, pl.ds(pl.multiple_of(m * ROWS, ROWS), ROWS)], hs.at[e], hr.at[e])

    def hid_near(e):
        return pltpu.make_async_copy(
            hid.at[m], X.at[e, pl.ds(pl.multiple_of(m * ROWS, ROWS), ROWS)], l_sem.at[4 + e]
        )

    def act_next(e, c):
        rows = pl.ds(pl.multiple_of(c * SEND, SEND), SEND)
        return to_next(Y.at[e, rows], X.at[e, rows], acs.at[e, c], acr.at[e, c])

    @pl.when(s == 0)
    def _():
        for e in range(2):
            hid_far(e).start()
            hid_near(e).start()

    for j in range(4):
        w_far(0, j).start()
        w_near(0, j).start()

    @pl.when(odd)
    def _():
        vb_far(0).start()
        vb_near(0).start()

    @pl.when(even)
    def _():
        for i in range(V_PARTS):
            va_next(0, i).start()

    for j in range(4):
        w_far(1, j).start()
        w_near(1, j).start()

    @pl.when(odd)
    def _():
        vb_far(1).start()
        vb_near(1).start()

    @pl.when(s == 0)
    def _():
        for e in range(2):
            hid_far(e).wait_recv()
            hid_near(e).wait()


    def saves(e):
        pairs = [
            (qkv.at[0], o_qkv), (prob, o_p), (mixed.at[0], o_mixed), (inv, o_inv),
            (xhat, o_xhat), (rstd, o_rstd), (X.at[0], o_x), (W.at[0], o_w), (V.at[0], o_v),
        ]
        return [pltpu.make_async_copy(a, b, o_sem.at[i]) for i, (a, b) in enumerate(pairs)]

    def finish(e, rows, resid):
        y, xh, rs = norm_rows(resid, ln_gain[e], ln_bias[e])
        if e == 0:
            xhat[rows, :] = xh
            rstd[rows, :] = jnp.broadcast_to(rs, (rs.shape[0], 128))
        return y

    def wait_w(e):
        for j in range(4):
            w_near(e, j).wait()
            w_far(e, j).wait_recv()

    def remote(src, dst, send, recv, **to):
        return pltpu.make_async_remote_copy(
            src_ref=src, dst_ref=dst, send_sem=send, recv_sem=recv, device_id=to, device_id_type=MESH
        )

    def peer(i):
        return lax.rem(own_slot + 1 + i, slots)

    def query_to(i):
        to = peer(i)
        return remote(
            rows_q.at[own_slot], rows_q.at[own_slot], qs.at[i], qr.at[own_slot], dp=to // 2, mp=lax.rem(to, 2)
        )

    def query_from(i):
        slot = peer(i)
        return remote(rows_q.at[slot], rows_q.at[slot], qs.at[i], qr.at[slot], dp=slot // 2, mp=lax.rem(slot, 2))

    def query_down(t):
        return remote(rows_q, rows_q, ds.at[t], dr.at[0], section=t)

    def part_up():
        return remote(part, parts.at[s], us.at[0], ur.at[s], section=last)

    def part_in(t):
        return remote(part, parts.at[t], us.at[0], ur.at[t], section=last)

    def block_to(i):
        to = peer(i)
        return remote(part.at[to], blocks.at[own_slot], bs.at[i], br.at[own_slot], dp=to // 2, mp=lax.rem(to, 2))

    def block_from(i):
        slot = peer(i)
        return remote(part.at[slot], blocks.at[slot], bs.at[i], br.at[slot], dp=slot // 2, mp=lax.rem(slot, 2))

    def each(count, what):
        def one(i, carry):
            what(i)
            return carry

        lax.fori_loop(0, count, one, 0)

    def queue_copy():
        return pltpu.make_async_copy(queue, queue_low, l_sem.at[6])

    def low_queue():
        queue_copy().wait()
        raw = queue_low[...].astype(F32)
        queue_low[...] = unit_rows(raw).astype(BF)

    def queue_share():
        width = queue_low.shape[1]
        query = rows_q[...].reshape(-1, width).astype(BF)
        weight = jnp.exp(mm(query, queue_low[...], 1, 1) * inv_tau - inv_tau)
        high = weight.astype(BF)
        rest = (weight - high.astype(F32)).astype(BF)
        pull = mm(high, queue_low[...]) + mm(rest, queue_low[...])
        sums = jnp.sum(weight, axis=-1, keepdims=True)
        part[:, :, :width] = pull.reshape(slots, 8, width)
        part[:, :, width:] = jnp.broadcast_to(sums, (sums.shape[0], 128)).reshape(slots, 8, 128)

    def share_below():
        query_down(0).wait_recv()
        queue_share()
        part_up().start()

    def share_last():
        rows_q[own_slot] = unit_rows(pool[0]).astype(BF).astype(F32)
        each(slots - 1, lambda i: query_to(i).start())
        each(slots - 1, lambda i: query_from(i).wait_recv())
        for t in range(last):
            query_down(t).start()
        queue_share()

    def share_sum():
        for t in range(last):
            part_in(t).wait_recv()
        part[...] = part[...] + jnp.sum(parts[...], axis=0)
        blocks[own_slot] = part[own_slot]
        each(slots - 1, lambda i: block_to(i).start())

    def head_end():
        width = queue_low.shape[1]
        pick[...] = jnp.full(pick.shape, -1, jnp.int32)
        pick[0:1, :CROPS_OF_ROW] = jnp.where(m == 0, partners[0:1, :], partners[1:2, :])
        chosen = (lax.broadcasted_iota(jnp.int32, (8, 8), 0) == pick[0:1, :8]).astype(F32)
        key_low = unit_rows(pool[1]).astype(BF).astype(F32)
        partner_low = mm(chosen, key_low, 0, 0)
        query_low = rows_q[own_slot]
        pos = jnp.sum(query_low * partner_low, axis=-1, keepdims=True) * inv_tau
        each(slots - 1, lambda i: block_from(i).wait_recv())
        total = jnp.sum(blocks[...], axis=0)
        pos_weight = jnp.exp(pos - inv_tau)
        denominator = pos_weight + total[:, width : width + 1]
        log_total = inv_tau + jnp.log(denominator)
        member = member_rows(seg_row, 8)
        counts = jnp.sum(member, axis=-1, keepdims=True)
        crops = slots * CROPS_OF_ROW
        real = lax.broadcasted_iota(jnp.int32, (8, 1), 0) < CROPS_OF_ROW
        loss = jnp.sum(jnp.where(real, log_total - pos, 0.0), axis=0, keepdims=True) * (1.0 / crops)
        grad = (total[:, :width] / denominator + (pos_weight / denominator - 1.0) * partner_low) * (
            inv_tau / crops
        )
        vectors = pool[0]
        scale = lax.rsqrt(jnp.sum(vectors * vectors, axis=-1, keepdims=True) + unit_eps)
        inner = jnp.sum(vectors * grad, axis=-1, keepdims=True)
        grad = scale * grad - vectors * (scale * scale * scale * inner)
        o_head[:8, :] = grad / jnp.maximum(counts, 1.0)
        o_head[8:, :] = jnp.broadcast_to(loss, (8, width))

    def attention(e):
        wait_w(e)

        def project(c, carry):
            @pl.when(s > 0)
            def _():
                for i in range(ROWS // SEND):
                    act_next(e, c * (ROWS // SEND) + i).wait_recv()

            r = pl.multiple_of(c * ROWS, ROWS)
            qkv_rows(X[e, pl.ds(r, ROWS), :], W.at[e], qkv.at[e], r, ROWS)
            return carry

        lax.fori_loop(0, chunks, project, 0)

        def attend(c, carry):
            r = pl.multiple_of(c * ROWS, ROWS)
            rows = pl.ds(r, ROWS)
            attend_rows(
                qkv.at[e], fq, fk, prob if e == 0 else None, inv if e == 0 else None, mixed.at[e], r, ROWS
            )
            branch = attn_out(mixed[e, rows, :], W.at[e], n_qkv)
            y = finish(e, rows, X[e, rows, :].astype(F32) + branch + out_bias[e])
            Y[e, rows, :] = y.astype(BF)
            for i in range(ROWS // SEND):
                act_next(e, c * (ROWS // SEND) + i).start()
            if e == 1:
                pl.when((s > 0) & (c == 0))(share_below)
            return carry

        lax.fori_loop(0, chunks, attend, 0)

    def feed(e):
        for i in range(V_PARTS):
            va_next(e, i).wait_recv()
            va_beside(e, i).start()
            va_core(e, i, 0).start()
        for i in range(V_PARTS):
            va_beside(e, i).wait_recv()
            va_core(e, i, 1).start()
        wait_w(e)
        vb_near(e).wait()
        vb_far(e).wait_recv()
        for i in range(V_PARTS):
            va_core(e, i, 0).wait_recv()
            va_core(e, i, 1).wait_recv()

        def one(c, carry):
            act_next(e, c).wait_recv()
            r = pl.multiple_of(c * SEND, SEND)
            rows = pl.ds(r, SEND)
            x = X[e, rows, :]
            branch = ffn_rows(x, W.at[e], V.at[e], prob if e == 0 else None, r, SEND)
            y = finish(e, rows, x.astype(F32) + branch + out_bias[e])

            @pl.when(s < last)
            def _():
                Y[e, rows, :] = y.astype(BF)
                act_next(e, c).start()

            @pl.when(s == last)
            def _():
                yf[rows, :] = y

            if e == 1:
                pl.when((s == last) & (c == sends // 2 - 1))(share_sum)
            return carry

        lax.fori_loop(0, sends, one, 0)

        @pl.when(s == last)
        def _():
            member = member_rows(seg_row, 8)
            counts = jnp.sum(member, axis=-1, keepdims=True)
            pool[e] = split_mm(member.astype(BF), yf[...]) / jnp.maximum(counts, 1.0)

    queue_copy().start()

    @pl.when(even)
    def _():
        across = jnp.broadcast_to(seg_row.astype(F32), (128, seq))
        fq[...], fk[...] = crop_features(across.T.astype(jnp.int32))

    @pl.when(s > 0)
    def _():
        low_queue()

    for e in range(2):
        @pl.when(even)
        def _():
            attention(e)
            if e == 0:
                for i in range(V_PARTS):
                    va_next(1, i).start()

        @pl.when(odd)
        def _():
            feed(e)

        if e == 0:
            pl.when(s == last)(share_last)
            for copy in saves(0):
                copy.start()

    @pl.when(s == 0)
    def _():
        low_queue()

    pl.when(s < last - 1)(share_below)
    pl.when(s == last)(head_end)
    for copy in saves(0):
        copy.wait()

    @pl.when(s < last)
    def _():
        part_up().wait_send()

    @pl.when(s == last)
    def _():
        for t in range(last):
            query_down(t).wait_send()
        each(slots - 1, lambda i: query_to(i).wait_send())
        each(slots - 1, lambda i: block_to(i).wait_send())

    for e in range(2):
        for j in range(4):
            w_far(e, j).wait_send()

        @pl.when(odd)
        def _():
            vb_far(e).wait_send()
            for i in range(V_PARTS):
                va_beside(e, i).wait_send()
                va_core(e, i, 0).wait_send()
                va_core(e, i, 1).wait_send()

        @pl.when(even)
        def _():
            for i in range(V_PARTS):
                va_next(e, i).wait_send()

        @pl.when(s == 0)
        def _():
            hid_far(e).wait_send()

        @pl.when(s < last)
        def _():
            for c in range(sends):
                act_next(e, c).wait_send()


PIECES = 8
ADOPTED = 3
WAIT_ROOT = 2
LAG = 3


def backward_kernel(
    i_qkv, i_p, i_mixed, i_inv, i_xhat, i_rstd, i_x, i_w, i_v, head, segments, ln_gain,
    o_gin, o_w, o_v, o_sum,
    qkv, prob, mixed, inv, xhat, rstd, X, W, V, G, gout, low, resid, gup, gsplit,
    mine, give, taken, part, leave, received, belong, sums, loss,
    i_sem, gs, gr, is_, ir, xs, xr, ps, pr, fs, fr, as_, ar, vs, vr, ss, sr, ls, lr,
):
    s, d, m = lax.axis_index("section"), lax.axis_index("dp"), lax.axis_index("mp")
    sections, planes = lax.axis_size("section"), lax.axis_size("dp")
    last = sections - 1
    other = 1 - m
    seq, width = X.shape
    chunks = seq // ROWS
    sends = seq // SEND
    n_qkv = qkv.shape[2]
    cols = W.shape[2]
    even = lax.rem(s, 2) == 0
    odd = lax.rem(s, 2) == 1
    load = {
        name: pltpu.make_async_copy(a, b, i_sem.at[i])
        for i, (name, a, b) in enumerate(
            [("xhat", i_xhat, xhat), ("rstd", i_rstd, rstd), ("v", i_v, V), ("p", i_p, prob), ("w", i_w, W),
             ("x", i_x, X), ("qkv", i_qkv, qkv), ("mixed", i_mixed, mixed), ("inv", i_inv, inv)]
        )
    }
    for name in ("xhat", "rstd"):
        load[name].start()
    pl.when(odd)(load["v"].start)
    for name in ("p", "w", "x"):
        load[name].start()

    @pl.when(even)
    def _():
        for name in ("qkv", "mixed", "inv"):
            load[name].start()

    barrier = pltpu.get_barrier_semaphore()
    for t in range(sections):
        for c in range(2):
            @pl.when((s != t) | (m != c))
            def _():
                pl.semaphore_signal(barrier, inc=1, device_id={"section": t, "mp": c}, device_id_type=MESH)

    def greet(i, carry):
        to = lax.rem(d + 1 + i, planes)
        for c in range(2):
            pl.semaphore_signal(barrier, inc=1, device_id={"dp": to, "mp": c}, device_id_type=MESH)
        return carry

    lax.fori_loop(0, planes - 1, greet, 0)
    pl.semaphore_wait(barrier, 2 * sections - 1 + 2 * (planes - 1))

    def remote(src, dst, send, recv, **to):
        return pltpu.make_async_remote_copy(
            src_ref=src, dst_ref=dst, send_sem=send, recv_sem=recv, device_id=to, device_id_type=MESH
        )

    def grad_prev(c):
        rows = pl.ds(pl.multiple_of(c * SEND, SEND), SEND)
        return remote(gout.at[rows], G.at[rows], gs.at[c], gr.at[c], section=s - 1)

    def spread(t, c):
        return remote(
            gsplit.at[t, pl.ds(c * ROWS, ROWS)], o_gin.at[m], is_.at[t * 2 + c], ir.at[m], section=t, mp=c
        )

    load["xhat"].wait()
    load["rstd"].wait()

    own_slot = d * 2 + m
    sums[own_slot] = jnp.zeros_like(sums[own_slot])

    @pl.when(s == last)
    def _():
        sums[own_slot, 3:4, :] = head[8:9, :]
        belong[...] = member_rows(jnp.where(m == 0, segments[0:1, :], segments[1:2, :]), 8)

    @pl.when(s >= last - 1)
    def _():
        taken[ADOPTED] = jnp.zeros_like(taken[ADOPTED])

    def through_norm(rows, g):
        xh = xhat[rows, :]
        grad = norm_back(g, xh, rstd[rows, :1], ln_gain[0])
        sums[own_slot, 0:1, :] += jnp.sum(grad, axis=0, keepdims=True)
        sums[own_slot, 1:2, :] += jnp.sum(g * xh, axis=0, keepdims=True)
        sums[own_slot, 2:3, :] += jnp.sum(g, axis=0, keepdims=True)
        resid[rows, :] = grad
        low[rows, :] = grad.astype(BF)

    half = cols // 4
    step_rows = width // PIECES

    def exchange(slot):
        to = received if slot == ADOPTED else taken.at[slot]
        return remote(give.at[slot], to, xs.at[slot], xr.at[slot], mp=other)

    def adopt(i):
        rows = pl.ds(pl.multiple_of(i * step_rows, step_rows), step_rows)
        to = jnp.where(s == last, last - 1, last)
        return remote(leave.at[rows], mine.at[ADOPTED, rows], as_.at[i], ar.at[i], section=to)

    def weight_grads(left, right, count):
        for h, out in ((other, give), (m, mine)):
            for j in range(4):
                at = slice(j % 2 * half, j % 2 * half + half)
                if j * half < count:
                    out[1 + j // 2, :, at] = mm(left[...], right[h, :, j * half : (j + 1) * half], 0, 0).astype(BF)
                else:
                    for k in range(2):
                        @pl.when(h == k)
                        def _():
                            out[1 + j // 2, :, at] = mm(
                                low[...], mixed[:, k * half : (k + 1) * half], 0, 0
                            ).astype(BF)
                if out is give and j % 2:
                    exchange(1 + j // 2).start()

    def sum_to(i):
        to = lax.rem(own_slot + 1 + i, 2 * planes)
        return remote(
            sums.at[own_slot], sums.at[own_slot], ss.at[i], sr.at[own_slot], dp=to // 2, mp=lax.rem(to, 2)
        )

    def sum_from(i):
        slot = lax.rem(own_slot + 1 + i, 2 * planes)
        return remote(sums.at[slot], sums.at[slot], ss.at[i], sr.at[slot], dp=slot // 2, mp=lax.rem(slot, 2))

    def start_sums():
        def one(i, carry):
            sum_to(i).start()
            return carry

        lax.fori_loop(0, 2 * planes - 1, one, 0)

    @pl.when(odd)
    def _():
        for name in ("v", "p", "w", "x"):
            load[name].wait()

        def one(c, carry):
            r = pl.multiple_of(c * SEND, SEND)
            rows = pl.ds(r, SEND)

            @pl.when(s == last)
            def _():
                own = belong[:, pl.ds(r, SEND)]
                high = head[:8, :].astype(BF).astype(F32)
                through_norm(rows, mm(own, high, 0, 0) + mm(own, head[:8, :] - high, 0, 0))

            @pl.when(s < last)
            def _():
                grad_prev(c).wait_recv()
                through_norm(rows, G[rows, :].astype(F32))

            dx = ffn_back_rows(low[rows, :], W, V, prob, gup, r, SEND)
            gout[rows, :] = (resid[rows, :] + dx).astype(BF)
            grad_prev(c).start()
            return carry

        lax.fori_loop(0, sends, one, 0)
        start_sums()
        unit = 256
        for h, out in ((other, give), (m, mine)):
            for c in range(cols // unit):
                act = prob[h * (cols // 512) + c * unit // 512, :, c * unit % 512 : c * unit % 512 + unit]
                grad = mm(act, low[...], 0, 0).astype(BF)
                r = c * unit % width
                if c * unit < width and out is mine:
                    leave[r : r + unit, :] = grad
                else:
                    out[ADOPTED if c * unit < width else 0, r : r + unit, :] = grad
            if out is give:
                exchange(ADOPTED).start()
                exchange(0).start()
        exchange(ADOPTED).wait_recv()

        def hand_over(i, carry):
            rows = pl.ds(pl.multiple_of(i * step_rows, step_rows), step_rows)
            leave[rows, :] = (leave[rows, :].astype(F32) + received[rows, :].astype(F32)).astype(BF)
            adopt(i).start()
            return carry

        lax.fori_loop(0, PIECES, hand_over, 0)
        weight_grads(X, gup, cols)
        exchange(0).wait_recv()

    @pl.when(even)
    def _():
        for name in ("p", "w", "x", "qkv", "mixed", "inv"):
            load[name].wait()

        def one(c, carry):
            rows = pl.ds(pl.multiple_of(c * SEND, SEND), SEND)
            grad_prev(c).wait_recv()
            through_norm(rows, G[rows, :].astype(F32))
            return carry

        lax.fori_loop(0, sends, one, 0)
        start_sums()
        attn_back_core(low, W, qkv, prob, inv, mixed, gup, n_qkv)

        def back(c, carry):
            rows = pl.ds(pl.multiple_of(c * ROWS, ROWS), ROWS)
            dx = mm(gup[0, rows, :n_qkv], W[0, :, :n_qkv], 1, 1) + mm(
                gup[1, rows, :n_qkv], W[1, :, :n_qkv], 1, 1
            )
            grad = (resid[rows, :] + dx).astype(BF)

            @pl.when(s > 0)
            def _():
                gout[rows, :] = grad
                for i in range(ROWS // SEND):
                    grad_prev(c * (ROWS // SEND) + i).start()

            @pl.when(s == 0)
            def _():
                part_width = gsplit.shape[2]
                for t in range(sections):
                    gsplit[t, rows, :] = grad[:, t * part_width : (t + 1) * part_width]

            return carry

        lax.fori_loop(0, chunks, back, 0)

        @pl.when(s == 0)
        def _():
            for t in range(sections):
                for c in range(2):
                    if t > 0:
                        spread(t, c).start()
                    else:
                        @pl.when(m != c)
                        def _():
                            spread(t, c).start()

                        @pl.when(m == c)
                        def _():
                            pltpu.make_async_copy(
                                gsplit.at[t, pl.ds(c * ROWS, ROWS)], o_gin.at[m], is_.at[t * 2 + c]
                            ).start()

        weight_grads(X, gup, n_qkv)

    for slot in (1, 2):
        exchange(slot).wait_recv()

    root_a, root_b = (planes - 1) // 2, planes // 2
    first = jnp.where(odd, 0, PIECES)
    total = jnp.where(s >= last - 1, 4 * PIECES, 3 * PIECES)
    lag = WAIT_ROOT + LAG * jnp.maximum(root_b - d, d - root_a)

    def place(i):
        slot = i // PIECES
        rows = pl.ds(pl.multiple_of(lax.rem(i, PIECES) * step_rows, step_rows), step_rows)
        root = jnp.where(lax.rem(i, 2) == 0, root_a, root_b)
        return slot, rows, root

    def part_right(i):
        slot, rows, _ = place(i)
        return remote(mine.at[slot, rows], part.at[0, slot, rows], ps.at[i], pr.at[0, i], dp=d + 1)

    def part_left(i):
        slot, rows, _ = place(i)
        return remote(mine.at[slot, rows], part.at[1, slot, rows], ps.at[i], pr.at[1, i], dp=d - 1)

    def at_home(i, what):
        slot, rows, _ = place(i)
        for k in range(4):
            @pl.when(slot == k)
            def _():
                if k in (1, 2):
                    what(o_w.at[rows, pl.ds((k - 1) * width, width)])
                else:
                    what(o_v.at[k // 3, rows])

    def send_whole(i, side, home_too):
        slot, rows, _ = place(i)

        def go(home):
            source = home if home_too else mine.at[slot, rows]
            remote(source, home, fs.at[side, i], fr.at[i], dp=d + (1 if side else -1)).start()

        at_home(i, go)

    def keep_root(i):
        slot, rows, _ = place(i)
        at_home(i, lambda home: pltpu.make_async_copy(mine.at[slot, rows], home, fr.at[i]).start())

    def whole_here(i):
        slot, rows, _ = place(i)
        pltpu.make_async_copy(mine.at[slot, rows], mine.at[slot, rows], fr.at[i]).wait()

    def whole_sent(i, side):
        slot, rows, _ = place(i)
        remote(mine.at[slot, rows], mine.at[slot, rows], fs.at[side, i], fr.at[i], dp=d).wait_send()

    def bring_home(i):
        rows = pl.ds(pl.multiple_of(i * step_rows, step_rows), step_rows)
        return remote(o_v.at[1, rows], o_v.at[1, rows], vs.at[i], vr.at[i], section=0)

    def add(i, *sides):
        slot, rows, _ = place(i)
        value = mine[slot, rows, :].astype(F32) + taken[slot, rows, :].astype(F32)
        for side in sides:
            value = value + part[side, slot, rows, :].astype(F32)
        mine[slot, rows, :] = value.astype(BF)

    def adopted_here(i):
        @pl.when(i >= ADOPTED * PIECES)
        def _():
            adopt(i - ADOPTED * PIECES).wait_recv()

    def pieces(i, carry):
        root = place(i)[2]

        @pl.when((i < total) & (d < root))
        def _():
            adopted_here(i)

            @pl.when(d > 0)
            def _():
                part_right(i).wait_recv()
                add(i, 0)

            @pl.when(d == 0)
            def _():
                add(i)

            part_right(i).start()

        @pl.when((i < total) & (d > root))
        def _():
            adopted_here(i)

            @pl.when(d < planes - 1)
            def _():
                part_left(i).wait_recv()
                add(i, 1)

            @pl.when(d == planes - 1)
            def _():
                add(i)

            part_left(i).start()

        k = i - WAIT_ROOT

        @pl.when((k >= first) & (k < total) & (d == place(k)[2]))
        def _():
            adopted_here(k)
            part_right(k).wait_recv()
            part_left(k).wait_recv()
            add(k, 0, 1)
            keep_root(k)
            send_whole(k, 0, False)
            send_whole(k, 1, False)

        @pl.when(i >= first + lag)
        def _():
            j = i - lag
            root = place(j)[2]
            whole_here(j)

            @pl.when((d < root) & (d > 0))
            def _():
                send_whole(j, 0, True)

            @pl.when((d > root) & (d < planes - 1))
            def _():
                send_whole(j, 1, True)

            @pl.when((s == last) & (j >= ADOPTED * PIECES))
            def _():
                bring_home(j - ADOPTED * PIECES).start()

        return carry

    lax.fori_loop(first, total + lag, pieces, 0)

    def settle(i, carry):
        root = place(i)[2]

        @pl.when(d != root)
        def _():
            part_right(i).wait_send()

        @pl.when((d <= root) & (d > 0))
        def _():
            whole_sent(i, 0)

        @pl.when((d >= root) & (d < planes - 1))
        def _():
            whole_sent(i, 1)

        return carry

    lax.fori_loop(first, total, settle, 0)

    def brought(i, carry):
        @pl.when(s == 0)
        def _():
            bring_home(i).wait_recv()

        @pl.when(s == last)
        def _():
            bring_home(i).wait_send()

        @pl.when(odd)
        def _():
            adopt(i).wait_send()

        return carry

    lax.fori_loop(0, PIECES, brought, 0)

    @pl.when(odd)
    def _():
        exchange(0).wait_send()
        exchange(ADOPTED).wait_send()

    for slot in (1, 2):
        exchange(slot).wait_send()

    @pl.when(s > 0)
    def _():
        for c in range(sends):
            grad_prev(c).wait_send()

    @pl.when(s == 0)
    def _():
        for t in range(sections):
            for c in range(2):
                if t > 0:
                    spread(t, c).wait_send()
                else:
                    @pl.when(m != c)
                    def _():
                        spread(t, c).wait_send()

                    @pl.when(m == c)
                    def _():
                        pltpu.make_async_copy(
                            gsplit.at[t, pl.ds(c * ROWS, ROWS)], o_gin.at[m], is_.at[t * 2 + c]
                        ).wait()

    def arrival(r):
        return remote(gsplit.at[0, pl.ds(0, ROWS)], o_gin.at[r], is_.at[0], ir.at[r], section=0, mp=r)

    for r in range(2):
        @pl.when((s != 0) | (m != r))
        def _():
            arrival(r).wait_recv()

    def sums_in(i, carry):
        sum_from(i).wait_recv()
        sum_to(i).wait_send()
        return carry

    def loss_down(t):
        return remote(loss, loss, ls.at[t], lr.at[0], section=t)

    lax.fori_loop(0, 2 * planes - 1, sums_in, 0)
    total_sums = jnp.sum(sums[...], axis=0)

    @pl.when(s == last)
    def _():
        loss[...] = total_sums
        for t in range(last):
            loss_down(t).start()
        for t in range(last):
            loss_down(t).wait_send()

    @pl.when(s < last)
    def _():
        loss_down(0).wait_recv()

    o_sum[...] = total_sums
    o_sum[3:4, :] = loss[3:4, :]


def local(
    hidden_in, segments, partners, queue, first_weight, second_weight, out_bias, ln_gain, ln_bias
):
    width = hidden_in.shape[-1]
    seq = segments.shape[1]
    w1 = jnp.transpose(first_weight[:, 0], (0, 2, 1, 3))
    w2 = second_weight.reshape(2, -1, width)
    half = w1.shape[3]
    cols, n_qkv, heads = 4 * half, 3 * half, 2 * half // HD
    anyspace = pl.BlockSpec(memory_space=pl.ANY)
    vmem = pl.BlockSpec(memory_space=pltpu.VMEM)
    shape = jax.ShapeDtypeStruct
    dma = pltpu.SemaphoreType.DMA
    saved = [
        shape((2, seq, n_qkv), BF), shape((heads, seq, seq), BF), shape((seq, width), BF),
        shape((heads // 2, seq, 128), F32), shape((seq, width), F32), shape((seq, 128), F32), shape((seq, width), BF), shape((2, width, cols), BF),
        shape((2, cols, width), BF),
    ]
    sections, planes = lax.axis_size("section"), lax.axis_size("dp")
    *kept, head = pl.pallas_call(
        forward_kernel,
        out_shape=saved + [shape((16, width), F32)],
        in_specs=[anyspace] * 4 + [vmem] * 5,
        out_specs=[anyspace] * 9 + [vmem],
        scratch_shapes=[
            pltpu.VMEM((2, 2, width, cols), BF), pltpu.VMEM((2, 2, cols, width), BF),
            pltpu.VMEM((2, seq, width), BF), pltpu.VMEM((2, seq, width), BF),
            pltpu.VMEM((2, 2, seq, n_qkv), BF), pltpu.VMEM((heads, seq, seq), BF),
            pltpu.VMEM((2, seq, width), BF), pltpu.VMEM((heads // 2, seq, 128), F32), pltpu.VMEM((seq, width), F32),
            pltpu.VMEM((seq, width), F32), pltpu.VMEM((seq, 128), F32),
            pltpu.VMEM((seq, 128), BF), pltpu.VMEM((seq, 128), BF), pltpu.VMEM((8, 128), jnp.int32),
            pltpu.VMEM((2, 8, width), F32), pltpu.VMEM((2 * planes, 8, width), F32),
            pltpu.VMEM(queue.shape, BF), pltpu.VMEM((2 * planes, 8, width + 128), F32),
            pltpu.VMEM((sections - 1, 2 * planes, 8, width + 128), F32),
            pltpu.VMEM((2 * planes, 8, width + 128), F32),
            dma((7,)), dma((2, 4)), dma((2, 4)), dma((2, 4)), dma((2,)), dma((2,)), dma((2, V_PARTS)), dma((2, V_PARTS)),
            dma((2, V_PARTS)), dma((2, V_PARTS)), dma((2, 2, V_PARTS)), dma((2, 2, V_PARTS)),
            dma((2,)), dma((2,)), dma((2, seq // SEND)), dma((2, seq // SEND)), dma((9,)),
            dma((2 * planes,)), dma((2 * planes,)), dma((sections - 1,)), dma((1,)), dma((1,)),
            dma((sections - 1,)), dma((2 * planes,)), dma((2 * planes,)),
        ],
        compiler_params=pltpu.CompilerParams(
            collective_id=0, has_side_effects=True, vmem_limit_bytes=VMEM_BYTES
        ),
        name="forward",
    )(hidden_in, w1, w2, queue, segments, partners, out_bias, ln_gain, ln_bias)
    half_width = width // lax.axis_size("section")
    gin, gw, gv, sums = pl.pallas_call(
        backward_kernel,
        out_shape=[
            shape((2, seq // 2, half_width), BF), shape((width, cols), BF), shape((2, width, width), BF),
            shape((8, width), F32),
        ],
        in_specs=[anyspace] * 9 + [vmem] * 3,
        out_specs=[vmem, anyspace, anyspace, vmem],
        scratch_shapes=[pltpu.VMEM(a.shape, a.dtype) for a in saved]
        + [
            pltpu.VMEM((seq, width), BF), pltpu.VMEM((seq, width), BF), pltpu.VMEM((seq, width), BF),
            pltpu.VMEM((seq, width), F32), pltpu.VMEM((2, seq, cols), BF),
            pltpu.VMEM((sections, seq, half_width), BF),
            pltpu.VMEM((4, width, width), BF), pltpu.VMEM((4, width, width), BF),
            pltpu.VMEM((4, width, width), BF), pltpu.VMEM((2, 4, width, width), BF),
            pltpu.VMEM((width, width), BF), pltpu.VMEM((width, width), BF), pltpu.VMEM((8, seq), F32),
            pltpu.VMEM((2 * planes, 8, width), F32), pltpu.VMEM((8, width), F32),
            dma((9,)), dma((seq // SEND,)), dma((seq // SEND,)), dma((2 * sections,)), dma((2,)),
            dma((4,)), dma((4,)), dma((4 * PIECES,)), dma((2, 4 * PIECES)), dma((2, 4 * PIECES)),
            dma((4 * PIECES,)), dma((PIECES,)), dma((PIECES,)), dma((PIECES,)), dma((PIECES,)), dma((2 * planes,)), dma((2 * planes,)),
            dma((sections - 1,)), dma((1,)),
        ],
        compiler_params=pltpu.CompilerParams(
            collective_id=1, has_side_effects=True, vmem_limit_bytes=VMEM_BYTES
        ),
        name="backward",
    )(*kept, head, segments, ln_gain)
    grad_first = gw.astype(F32).reshape(width, 4, -1)
    odd = lax.axis_index("section") % 2 == 1
    grad_second = jnp.where(odd, gv[0], gv[1]).astype(F32).reshape(second_weight.shape[2:])
    return (
        sums[3, 0], gin, grad_first[None], grad_second[None], sums[0:1], sums[1:2], sums[2:3],
    )


def solution(mesh):
    in_specs = (
        P("dp", "mp", None), P("dp", None), P("dp", None), P(("section", "dp", "mp"), None),
        P(None, "section", None, None, "mp"), P(None, "section", None, "mp", None),
        P(None, "section", None), P(None, "section", None), P(None, "section", None),
    )
    out_specs = (
        P(), P("dp", "mp", "section"), P("section", None, None, "mp"), P("section", None, "mp", None),
        P("section", None), P("section", None), P("section", None),
    )
    return jax.shard_map(local, mesh=mesh, in_specs=in_specs, out_specs=out_specs, check_vma=False)
```

```python
import functools
import jax
import jax.numpy as jnp
from jax import lax
from jax.experimental import pallas as pl
from jax.experimental.pallas import tpu as pltpu

F32 = jnp.float32
BF = jnp.bfloat16
HD = 64
NEG = -1e30
LN_EPS = 1e-12


def mm(a, b, ca=1, cb=0):
    return lax.dot_general(a, b, (((ca,), (cb,)), ((), ())), preferred_element_type=F32)


def norm_rows(resid, gain, shift):
    centre = resid - jnp.mean(resid, axis=-1, keepdims=True)
    spread = jnp.mean(centre * centre, axis=-1, keepdims=True)
    rstd = lax.rsqrt(spread + LN_EPS)
    xhat = centre * rstd
    return xhat * gain + shift, xhat, rstd


def norm_back(g, xhat, rstd, gain):
    gg = g * gain
    m1 = jnp.mean(gg, axis=-1, keepdims=True)
    m2 = jnp.mean(gg * xhat, axis=-1, keepdims=True)
    return rstd * (gg - m1 - xhat * m2)


def lane_low(shape):
    return lax.broadcasted_iota(jnp.int32, shape, len(shape) - 1) < HD


def qkv_rows(x, w_ref, qkv_ref, row0, rows):
    for h in range(2):
        n = qkv_ref.shape[2]
        qkv_ref[h, pl.ds(row0, rows), :] = mm(x, w_ref[h, :, :n]).astype(BF)


def crop_features(seg_col):
    lane = lax.broadcasted_iota(jnp.int32, seg_col.shape, 1)
    hit = lane == seg_col
    as_query = jnp.where(hit, NEG, 0.0).astype(BF)
    as_key = jnp.where(hit | (lane >= 8), 0.0, 1.0).astype(BF)
    return as_query, as_key


def attend_rows(qkv_ref, fq_ref, fk_ref, p_ref, inv_ref, mixed_ref, row0, rows):
    half = qkv_ref.shape[2] // 3
    pairs = half // 128
    low = lane_low((rows, 128))
    fq = fq_ref[pl.ds(row0, rows), :]
    fk = fk_ref[...]
    ones = jnp.ones((fk.shape[0], 128), BF)
    for h in range(2):
        for pp in range(pairs):
            q = qkv_ref[h, pl.ds(row0, rows), pl.ds(pp * 128, 128)] * jnp.asarray(HD ** -0.5, BF)
            k = jnp.concatenate([qkv_ref[h, :, pl.ds(half + pp * 128, 128)], fk], axis=1)
            v = jnp.concatenate([qkv_ref[h, :, pl.ds(2 * half + pp * 128, 128)], ones], axis=1)
            outs, invs = [], []
            for a in range(2):
                qa = jnp.where(low if a == 0 else ~low, q, jnp.zeros_like(q))
                s = mm(jnp.concatenate([qa, fq], axis=1), k, 1, 1)
                p = jnp.exp(s - jnp.max(s, axis=-1, keepdims=True)).astype(BF)
                if p_ref is not None:
                    p_ref[(h * pairs + pp) * 2 + a, pl.ds(row0, rows), :] = p
                o = mm(p, v)
                inv = 1.0 / o[:, 128:]
                outs.append(o[:, :128] * inv)
                invs.append(inv)
            if inv_ref is not None:
                inv_ref[h * pairs + pp, pl.ds(row0, rows), :] = jnp.where(low, invs[0], invs[1])
            mixed_ref[pl.ds(row0, rows), pl.ds(h * half + pp * 128, 128)] = jnp.where(
                low, outs[0], outs[1]
            ).astype(BF)


def attn_out(mixed, w_ref, n_qkv):
    half = mixed.shape[1] // 2
    return mm(mixed[:, :half], w_ref[0, :, n_qkv:], 1, 1) + mm(
        mixed[:, half:], w_ref[1, :, n_qkv:], 1, 1
    )


def gelu_parts(up, want_slope):
    cdf = 0.5 * (1.0 + lax.erf(up * (0.5 ** 0.5)))
    act = up * cdf
    if not want_slope:
        return act, None
    slope = cdf + up * (jnp.exp(-0.5 * up * up) * 0.3989422804014327)
    return act, slope


def ffn_rows(x, w_ref, v_ref, keep_ref, row0, rows, tile=512):
    acc = None
    for h in range(2):
        n = w_ref.shape[2]
        for c in range(0, n, tile):
            up = mm(x, w_ref[h, :, c : c + tile])
            act, slope = gelu_parts(up, keep_ref is not None)
            act = act.astype(BF)
            if keep_ref is not None:
                at = (h * n + c) // tile
                keep_ref[at, pl.ds(row0, rows), :] = act
                keep_ref[keep_ref.shape[0] // 2 + at, pl.ds(row0, rows), :] = slope.astype(BF)
            part = mm(act, v_ref[h, c : c + tile, :])
            acc = part if acc is None else acc + part
    return acc


def ffn_back_rows(low, w_ref, v_ref, keep_ref, gup_ref, row0, rows, tile=512):
    acc = None
    for h in range(2):
        n = w_ref.shape[2]
        for c in range(0, n, tile):
            dact = mm(low, v_ref[h, c : c + tile, :], 1, 1)
            at = keep_ref.shape[0] // 2 + (h * n + c) // tile
            gup = (dact * keep_ref[at, pl.ds(row0, rows), :].astype(F32)).astype(BF)
            gup_ref[h, pl.ds(row0, rows), c : c + tile] = gup
            part = mm(gup, w_ref[h, :, c : c + tile], 1, 1)
            acc = part if acc is None else acc + part
    return acc


def attn_back_core(low_ref, w_ref, qkv_ref, p_ref, inv_ref, mixed_ref, dqkv_ref, n_qkv):
    half = n_qkv // 3
    pairs = half // 128
    seq = low_ref.shape[0]
    low = lane_low((seq, 128))
    ones = jnp.ones((seq, 128), BF)
    scale = HD ** -0.5
    for h in range(2):
        for pp in range(pairs):
            at = pp * 128
            gm = mm(low_ref[...], w_ref[h, :, n_qkv + at : n_qkv + at + 128]).astype(BF)
            gs = gm.astype(F32) * inv_ref[h * pairs + pp]
            ts = -(gs * mixed_ref[:, h * half + at : h * half + at + 128].astype(F32))
            gs, ts = gs.astype(BF), ts.astype(BF)
            q = qkv_ref[h, :, pl.ds(at, 128)]
            k = qkv_ref[h, :, pl.ds(half + at, 128)]
            v = jnp.concatenate([qkv_ref[h, :, pl.ds(2 * half + at, 128)], ones], axis=1)
            none = jnp.zeros_like(q)
            dq = dk = dv = 0.0
            for a in range(2):
                keep = low if a == 0 else ~low
                ga = jnp.where(keep, gs, none)
                pb = p_ref[(h * pairs + pp) * 2 + a, :, :]
                g = mm(jnp.concatenate([ga, jnp.where(keep, ts, none)], axis=1), v, 1, 1)
                ds = (pb.astype(F32) * g).astype(BF)
                dq = dq + mm(ds, jnp.where(keep, k, none))
                dk = dk + mm(ds, jnp.where(keep, q, none), 0, 0)
                dv = dv + mm(pb, ga, 0, 0)
            dqkv_ref[h, :, pl.ds(at, 128)] = (dq * scale).astype(BF)
            dqkv_ref[h, :, pl.ds(half + at, 128)] = (dk * scale).astype(BF)
            dqkv_ref[h, :, pl.ds(2 * half + at, 128)] = dv.astype(BF)


from jax.sharding import PartitionSpec as P

MESH = pl.DeviceIdType.MESH
inv_tau = 20.0
unit_eps = 1e-06
ROWS = 256
SEND = 128
V_PARTS = 4
VMEM_BYTES = 62 * 2**20


CROPS_OF_ROW = 6


def unit_rows(vectors):
    return vectors * lax.rsqrt(jnp.sum(vectors * vectors, axis=-1, keepdims=True) + unit_eps)


def member_rows(seg_row, count):
    return (lax.broadcasted_iota(jnp.int32, (count, seg_row.shape[1]), 0) == seg_row).astype(F32)


def split_mm(member, value):
    high = value.astype(BF)
    rest = (value - high.astype(F32)).astype(BF)
    return mm(member, high) + mm(member, rest)


def forward_kernel(
    hid, w1, w2, queue, segments, partners, out_bias, ln_gain, ln_bias,
    o_qkv, o_p, o_mixed, o_inv, o_xhat, o_rstd, o_x, o_w, o_v, o_head,
    W, V, X, Y, qkv, prob, mixed, inv, yf, xhat, rstd, fq, fk, pick, pool, rows_q, queue_low, part, total, parts, blocks,
    l_sem, wl, ws, wr, vbs, vbr, vas, var, vzs, vzr, vfs, vfr, r0s, r0r, r2s, r2r, r3s, hs, hr, acs, acr, o_sem,
    qs, qr, ds, dr, us, ur, bs, br,
):
    s, d, m = lax.axis_index("section"), lax.axis_index("dp"), lax.axis_index("mp")
    last, planes = lax.axis_size("section") - 1, lax.axis_size("dp")
    own_slot, slots = d * 2 + m, 2 * planes
    lane_d = lax.rem(d, 2)
    beside = d + 1 - 2 * lane_d
    other = 1 - m
    seq = X.shape[1]
    chunks = seq // ROWS
    sends = seq // SEND
    n_qkv = qkv.shape[3]
    va_rows = w2.shape[1]
    even = lax.rem(s, 2) == 0
    odd = lax.rem(s, 2) == 1

    barrier = pltpu.get_barrier_semaphore()
    pl.semaphore_signal(barrier, inc=1, device_id={"mp": other}, device_id_type=MESH)

    @pl.when(s > 0)
    def _():
        pl.semaphore_signal(barrier, inc=1, device_id={"section": s - 1}, device_id_type=MESH)

    @pl.when(s < last)
    def _():
        pl.semaphore_signal(barrier, inc=1, device_id={"section": s + 1}, device_id_type=MESH)

    @pl.when(s < last - 1)
    def _():
        pl.semaphore_signal(barrier, inc=1, device_id={"section": last}, device_id_type=MESH)

    @pl.when(s == last)
    def _():
        for t in range(last - 1):
            pl.semaphore_signal(barrier, inc=1, device_id={"section": t}, device_id_type=MESH)

    def greet(i, carry):
        for c in range(2):
            pl.semaphore_signal(
                barrier, inc=1, device_id={"dp": lax.rem(d + 1 + i, planes), "mp": c}, device_id_type=MESH
            )
        return carry

    lax.fori_loop(0, planes - 1, greet, 0)

    @pl.when((s == 0) | (s == 2))
    def _():
        pl.semaphore_signal(barrier, inc=1, device_id={"section": 2 - s}, device_id_type=MESH)

    pl.semaphore_wait(
        barrier,
        1
        + 2 * (planes - 1)
        + jnp.where((s == 0) | (s == 2), 1, 0)
        + jnp.where(s > 0, 1, 0)
        + jnp.where(s < last, 1, 0)
        + jnp.where(s < last - 1, 1, 0)
        + jnp.where(s == last, last - 1, 0),
    )

    def remote(src, dst, send, recv, **to):
        return pltpu.make_async_remote_copy(
            src_ref=src, dst_ref=dst, send_sem=send, recv_sem=recv, device_id=to, device_id_type=MESH
        )

    def to_core(src, dst, ss, rs):
        return pltpu.make_async_remote_copy(
            src_ref=src, dst_ref=dst, send_sem=ss, recv_sem=rs,
            device_id={"mp": other}, device_id_type=MESH,
        )

    def to_next(src, dst, ss, rs):
        return pltpu.make_async_remote_copy(
            src_ref=src, dst_ref=dst, send_sem=ss, recv_sem=rs,
            device_id={"section": s + 1}, device_id_type=MESH,
        )

    def w_place(e, j):
        half = w1.shape[3]
        return W.at[e, m, :, pl.ds(j * half, half)]

    def w_far(e, j):
        return to_core(w1.at[e, j], w_place(e, j), ws.at[e, j], wr.at[e, j])

    def w_near(e, j):
        return pltpu.make_async_copy(w1.at[e, j], w_place(e, j), wl.at[e, j])

    def vb_far(e):
        return to_core(w2.at[e], V.at[e, m, pl.ds(va_rows, va_rows)], vbs.at[e], vbr.at[e])

    def vb_near(e):
        return pltpu.make_async_copy(w2.at[e], V.at[e, m, pl.ds(va_rows, va_rows)], l_sem.at[2 + e])

    seg_row = jnp.where(m == 0, segments[0:1, :], segments[1:2, :])

    def va_part(e, i, side):
        half = va_rows // 2
        start = jnp.where(lane_d == side, 0, half) + i * (half // V_PARTS)
        return pl.ds(pl.multiple_of(start, half // V_PARTS), half // V_PARTS)

    def va_next(e, i):
        rows = va_part(e, i, 0)
        return to_next(w2.at[e, rows], V.at[e, m, rows], vas.at[e, i], var.at[e, i])

    detour = [(1, i) for i in range(V_PARTS)]

    def aside(e, i):
        return Y.at[e, pl.ds(i * (va_rows // 2 // V_PARTS), va_rows // 2 // V_PARTS)]

    def detour_0(e, i):
        rows = va_part(e, i, 0)
        return remote(w2.at[e, rows], V.at[e, m, rows], r0s.at[e, i], r0r.at[e, i], section=2)

    def detour_2(e, i):
        return remote(V.at[e, m, va_part(e, i, 0)], aside(e, i), r2s.at[e, i], r2r.at[e, i], section=3)

    def detour_3(e, i):
        return remote(aside(e, i), V.at[e, m, va_part(e, i, 0)], r3s.at[e, i], var.at[e, i], section=1)

    def straight(e, i):
        return even & ((s > 0) | ((e, i) not in detour))

    def va_beside(e, i):
        rows = va_part(e, i, 0)
        return pltpu.make_async_remote_copy(
            src_ref=V.at[e, m, rows], dst_ref=V.at[e, m, rows], send_sem=vzs.at[e, i], recv_sem=vzr.at[e, i],
            device_id={"dp": beside}, device_id_type=MESH,
        )

    def va_core(e, i, side):
        part = V.at[e, m, va_part(e, i, side)]
        return to_core(part, part, vfs.at[e, side, i], vfr.at[e, side, i])

    def hid_far(e):
        return to_core(hid.at[other], X.at[e, pl.ds(pl.multiple_of(m * ROWS, ROWS), ROWS)], hs.at[e], hr.at[e])

    def hid_near(e):
        return pltpu.make_async_copy(
            hid.at[m], X.at[e, pl.ds(pl.multiple_of(m * ROWS, ROWS), ROWS)], l_sem.at[4 + e]
        )

    def act_next(e, c):
        rows = pl.ds(pl.multiple_of(c * SEND, SEND), SEND)
        return to_next(Y.at[e, rows], X.at[e, rows], acs.at[e, c], acr.at[e, c])

    @pl.when(s == 0)
    def _():
        for e in range(2):
            hid_far(e).start()
            hid_near(e).start()

    for j in range(4):
        w_far(0, j).start()
        w_near(0, j).start()

    @pl.when(odd)
    def _():
        vb_far(0).start()
        vb_near(0).start()

    for i in range(V_PARTS):
        pl.when(straight(0, i))(va_next(0, i).start)

    @pl.when(s == 0)
    def _():
        for piece in detour:
            detour_0(*piece).start()

    def second_weights():
        for j in range(4):
            w_far(1, j).start()
            w_near(1, j).start()

    pl.when(s > 0)(second_weights)

    @pl.when(odd)
    def _():
        vb_far(1).start()
        vb_near(1).start()

    @pl.when(s == 0)
    def _():
        for e in range(2):
            hid_far(e).wait_recv()
            hid_near(e).wait()


    def saves(e):
        pairs = [
            (qkv.at[0], o_qkv), (prob, o_p), (mixed.at[0], o_mixed), (inv, o_inv),
            (xhat, o_xhat), (rstd, o_rstd), (X.at[0], o_x), (W.at[0], o_w), (V.at[0], o_v),
        ]
        return [pltpu.make_async_copy(a, b, o_sem.at[i]) for i, (a, b) in enumerate(pairs)]

    def finish(e, rows, resid):
        y, xh, rs = norm_rows(resid, ln_gain[e], ln_bias[e])
        if e == 0:
            xhat[rows, :] = xh
            rstd[rows, :] = jnp.broadcast_to(rs, (rs.shape[0], 128))
        return y

    def wait_w(e):
        for j in range(4):
            w_near(e, j).wait()
            w_far(e, j).wait_recv()

    def peer(i):
        return lax.rem(own_slot + 1 + i, slots)

    def query_to(i):
        to = peer(i)
        return remote(
            rows_q.at[own_slot], rows_q.at[own_slot], qs.at[i], qr.at[own_slot], dp=to // 2, mp=lax.rem(to, 2)
        )

    def query_from(i):
        slot = peer(i)
        return remote(rows_q.at[slot], rows_q.at[slot], qs.at[i], qr.at[slot], dp=slot // 2, mp=lax.rem(slot, 2))

    def query_down(t):
        return remote(rows_q.at[own_slot], rows_q.at[own_slot], ds.at[t], dr.at[0], section=t)

    def total_up():
        return remote(total, parts.at[s], us.at[0], ur.at[s], section=last)

    def total_in(t):
        return remote(total, parts.at[t], us.at[0], ur.at[t], section=last)

    def block_to(i):
        to = peer(i)
        return remote(part.at[to], blocks.at[own_slot], bs.at[i], br.at[own_slot], dp=to // 2, mp=lax.rem(to, 2))

    def block_from(i):
        slot = peer(i)
        return remote(part.at[slot], blocks.at[slot], bs.at[i], br.at[slot], dp=slot // 2, mp=lax.rem(slot, 2))

    def each(count, what):
        def one(i, carry):
            what(i)
            return carry

        lax.fori_loop(0, count, one, 0)

    def queue_copy():
        return pltpu.make_async_copy(queue, queue_low, l_sem.at[6])

    def low_queue():
        queue_copy().wait()
        raw = queue_low[...].astype(F32)
        queue_low[...] = unit_rows(raw).astype(BF)

    def queue_share():
        width = queue_low.shape[1]
        query = rows_q[...].reshape(-1, width).astype(BF)
        weight = jnp.exp(mm(query, queue_low[...], 1, 1) * inv_tau - inv_tau)
        high = weight.astype(BF)
        rest = (weight - high.astype(F32)).astype(BF)
        pull = mm(high, queue_low[...]) + mm(rest, queue_low[...])
        sums = jnp.sum(weight, axis=-1, keepdims=True)
        part[:, :, :width] = pull.reshape(slots, 8, width)
        part[:, :, width:] = jnp.broadcast_to(sums, (sums.shape[0], 128)).reshape(slots, 8, 128)

    def share():
        @pl.when(s == last)
        def _():
            rows_q[own_slot] = unit_rows(pool[0]).astype(BF).astype(F32)
            for t in range(last):
                query_down(t).start()

        @pl.when(s < last)
        def _():
            query_down(0).wait_recv()

        each(slots - 1, lambda i: query_to(i).start())
        each(slots - 1, lambda i: query_from(i).wait_recv())
        queue_share()
        blocks[own_slot] = part[own_slot]
        each(slots - 1, lambda i: block_to(i).start())

    def share_end():
        each(slots - 1, lambda i: block_from(i).wait_recv())
        total[...] = jnp.sum(blocks[...], axis=0)

    def share_below():
        share()
        share_end()
        total_up().start()

    def head_end():
        share_end()
        for t in range(last):
            total_in(t).wait_recv()
        width = queue_low.shape[1]
        pick[...] = jnp.full(pick.shape, -1, jnp.int32)
        pick[0:1, :CROPS_OF_ROW] = jnp.where(m == 0, partners[0:1, :], partners[1:2, :])
        chosen = (lax.broadcasted_iota(jnp.int32, (8, 8), 0) == pick[0:1, :8]).astype(F32)
        key_low = unit_rows(pool[1]).astype(BF).astype(F32)
        partner_low = mm(chosen, key_low, 0, 0)
        query_low = rows_q[own_slot]
        pos = jnp.sum(query_low * partner_low, axis=-1, keepdims=True) * inv_tau
        sums = total[...] + jnp.sum(parts[...], axis=0)
        pos_weight = jnp.exp(pos - inv_tau)
        denominator = pos_weight + sums[:, width : width + 1]
        log_total = inv_tau + jnp.log(denominator)
        member = member_rows(seg_row, 8)
        counts = jnp.sum(member, axis=-1, keepdims=True)
        crops = slots * CROPS_OF_ROW
        real = lax.broadcasted_iota(jnp.int32, (8, 1), 0) < CROPS_OF_ROW
        loss = jnp.sum(jnp.where(real, log_total - pos, 0.0), axis=0, keepdims=True) * (1.0 / crops)
        grad = (sums[:, :width] / denominator + (pos_weight / denominator - 1.0) * partner_low) * (
            inv_tau / crops
        )
        vectors = pool[0]
        scale = lax.rsqrt(jnp.sum(vectors * vectors, axis=-1, keepdims=True) + unit_eps)
        inner = jnp.sum(vectors * grad, axis=-1, keepdims=True)
        grad = scale * grad - vectors * (scale * scale * scale * inner)
        o_head[:8, :] = grad / jnp.maximum(counts, 1.0)
        o_head[8:, :] = jnp.broadcast_to(loss, (8, width))

    def attention(e):
        wait_w(e)
        if e == 0:
            pl.when(s == 0)(second_weights)

        def project(c, carry):
            @pl.when(s > 0)
            def _():
                for i in range(ROWS // SEND):
                    act_next(e, c * (ROWS // SEND) + i).wait_recv()

            r = pl.multiple_of(c * ROWS, ROWS)
            qkv_rows(X[e, pl.ds(r, ROWS), :], W.at[e], qkv.at[e], r, ROWS)
            return carry

        lax.fori_loop(0, chunks, project, 0)

        def attend(c, carry):
            r = pl.multiple_of(c * ROWS, ROWS)
            rows = pl.ds(r, ROWS)
            attend_rows(
                qkv.at[e], fq, fk, prob if e == 0 else None, inv if e == 0 else None, mixed.at[e], r, ROWS
            )
            branch = attn_out(mixed[e, rows, :], W.at[e], n_qkv)
            y = finish(e, rows, X[e, rows, :].astype(F32) + branch + out_bias[e])
            Y[e, rows, :] = y.astype(BF)
            for i in range(ROWS // SEND):
                act_next(e, c * (ROWS // SEND) + i).start()
            return carry

        lax.fori_loop(0, chunks, attend, 0)

    def pass_on(e, i):
        va_next(e, i).wait_recv()
        va_beside(e, i).start()
        va_core(e, i, 0).start()

    def feed(e):
        if e == 0:
            for i in range(V_PARTS):
                pass_on(0, i)
        for i in range(V_PARTS):
            va_beside(e, i).wait_recv()
            va_core(e, i, 1).start()
        wait_w(e)
        vb_near(e).wait()
        vb_far(e).wait_recv()
        for i in range(V_PARTS):
            va_core(e, i, 0).wait_recv()
            va_core(e, i, 1).wait_recv()

        def one(c, carry):
            if e == 0:
                pass_on(1, c)
            act_next(e, c).wait_recv()
            r = pl.multiple_of(c * SEND, SEND)
            rows = pl.ds(r, SEND)
            x = X[e, rows, :]
            branch = ffn_rows(x, W.at[e], V.at[e], prob if e == 0 else None, r, SEND)
            y = finish(e, rows, x.astype(F32) + branch + out_bias[e])

            @pl.when(s < last)
            def _():
                Y[e, rows, :] = y.astype(BF)
                act_next(e, c).start()

            @pl.when(s == last)
            def _():
                yf[rows, :] = y

            return carry

        lax.fori_loop(0, sends, one, 0)

        @pl.when(s == last)
        def _():
            member = member_rows(seg_row, 8)
            counts = jnp.sum(member, axis=-1, keepdims=True)
            pool[e] = split_mm(member.astype(BF), yf[...]) / jnp.maximum(counts, 1.0)

    queue_copy().start()

    @pl.when(even)
    def _():
        across = jnp.broadcast_to(seg_row.astype(F32), (128, seq))
        fq[...], fk[...] = crop_features(across.T.astype(jnp.int32))

    @pl.when(s > 0)
    def _():
        low_queue()

    @pl.when(s == 2)
    def _():
        for piece in detour:
            detour_0(*piece).wait_recv()
            detour_2(*piece).start()

    for i in range(V_PARTS):
        pl.when(straight(1, i))(va_next(1, i).start)

    @pl.when(s == 3)
    def _():
        for piece in detour:
            detour_2(*piece).wait_recv()
            detour_3(*piece).start()

    for e in range(2):
        @pl.when(even)
        def _():
            attention(e)

        @pl.when(odd)
        def _():
            feed(e)

        if e == 0:
            pl.when(s == last)(share)
            for copy in saves(0):
                copy.start()

    @pl.when(s == 0)
    def _():
        low_queue()

    pl.when(s < last)(share_below)
    pl.when(s == last)(head_end)
    for copy in saves(0):
        copy.wait()
    for piece in detour:
        pl.when(s == 0)(detour_0(*piece).wait_send)
        pl.when(s == 2)(detour_2(*piece).wait_send)
        pl.when(s == 3)(detour_3(*piece).wait_send)

    @pl.when(s < last)
    def _():
        total_up().wait_send()

    @pl.when(s == last)
    def _():
        for t in range(last):
            query_down(t).wait_send()

    each(slots - 1, lambda i: query_to(i).wait_send())
    each(slots - 1, lambda i: block_to(i).wait_send())

    for e in range(2):
        for j in range(4):
            w_far(e, j).wait_send()

        @pl.when(odd)
        def _():
            vb_far(e).wait_send()
            for i in range(V_PARTS):
                va_beside(e, i).wait_send()
                va_core(e, i, 0).wait_send()
                va_core(e, i, 1).wait_send()

        for i in range(V_PARTS):
            pl.when(straight(e, i))(va_next(e, i).wait_send)

        @pl.when(s == 0)
        def _():
            hid_far(e).wait_send()

        @pl.when(s < last)
        def _():
            for c in range(sends):
                act_next(e, c).wait_send()


PIECES = 8
ADOPTED = 3
WAIT_ROOT = 2
LAG = 3


def backward_kernel(
    i_qkv, i_p, i_mixed, i_inv, i_xhat, i_rstd, i_x, i_w, i_v, head, segments, ln_gain,
    o_gin, o_w, o_v, o_sum,
    qkv, prob, mixed, inv, xhat, rstd, X, W, V, G, gout, low, resid, gup, gsplit,
    mine, give, taken, part, leave, received, belong, sums, loss,
    i_sem, gs, gr, is_, ir, xs, xr, ps, pr, fs, fr, as_, ar, vs, vr, ss, sr, ls, lr,
):
    s, d, m = lax.axis_index("section"), lax.axis_index("dp"), lax.axis_index("mp")
    sections, planes = lax.axis_size("section"), lax.axis_size("dp")
    last = sections - 1
    other = 1 - m
    seq, width = X.shape
    chunks = seq // ROWS
    sends = seq // SEND
    n_qkv = qkv.shape[2]
    cols = W.shape[2]
    even = lax.rem(s, 2) == 0
    odd = lax.rem(s, 2) == 1
    tiles = prob.shape[0] // 2
    load = {
        name: pltpu.make_async_copy(a, b, i_sem.at[i])
        for i, (name, a, b) in enumerate(
            [("xhat", i_xhat, xhat), ("rstd", i_rstd, rstd), ("v", i_v, V),
             ("slope", i_p.at[pl.ds(tiles, tiles)], prob.at[pl.ds(tiles, tiles)]), ("w", i_w, W),
             ("act", i_p.at[pl.ds(0, tiles)], prob.at[pl.ds(0, tiles)]), ("x", i_x, X),
             ("qkv", i_qkv, qkv), ("mixed", i_mixed, mixed), ("inv", i_inv, inv)]
        )
    }
    for name in ("xhat", "rstd"):
        load[name].start()
    pl.when(odd)(load["v"].start)
    for name in ("slope", "w", "act", "x"):
        load[name].start()

    @pl.when(even)
    def _():
        for name in ("qkv", "mixed", "inv"):
            load[name].start()

    barrier = pltpu.get_barrier_semaphore()
    for t in range(sections):
        for c in range(2):
            @pl.when((s != t) | (m != c))
            def _():
                pl.semaphore_signal(barrier, inc=1, device_id={"section": t, "mp": c}, device_id_type=MESH)

    def greet(i, carry):
        to = lax.rem(d + 1 + i, planes)
        for c in range(2):
            pl.semaphore_signal(barrier, inc=1, device_id={"dp": to, "mp": c}, device_id_type=MESH)
        return carry

    lax.fori_loop(0, planes - 1, greet, 0)
    pl.semaphore_wait(barrier, 2 * sections - 1 + 2 * (planes - 1))

    def remote(src, dst, send, recv, **to):
        return pltpu.make_async_remote_copy(
            src_ref=src, dst_ref=dst, send_sem=send, recv_sem=recv, device_id=to, device_id_type=MESH
        )

    def grad_prev(c):
        rows = pl.ds(pl.multiple_of(c * SEND, SEND), SEND)
        return remote(gout.at[rows], G.at[rows], gs.at[c], gr.at[c], section=s - 1)

    def spread(t, c):
        return remote(
            gsplit.at[t, pl.ds(c * ROWS, ROWS)], o_gin.at[m], is_.at[t * 2 + c], ir.at[m], section=t, mp=c
        )

    load["xhat"].wait()
    load["rstd"].wait()

    own_slot = d * 2 + m
    sums[own_slot] = jnp.zeros_like(sums[own_slot])

    @pl.when(s == last)
    def _():
        sums[own_slot, 3:4, :] = head[8:9, :]
        belong[...] = member_rows(jnp.where(m == 0, segments[0:1, :], segments[1:2, :]), 8)

    @pl.when(s >= last - 1)
    def _():
        taken[ADOPTED] = jnp.zeros_like(taken[ADOPTED])

    def through_norm(rows, g):
        xh = xhat[rows, :]
        grad = norm_back(g, xh, rstd[rows, :1], ln_gain[0])
        sums[own_slot, 0:1, :] += jnp.sum(grad, axis=0, keepdims=True)
        sums[own_slot, 1:2, :] += jnp.sum(g * xh, axis=0, keepdims=True)
        sums[own_slot, 2:3, :] += jnp.sum(g, axis=0, keepdims=True)
        resid[rows, :] = grad
        low[rows, :] = grad.astype(BF)

    half = cols // 4
    step_rows = width // PIECES

    def exchange(slot):
        to = received if slot == ADOPTED else taken.at[slot]
        return remote(give.at[slot], to, xs.at[slot], xr.at[slot], mp=other)

    def adopt(i):
        rows = pl.ds(pl.multiple_of(i * step_rows, step_rows), step_rows)
        to = jnp.where(s == last, last - 1, last)
        return remote(leave.at[rows], mine.at[ADOPTED, rows], as_.at[i], ar.at[i], section=to)

    def weight_grads(left, right, count):
        for h, out in ((other, give), (m, mine)):
            for j in range(4):
                at = slice(j % 2 * half, j % 2 * half + half)
                if j * half < count:
                    out[1 + j // 2, :, at] = mm(left[...], right[h, :, j * half : (j + 1) * half], 0, 0).astype(BF)
                else:
                    for k in range(2):
                        @pl.when(h == k)
                        def _():
                            out[1 + j // 2, :, at] = mm(
                                low[...], mixed[:, k * half : (k + 1) * half], 0, 0
                            ).astype(BF)
                if out is give and j % 2:
                    exchange(1 + j // 2).start()

    def sum_to(i):
        to = lax.rem(own_slot + 1 + i, 2 * planes)
        return remote(
            sums.at[own_slot], sums.at[own_slot], ss.at[i], sr.at[own_slot], dp=to // 2, mp=lax.rem(to, 2)
        )

    def sum_from(i):
        slot = lax.rem(own_slot + 1 + i, 2 * planes)
        return remote(sums.at[slot], sums.at[slot], ss.at[i], sr.at[slot], dp=slot // 2, mp=lax.rem(slot, 2))

    def start_sums():
        def one(i, carry):
            sum_to(i).start()
            return carry

        lax.fori_loop(0, 2 * planes - 1, one, 0)

    @pl.when(odd)
    def _():
        load["v"].wait()
        load["slope"].wait()
        load["w"].wait()

        def feed_rows(r, count):
            rows = pl.ds(r, count)
            dx = ffn_back_rows(low[rows, :], W, V, prob, gup, r, count)
            gout[rows, :] = (resid[rows, :] + dx).astype(BF)

        @pl.when(s == last)
        def _():
            for r in range(0, seq, ROWS):
                rows = pl.ds(r, ROWS)
                own = belong[:, rows]
                high = head[:8, :].astype(BF).astype(F32)
                through_norm(rows, mm(own, high, 0, 0) + mm(own, head[:8, :] - high, 0, 0))
                feed_rows(r, ROWS)
                for c in range(r // SEND, (r + ROWS) // SEND):
                    grad_prev(c).start()

        @pl.when(s < last)
        def _():
            at = 0
            for count in (ROWS,) + (SEND,) * ((seq - ROWS) // SEND):
                for c in range(at // SEND, (at + count) // SEND):
                    grad_prev(c).wait_recv()
                rows = pl.ds(at, count)
                through_norm(rows, G[rows, :].astype(F32))
                feed_rows(at, count)
                for c in range(at // SEND, (at + count) // SEND):
                    grad_prev(c).start()
                at += count

        load["act"].wait()
        load["x"].wait()
        start_sums()
        unit = 256
        for h, out in ((other, give), (m, mine)):
            for c in range(cols // unit):
                act = prob[h * (cols // 512) + c * unit // 512, :, c * unit % 512 : c * unit % 512 + unit]
                grad = mm(act, low[...], 0, 0).astype(BF)
                r = c * unit % width
                if c * unit < width and out is mine:
                    leave[r : r + unit, :] = grad
                else:
                    out[ADOPTED if c * unit < width else 0, r : r + unit, :] = grad
            if out is give:
                exchange(ADOPTED).start()
                exchange(0).start()
        exchange(ADOPTED).wait_recv()

        def hand_over(i, carry):
            rows = pl.ds(pl.multiple_of(i * step_rows, step_rows), step_rows)
            leave[rows, :] = (leave[rows, :].astype(F32) + received[rows, :].astype(F32)).astype(BF)
            adopt(i).start()
            return carry

        lax.fori_loop(0, PIECES, hand_over, 0)
        weight_grads(X, gup, cols)
        exchange(0).wait_recv()

    @pl.when(even)
    def _():
        for name in ("slope", "act", "w", "x", "qkv", "mixed", "inv"):
            load[name].wait()

        def one(c, carry):
            rows = pl.ds(pl.multiple_of(c * SEND, SEND), SEND)
            grad_prev(c).wait_recv()
            through_norm(rows, G[rows, :].astype(F32))
            return carry

        lax.fori_loop(0, sends, one, 0)
        start_sums()
        attn_back_core(low, W, qkv, prob, inv, mixed, gup, n_qkv)

        def back(c, carry):
            rows = pl.ds(pl.multiple_of(c * ROWS, ROWS), ROWS)
            dx = mm(gup[0, rows, :n_qkv], W[0, :, :n_qkv], 1, 1) + mm(
                gup[1, rows, :n_qkv], W[1, :, :n_qkv], 1, 1
            )
            grad = (resid[rows, :] + dx).astype(BF)

            @pl.when(s > 0)
            def _():
                gout[rows, :] = grad
                for i in range(ROWS // SEND):
                    grad_prev(c * (ROWS // SEND) + i).start()

            @pl.when(s == 0)
            def _():
                part_width = gsplit.shape[2]
                for t in range(sections):
                    gsplit[t, rows, :] = grad[:, t * part_width : (t + 1) * part_width]

            return carry

        lax.fori_loop(0, chunks, back, 0)

        @pl.when(s == 0)
        def _():
            for t in range(sections):
                for c in range(2):
                    if t > 0:
                        spread(t, c).start()
                    else:
                        @pl.when(m != c)
                        def _():
                            spread(t, c).start()

                        @pl.when(m == c)
                        def _():
                            pltpu.make_async_copy(
                                gsplit.at[t, pl.ds(c * ROWS, ROWS)], o_gin.at[m], is_.at[t * 2 + c]
                            ).start()

        weight_grads(X, gup, n_qkv)

    for slot in (1, 2):
        exchange(slot).wait_recv()

    root_a, root_b = (planes - 1) // 2, planes // 2
    first = jnp.where(odd, 0, PIECES)
    total = jnp.where(s >= last - 1, 4 * PIECES, 3 * PIECES)
    lag = WAIT_ROOT + LAG * jnp.maximum(root_b - d, d - root_a)

    def place(i):
        slot = i // PIECES
        rows = pl.ds(pl.multiple_of(lax.rem(i, PIECES) * step_rows, step_rows), step_rows)
        root = jnp.where(lax.rem(i, 2) == 0, root_a, root_b)
        return slot, rows, root

    def part_right(i):
        slot, rows, _ = place(i)
        return remote(mine.at[slot, rows], part.at[0, slot, rows], ps.at[i], pr.at[0, i], dp=d + 1)

    def part_left(i):
        slot, rows, _ = place(i)
        return remote(mine.at[slot, rows], part.at[1, slot, rows], ps.at[i], pr.at[1, i], dp=d - 1)

    def at_home(i, what):
        slot, rows, _ = place(i)
        for k in range(4):
            @pl.when(slot == k)
            def _():
                if k in (1, 2):
                    what(o_w.at[rows, pl.ds((k - 1) * width, width)])
                else:
                    what(o_v.at[k // 3, rows])

    def send_whole(i, side, home_too):
        slot, rows, _ = place(i)

        def go(home):
            source = home if home_too else mine.at[slot, rows]
            remote(source, home, fs.at[side, i], fr.at[i], dp=d + (1 if side else -1)).start()

        at_home(i, go)

    def keep_root(i):
        slot, rows, _ = place(i)
        at_home(i, lambda home: pltpu.make_async_copy(mine.at[slot, rows], home, fr.at[i]).start())

    def whole_here(i):
        slot, rows, _ = place(i)
        pltpu.make_async_copy(mine.at[slot, rows], mine.at[slot, rows], fr.at[i]).wait()

    def whole_sent(i, side):
        slot, rows, _ = place(i)
        remote(mine.at[slot, rows], mine.at[slot, rows], fs.at[side, i], fr.at[i], dp=d).wait_send()

    def bring_home(i):
        rows = pl.ds(pl.multiple_of(i * step_rows, step_rows), step_rows)
        return remote(o_v.at[1, rows], o_v.at[1, rows], vs.at[i], vr.at[i], section=0)

    def add(i, *sides):
        slot, rows, _ = place(i)
        value = mine[slot, rows, :].astype(F32) + taken[slot, rows, :].astype(F32)
        for side in sides:
            value = value + part[side, slot, rows, :].astype(F32)
        mine[slot, rows, :] = value.astype(BF)

    def adopted_here(i):
        @pl.when(i >= ADOPTED * PIECES)
        def _():
            adopt(i - ADOPTED * PIECES).wait_recv()

    def pieces(i, carry):
        root = place(i)[2]

        @pl.when((i < total) & (d < root))
        def _():
            adopted_here(i)

            @pl.when(d > 0)
            def _():
                part_right(i).wait_recv()
                add(i, 0)

            @pl.when(d == 0)
            def _():
                add(i)

            part_right(i).start()

        @pl.when((i < total) & (d > root))
        def _():
            adopted_here(i)

            @pl.when(d < planes - 1)
            def _():
                part_left(i).wait_recv()
                add(i, 1)

            @pl.when(d == planes - 1)
            def _():
                add(i)

            part_left(i).start()

        k = i - WAIT_ROOT

        @pl.when((k >= first) & (k < total) & (d == place(k)[2]))
        def _():
            adopted_here(k)
            part_right(k).wait_recv()
            part_left(k).wait_recv()
            add(k, 0, 1)
            keep_root(k)
            send_whole(k, 0, False)
            send_whole(k, 1, False)

        @pl.when(i >= first + lag)
        def _():
            j = i - lag
            root = place(j)[2]
            whole_here(j)

            @pl.when((d < root) & (d > 0))
            def _():
                send_whole(j, 0, True)

            @pl.when((d > root) & (d < planes - 1))
            def _():
                send_whole(j, 1, True)

            @pl.when((s == last) & (j >= ADOPTED * PIECES))
            def _():
                bring_home(j - ADOPTED * PIECES).start()

        return carry

    lax.fori_loop(first, total + lag, pieces, 0)

    def settle(i, carry):
        root = place(i)[2]

        @pl.when(d != root)
        def _():
            part_right(i).wait_send()

        @pl.when((d <= root) & (d > 0))
        def _():
            whole_sent(i, 0)

        @pl.when((d >= root) & (d < planes - 1))
        def _():
            whole_sent(i, 1)

        return carry

    lax.fori_loop(first, total, settle, 0)

    def brought(i, carry):
        @pl.when(s == 0)
        def _():
            bring_home(i).wait_recv()

        @pl.when(s == last)
        def _():
            bring_home(i).wait_send()

        @pl.when(odd)
        def _():
            adopt(i).wait_send()

        return carry

    lax.fori_loop(0, PIECES, brought, 0)

    @pl.when(odd)
    def _():
        exchange(0).wait_send()
        exchange(ADOPTED).wait_send()

    for slot in (1, 2):
        exchange(slot).wait_send()

    @pl.when(s > 0)
    def _():
        for c in range(sends):
            grad_prev(c).wait_send()

    @pl.when(s == 0)
    def _():
        for t in range(sections):
            for c in range(2):
                if t > 0:
                    spread(t, c).wait_send()
                else:
                    @pl.when(m != c)
                    def _():
                        spread(t, c).wait_send()

                    @pl.when(m == c)
                    def _():
                        pltpu.make_async_copy(
                            gsplit.at[t, pl.ds(c * ROWS, ROWS)], o_gin.at[m], is_.at[t * 2 + c]
                        ).wait()

    def arrival(r):
        return remote(gsplit.at[0, pl.ds(0, ROWS)], o_gin.at[r], is_.at[0], ir.at[r], section=0, mp=r)

    for r in range(2):
        @pl.when((s != 0) | (m != r))
        def _():
            arrival(r).wait_recv()

    def sums_in(i, carry):
        sum_from(i).wait_recv()
        sum_to(i).wait_send()
        return carry

    def loss_down(t):
        return remote(loss, loss, ls.at[t], lr.at[0], section=t)

    lax.fori_loop(0, 2 * planes - 1, sums_in, 0)
    total_sums = jnp.sum(sums[...], axis=0)

    @pl.when(s == last)
    def _():
        loss[...] = total_sums
        for t in range(last):
            loss_down(t).start()
        for t in range(last):
            loss_down(t).wait_send()

    @pl.when(s < last)
    def _():
        loss_down(0).wait_recv()

    o_sum[...] = total_sums
    o_sum[3:4, :] = loss[3:4, :]


def local(
    hidden_in, segments, partners, queue, first_weight, second_weight, out_bias, ln_gain, ln_bias
):
    width = hidden_in.shape[-1]
    seq = segments.shape[1]
    w1 = jnp.transpose(first_weight[:, 0], (0, 2, 1, 3))
    w2 = second_weight.reshape(2, -1, width)
    half = w1.shape[3]
    cols, n_qkv, heads = 4 * half, 3 * half, 2 * half // HD
    anyspace = pl.BlockSpec(memory_space=pl.ANY)
    vmem = pl.BlockSpec(memory_space=pltpu.VMEM)
    shape = jax.ShapeDtypeStruct
    dma = pltpu.SemaphoreType.DMA
    saved = [
        shape((2, seq, n_qkv), BF), shape((heads, seq, seq), BF), shape((seq, width), BF),
        shape((heads // 2, seq, 128), F32), shape((seq, width), F32), shape((seq, 128), F32), shape((seq, width), BF), shape((2, width, cols), BF),
        shape((2, cols, width), BF),
    ]
    sections, planes = lax.axis_size("section"), lax.axis_size("dp")
    *kept, head = pl.pallas_call(
        forward_kernel,
        out_shape=saved + [shape((16, width), F32)],
        in_specs=[anyspace] * 4 + [vmem] * 5,
        out_specs=[anyspace] * 9 + [vmem],
        scratch_shapes=[
            pltpu.VMEM((2, 2, width, cols), BF), pltpu.VMEM((2, 2, cols, width), BF),
            pltpu.VMEM((2, seq, width), BF), pltpu.VMEM((2, seq, width), BF),
            pltpu.VMEM((2, 2, seq, n_qkv), BF), pltpu.VMEM((heads, seq, seq), BF),
            pltpu.VMEM((2, seq, width), BF), pltpu.VMEM((heads // 2, seq, 128), F32), pltpu.VMEM((seq, width), F32),
            pltpu.VMEM((seq, width), F32), pltpu.VMEM((seq, 128), F32),
            pltpu.VMEM((seq, 128), BF), pltpu.VMEM((seq, 128), BF), pltpu.VMEM((8, 128), jnp.int32),
            pltpu.VMEM((2, 8, width), F32), pltpu.VMEM((2 * planes, 8, width), F32),
            pltpu.VMEM(queue.shape, BF), pltpu.VMEM((2 * planes, 8, width + 128), F32),
            pltpu.VMEM((8, width + 128), F32), pltpu.VMEM((sections - 1, 8, width + 128), F32),
            pltpu.VMEM((2 * planes, 8, width + 128), F32),
            dma((7,)), dma((2, 4)), dma((2, 4)), dma((2, 4)), dma((2,)), dma((2,)), dma((2, V_PARTS)), dma((2, V_PARTS)),
            dma((2, V_PARTS)), dma((2, V_PARTS)), dma((2, 2, V_PARTS)), dma((2, 2, V_PARTS)),
            *[dma((2, V_PARTS))] * 5,
            dma((2,)), dma((2,)), dma((2, seq // SEND)), dma((2, seq // SEND)), dma((9,)),
            dma((2 * planes,)), dma((2 * planes,)), dma((sections - 1,)), dma((1,)), dma((1,)),
            dma((sections - 1,)), dma((2 * planes,)), dma((2 * planes,)),
        ],
        compiler_params=pltpu.CompilerParams(
            collective_id=0, has_side_effects=True, vmem_limit_bytes=VMEM_BYTES
        ),
        name="forward",
    )(hidden_in, w1, w2, queue, segments, partners, out_bias, ln_gain, ln_bias)
    half_width = width // lax.axis_size("section")
    gin, gw, gv, sums = pl.pallas_call(
        backward_kernel,
        out_shape=[
            shape((2, seq // 2, half_width), BF), shape((width, cols), BF), shape((2, width, width), BF),
            shape((8, width), F32),
        ],
        in_specs=[anyspace] * 9 + [vmem] * 3,
        out_specs=[vmem, anyspace, anyspace, vmem],
        scratch_shapes=[pltpu.VMEM(a.shape, a.dtype) for a in saved]
        + [
            pltpu.VMEM((seq, width), BF), pltpu.VMEM((seq, width), BF), pltpu.VMEM((seq, width), BF),
            pltpu.VMEM((seq, width), F32), pltpu.VMEM((2, seq, cols), BF),
            pltpu.VMEM((sections, seq, half_width), BF),
            pltpu.VMEM((4, width, width), BF), pltpu.VMEM((4, width, width), BF),
            pltpu.VMEM((4, width, width), BF), pltpu.VMEM((2, 4, width, width), BF),
            pltpu.VMEM((width, width), BF), pltpu.VMEM((width, width), BF), pltpu.VMEM((8, seq), F32),
            pltpu.VMEM((2 * planes, 8, width), F32), pltpu.VMEM((8, width), F32),
            dma((10,)), dma((seq // SEND,)), dma((seq // SEND,)), dma((2 * sections,)), dma((2,)),
            dma((4,)), dma((4,)), dma((4 * PIECES,)), dma((2, 4 * PIECES)), dma((2, 4 * PIECES)),
            dma((4 * PIECES,)), dma((PIECES,)), dma((PIECES,)), dma((PIECES,)), dma((PIECES,)), dma((2 * planes,)), dma((2 * planes,)),
            dma((sections - 1,)), dma((1,)),
        ],
        compiler_params=pltpu.CompilerParams(
            collective_id=1, has_side_effects=True, vmem_limit_bytes=VMEM_BYTES
        ),
        name="backward",
    )(*kept, head, segments, ln_gain)
    grad_first = gw.astype(F32).reshape(width, 4, -1)
    odd = lax.axis_index("section") % 2 == 1
    grad_second = jnp.where(odd, gv[0], gv[1]).astype(F32).reshape(second_weight.shape[2:])
    return (
        sums[3, 0], gin, grad_first[None], grad_second[None], sums[0:1], sums[1:2], sums[2:3],
    )


def solution(mesh):
    in_specs = (
        P("dp", "mp", None), P("dp", None), P("dp", None), P(("section", "dp", "mp"), None),
        P(None, "section", None, None, "mp"), P(None, "section", None, "mp", None),
        P(None, "section", None), P(None, "section", None), P(None, "section", None),
    )
    out_specs = (
        P(), P("dp", "mp", "section"), P("section", None, None, "mp"), P("section", None, "mp", None),
        P("section", None), P("section", None), P("section", None),
    )
    return jax.shard_map(local, mesh=mesh, in_specs=in_specs, out_specs=out_specs, check_vma=False)
```

```python
import functools
import jax
import jax.numpy as jnp
from jax import lax
from jax.experimental import pallas as pl
from jax.experimental.pallas import tpu as pltpu

F32 = jnp.float32
BF = jnp.bfloat16
HD = 64
NEG = -1e30
LN_EPS = 1e-12


def mm(a, b, ca=1, cb=0):
    return lax.dot_general(a, b, (((ca,), (cb,)), ((), ())), preferred_element_type=F32)


def norm_rows(resid, gain, shift):
    centre = resid - jnp.mean(resid, axis=-1, keepdims=True)
    spread = jnp.mean(centre * centre, axis=-1, keepdims=True)
    rstd = lax.rsqrt(spread + LN_EPS)
    xhat = centre * rstd
    return xhat * gain + shift, xhat, rstd


def norm_back(g, xhat, rstd, gain):
    gg = g * gain
    m1 = jnp.mean(gg, axis=-1, keepdims=True)
    m2 = jnp.mean(gg * xhat, axis=-1, keepdims=True)
    return rstd * (gg - m1 - xhat * m2)


def lane_low(shape):
    return lax.broadcasted_iota(jnp.int32, shape, len(shape) - 1) < HD


def qkv_rows(x, w_ref, qkv_ref, row0, rows):
    for h in range(2):
        n = qkv_ref.shape[2]
        qkv_ref[h, pl.ds(row0, rows), :] = mm(x, w_ref[h, :, :n]).astype(BF)


def crop_features(seg_col):
    lane = lax.broadcasted_iota(jnp.int32, seg_col.shape, 1)
    hit = lane == seg_col
    as_query = jnp.where(hit, NEG, 0.0).astype(BF)
    as_key = jnp.where(hit | (lane >= 8), 0.0, 1.0).astype(BF)
    return as_query, as_key


def attend_rows(qkv_ref, fq_ref, fk_ref, p_ref, inv_ref, mixed_ref, row0, rows):
    half = qkv_ref.shape[2] // 3
    pairs = half // 128
    low = lane_low((rows, 128))
    fq = fq_ref[pl.ds(row0, rows), :]
    fk = fk_ref[...]
    ones = jnp.ones((fk.shape[0], 128), BF)
    for h in range(2):
        for pp in range(pairs):
            q = qkv_ref[h, pl.ds(row0, rows), pl.ds(pp * 128, 128)] * jnp.asarray(HD ** -0.5, BF)
            k = jnp.concatenate([qkv_ref[h, :, pl.ds(half + pp * 128, 128)], fk], axis=1)
            v = jnp.concatenate([qkv_ref[h, :, pl.ds(2 * half + pp * 128, 128)], ones], axis=1)
            outs, invs = [], []
            for a in range(2):
                qa = jnp.where(low if a == 0 else ~low, q, jnp.zeros_like(q))
                s = mm(jnp.concatenate([qa, fq], axis=1), k, 1, 1)
                p = jnp.exp(s - jnp.max(s, axis=-1, keepdims=True)).astype(BF)
                if p_ref is not None:
                    p_ref[(h * pairs + pp) * 2 + a, pl.ds(row0, rows), :] = p
                o = mm(p, v)
                inv = 1.0 / o[:, 128:]
                outs.append(o[:, :128] * inv)
                invs.append(inv)
            if inv_ref is not None:
                inv_ref[h * pairs + pp, pl.ds(row0, rows), :] = jnp.where(low, invs[0], invs[1])
            mixed_ref[pl.ds(row0, rows), pl.ds(h * half + pp * 128, 128)] = jnp.where(
                low, outs[0], outs[1]
            ).astype(BF)


def attn_out(mixed, w_ref, n_qkv):
    half = mixed.shape[1] // 2
    return mm(mixed[:, :half], w_ref[0, :, n_qkv:], 1, 1) + mm(
        mixed[:, half:], w_ref[1, :, n_qkv:], 1, 1
    )


def gelu_parts(up, want_slope):
    cdf = 0.5 * (1.0 + lax.erf(up * (0.5 ** 0.5)))
    act = up * cdf
    if not want_slope:
        return act, None
    slope = cdf + up * (jnp.exp(-0.5 * up * up) * 0.3989422804014327)
    return act, slope


def ffn_rows(x, w_ref, v_ref, keep_ref, row0, rows, tile=512):
    acc = None
    for h in range(2):
        n = w_ref.shape[2]
        for c in range(0, n, tile):
            up = mm(x, w_ref[h, :, c : c + tile])
            act, slope = gelu_parts(up, keep_ref is not None)
            act = act.astype(BF)
            if keep_ref is not None:
                at = (h * n + c) // tile
                keep_ref[at, pl.ds(row0, rows), :] = act
                keep_ref[keep_ref.shape[0] // 2 + at, pl.ds(row0, rows), :] = slope.astype(BF)
            part = mm(act, v_ref[h, c : c + tile, :])
            acc = part if acc is None else acc + part
    return acc


def ffn_back_rows(low, w_ref, v_ref, keep_ref, gup_ref, row0, rows, ready=None, tile=512):
    acc = None
    for h in range(2):
        n = w_ref.shape[2]
        for c in range(0, n, tile):
            if ready is not None:
                ready((h * n + c) // tile)
            dact = mm(low, v_ref[h, c : c + tile, :], 1, 1)
            at = keep_ref.shape[0] // 2 + (h * n + c) // tile
            gup = (dact * keep_ref[at, pl.ds(row0, rows), :].astype(F32)).astype(BF)
            gup_ref[h, pl.ds(row0, rows), c : c + tile] = gup
            part = mm(gup, w_ref[h, :, c : c + tile], 1, 1)
            acc = part if acc is None else acc + part
    return acc


def attn_back_core(low_ref, w_ref, qkv_ref, p_ref, inv_ref, mixed_ref, dqkv_ref, n_qkv):
    half = n_qkv // 3
    pairs = half // 128
    seq = low_ref.shape[0]
    low = lane_low((seq, 128))
    ones = jnp.ones((seq, 128), BF)
    scale = HD ** -0.5
    for h in range(2):
        for pp in range(pairs):
            at = pp * 128
            gm = mm(low_ref[...], w_ref[h, :, n_qkv + at : n_qkv + at + 128]).astype(BF)
            gs = gm.astype(F32) * inv_ref[h * pairs + pp]
            ts = -(gs * mixed_ref[:, h * half + at : h * half + at + 128].astype(F32))
            gs, ts = gs.astype(BF), ts.astype(BF)
            q = qkv_ref[h, :, pl.ds(at, 128)]
            k = qkv_ref[h, :, pl.ds(half + at, 128)]
            v = jnp.concatenate([qkv_ref[h, :, pl.ds(2 * half + at, 128)], ones], axis=1)
            none = jnp.zeros_like(q)
            dq = dk = dv = 0.0
            for a in range(2):
                keep = low if a == 0 else ~low
                ga = jnp.where(keep, gs, none)
                pb = p_ref[(h * pairs + pp) * 2 + a, :, :]
                g = mm(jnp.concatenate([ga, jnp.where(keep, ts, none)], axis=1), v, 1, 1)
                ds = (pb.astype(F32) * g).astype(BF)
                dq = dq + mm(ds, jnp.where(keep, k, none))
                dk = dk + mm(ds, jnp.where(keep, q, none), 0, 0)
                dv = dv + mm(pb, ga, 0, 0)
            dqkv_ref[h, :, pl.ds(at, 128)] = (dq * scale).astype(BF)
            dqkv_ref[h, :, pl.ds(half + at, 128)] = (dk * scale).astype(BF)
            dqkv_ref[h, :, pl.ds(2 * half + at, 128)] = dv.astype(BF)


from jax.sharding import PartitionSpec as P

MESH = pl.DeviceIdType.MESH
inv_tau = 20.0
unit_eps = 1e-06
ROWS = 256
SEND = 128
V_PARTS = 4
VMEM_BYTES = 62 * 2**20


CROPS_OF_ROW = 6


def unit_rows(vectors):
    return vectors * lax.rsqrt(jnp.sum(vectors * vectors, axis=-1, keepdims=True) + unit_eps)


def member_rows(seg_row, count):
    return (lax.broadcasted_iota(jnp.int32, (count, seg_row.shape[1]), 0) == seg_row).astype(F32)


def split_mm(member, value):
    high = value.astype(BF)
    rest = (value - high.astype(F32)).astype(BF)
    return mm(member, high) + mm(member, rest)


def forward_kernel(
    hid, w1, w2, queue, segments, partners, out_bias, ln_gain, ln_bias,
    o_qkv, o_p, o_mixed, o_inv, o_xhat, o_rstd, o_x, o_w, o_v, o_head,
    W, V, X, Y, qkv, prob, mixed, inv, yf, xhat, rstd, fq, fk, pick, pool, rows_q, queue_low, part, total, parts, blocks,
    l_sem, wl, ws, wr, vbs, vbr, vas, var, vzs, vzr, vfs, vfr, r0s, r0r, r2s, r2r, r3s, hs, hr, acs, acr, o_sem,
    qs, qr, ds, dr, us, ur, bs, br,
):
    s, d, m = lax.axis_index("section"), lax.axis_index("dp"), lax.axis_index("mp")
    last, planes = lax.axis_size("section") - 1, lax.axis_size("dp")
    own_slot, slots = d * 2 + m, 2 * planes
    lane_d = lax.rem(d, 2)
    beside = d + 1 - 2 * lane_d
    other = 1 - m
    seq = X.shape[1]
    chunks = seq // ROWS
    sends = seq // SEND
    n_qkv = qkv.shape[3]
    va_rows = w2.shape[1]
    even = lax.rem(s, 2) == 0
    odd = lax.rem(s, 2) == 1

    barrier = pltpu.get_barrier_semaphore()
    pl.semaphore_signal(barrier, inc=1, device_id={"mp": other}, device_id_type=MESH)

    @pl.when(s > 0)
    def _():
        pl.semaphore_signal(barrier, inc=1, device_id={"section": s - 1}, device_id_type=MESH)

    @pl.when(s < last)
    def _():
        pl.semaphore_signal(barrier, inc=1, device_id={"section": s + 1}, device_id_type=MESH)

    @pl.when(s < last - 1)
    def _():
        pl.semaphore_signal(barrier, inc=1, device_id={"section": last}, device_id_type=MESH)

    @pl.when(s == last)
    def _():
        for t in range(last - 1):
            pl.semaphore_signal(barrier, inc=1, device_id={"section": t}, device_id_type=MESH)

    def greet(i, carry):
        for c in range(2):
            pl.semaphore_signal(
                barrier, inc=1, device_id={"dp": lax.rem(d + 1 + i, planes), "mp": c}, device_id_type=MESH
            )
        return carry

    lax.fori_loop(0, planes - 1, greet, 0)

    @pl.when((s == 0) | (s == 2))
    def _():
        pl.semaphore_signal(barrier, inc=1, device_id={"section": 2 - s}, device_id_type=MESH)

    pl.semaphore_wait(
        barrier,
        1
        + 2 * (planes - 1)
        + jnp.where((s == 0) | (s == 2), 1, 0)
        + jnp.where(s > 0, 1, 0)
        + jnp.where(s < last, 1, 0)
        + jnp.where(s < last - 1, 1, 0)
        + jnp.where(s == last, last - 1, 0),
    )

    def remote(src, dst, send, recv, **to):
        return pltpu.make_async_remote_copy(
            src_ref=src, dst_ref=dst, send_sem=send, recv_sem=recv, device_id=to, device_id_type=MESH
        )

    def to_core(src, dst, ss, rs):
        return pltpu.make_async_remote_copy(
            src_ref=src, dst_ref=dst, send_sem=ss, recv_sem=rs,
            device_id={"mp": other}, device_id_type=MESH,
        )

    def to_next(src, dst, ss, rs):
        return pltpu.make_async_remote_copy(
            src_ref=src, dst_ref=dst, send_sem=ss, recv_sem=rs,
            device_id={"section": s + 1}, device_id_type=MESH,
        )

    def w_place(e, j):
        half = w1.shape[3]
        return W.at[e, m, :, pl.ds(j * half, half)]

    def w_far(e, j):
        return to_core(w1.at[e, j], w_place(e, j), ws.at[e, j], wr.at[e, j])

    def w_near(e, j):
        return pltpu.make_async_copy(w1.at[e, j], w_place(e, j), wl.at[e, j])

    def vb_far(e):
        return to_core(w2.at[e], V.at[e, m, pl.ds(va_rows, va_rows)], vbs.at[e], vbr.at[e])

    def vb_near(e):
        return pltpu.make_async_copy(w2.at[e], V.at[e, m, pl.ds(va_rows, va_rows)], l_sem.at[2 + e])

    seg_row = jnp.where(m == 0, segments[0:1, :], segments[1:2, :])

    def va_part(e, i, side):
        half = va_rows // 2
        start = jnp.where(lane_d == side, 0, half) + i * (half // V_PARTS)
        return pl.ds(pl.multiple_of(start, half // V_PARTS), half // V_PARTS)

    def va_next(e, i):
        rows = va_part(e, i, 0)
        return to_next(w2.at[e, rows], V.at[e, m, rows], vas.at[e, i], var.at[e, i])

    detour = [(1, i) for i in range(V_PARTS)]

    def aside(e, i):
        return Y.at[e, pl.ds(i * (va_rows // 2 // V_PARTS), va_rows // 2 // V_PARTS)]

    def detour_0(e, i):
        rows = va_part(e, i, 0)
        return remote(w2.at[e, rows], V.at[e, m, rows], r0s.at[e, i], r0r.at[e, i], section=2)

    def detour_2(e, i):
        return remote(V.at[e, m, va_part(e, i, 0)], aside(e, i), r2s.at[e, i], r2r.at[e, i], section=3)

    def detour_3(e, i):
        return remote(aside(e, i), V.at[e, m, va_part(e, i, 0)], r3s.at[e, i], var.at[e, i], section=1)

    def straight(e, i):
        return even & ((s > 0) | ((e, i) not in detour))

    def va_beside(e, i):
        rows = va_part(e, i, 0)
        return pltpu.make_async_remote_copy(
            src_ref=V.at[e, m, rows], dst_ref=V.at[e, m, rows], send_sem=vzs.at[e, i], recv_sem=vzr.at[e, i],
            device_id={"dp": beside}, device_id_type=MESH,
        )

    def va_core(e, i, side):
        part = V.at[e, m, va_part(e, i, side)]
        return to_core(part, part, vfs.at[e, side, i], vfr.at[e, side, i])

    def hid_far(e):
        return to_core(hid.at[other], X.at[e, pl.ds(pl.multiple_of(m * ROWS, ROWS), ROWS)], hs.at[e], hr.at[e])

    def hid_near(e):
        return pltpu.make_async_copy(
            hid.at[m], X.at[e, pl.ds(pl.multiple_of(m * ROWS, ROWS), ROWS)], l_sem.at[4 + e]
        )

    def act_next(e, c):
        rows = pl.ds(pl.multiple_of(c * SEND, SEND), SEND)
        return to_next(Y.at[e, rows], X.at[e, rows], acs.at[e, c], acr.at[e, c])

    @pl.when(s == 0)
    def _():
        for e in range(2):
            hid_far(e).start()
            hid_near(e).start()

    for j in range(4):
        w_far(0, j).start()
        w_near(0, j).start()

    @pl.when(odd)
    def _():
        vb_far(0).start()
        vb_near(0).start()

    for i in range(V_PARTS):
        pl.when(straight(0, i))(va_next(0, i).start)

    @pl.when(s == 0)
    def _():
        for piece in detour:
            detour_0(*piece).start()

    def second_weights():
        for j in range(4):
            w_far(1, j).start()
            w_near(1, j).start()

    pl.when(s > 0)(second_weights)

    @pl.when(odd)
    def _():
        vb_far(1).start()
        vb_near(1).start()

    @pl.when(s == 0)
    def _():
        for e in range(2):
            hid_far(e).wait_recv()
            hid_near(e).wait()


    def saves(e):
        pairs = [
            (qkv.at[0], o_qkv), (prob, o_p), (mixed.at[0], o_mixed), (inv, o_inv),
            (xhat, o_xhat), (rstd, o_rstd), (X.at[0], o_x), (W.at[0], o_w), (V.at[0], o_v),
        ]
        return [pltpu.make_async_copy(a, b, o_sem.at[i]) for i, (a, b) in enumerate(pairs)]

    def finish(e, rows, resid):
        y, xh, rs = norm_rows(resid, ln_gain[e], ln_bias[e])
        if e == 0:
            xhat[rows, :] = xh
            rstd[rows, :] = jnp.broadcast_to(rs, (rs.shape[0], 128))
        return y

    def wait_w(e):
        for j in range(4):
            w_near(e, j).wait()
            w_far(e, j).wait_recv()

    def peer(i):
        return lax.rem(own_slot + 1 + i, slots)

    def query_to(i):
        to = peer(i)
        return remote(
            rows_q.at[own_slot], rows_q.at[own_slot], qs.at[i], qr.at[own_slot], dp=to // 2, mp=lax.rem(to, 2)
        )

    def query_from(i):
        slot = peer(i)
        return remote(rows_q.at[slot], rows_q.at[slot], qs.at[i], qr.at[slot], dp=slot // 2, mp=lax.rem(slot, 2))

    def query_down(t):
        return remote(rows_q.at[own_slot], rows_q.at[own_slot], ds.at[t], dr.at[0], section=t)

    def total_up():
        return remote(total, parts.at[s], us.at[0], ur.at[s], section=last)

    def total_in(t):
        return remote(total, parts.at[t], us.at[0], ur.at[t], section=last)

    def block_to(i):
        to = peer(i)
        return remote(part.at[to], blocks.at[own_slot], bs.at[i], br.at[own_slot], dp=to // 2, mp=lax.rem(to, 2))

    def block_from(i):
        slot = peer(i)
        return remote(part.at[slot], blocks.at[slot], bs.at[i], br.at[slot], dp=slot // 2, mp=lax.rem(slot, 2))

    def each(count, what):
        def one(i, carry):
            what(i)
            return carry

        lax.fori_loop(0, count, one, 0)

    def queue_copy():
        return pltpu.make_async_copy(queue, queue_low, l_sem.at[6])

    def low_queue():
        queue_copy().wait()
        raw = queue_low[...].astype(F32)
        queue_low[...] = unit_rows(raw).astype(BF)

    def queue_share():
        width = queue_low.shape[1]
        query = rows_q[...].reshape(-1, width).astype(BF)
        weight = jnp.exp(mm(query, queue_low[...], 1, 1) * inv_tau - inv_tau)
        high = weight.astype(BF)
        rest = (weight - high.astype(F32)).astype(BF)
        pull = mm(high, queue_low[...]) + mm(rest, queue_low[...])
        sums = jnp.sum(weight, axis=-1, keepdims=True)
        part[:, :, :width] = pull.reshape(slots, 8, width)
        part[:, :, width:] = jnp.broadcast_to(sums, (sums.shape[0], 128)).reshape(slots, 8, 128)

    def share():
        @pl.when(s == last)
        def _():
            rows_q[own_slot] = unit_rows(pool[0]).astype(BF).astype(F32)
            for t in range(last):
                query_down(t).start()

        @pl.when(s < last)
        def _():
            query_down(0).wait_recv()

        each(slots - 1, lambda i: query_to(i).start())
        each(slots - 1, lambda i: query_from(i).wait_recv())
        queue_share()
        blocks[own_slot] = part[own_slot]
        each(slots - 1, lambda i: block_to(i).start())

    def share_end():
        each(slots - 1, lambda i: block_from(i).wait_recv())
        total[...] = jnp.sum(blocks[...], axis=0)

    def share_below():
        share()
        share_end()
        total_up().start()

    def head_end():
        share_end()
        for t in range(last):
            total_in(t).wait_recv()
        width = queue_low.shape[1]
        pick[...] = jnp.full(pick.shape, -1, jnp.int32)
        pick[0:1, :CROPS_OF_ROW] = jnp.where(m == 0, partners[0:1, :], partners[1:2, :])
        chosen = (lax.broadcasted_iota(jnp.int32, (8, 8), 0) == pick[0:1, :8]).astype(F32)
        key_low = unit_rows(pool[1]).astype(BF).astype(F32)
        partner_low = mm(chosen, key_low, 0, 0)
        query_low = rows_q[own_slot]
        pos = jnp.sum(query_low * partner_low, axis=-1, keepdims=True) * inv_tau
        sums = total[...] + jnp.sum(parts[...], axis=0)
        pos_weight = jnp.exp(pos - inv_tau)
        denominator = pos_weight + sums[:, width : width + 1]
        log_total = inv_tau + jnp.log(denominator)
        member = member_rows(seg_row, 8)
        counts = jnp.sum(member, axis=-1, keepdims=True)
        crops = slots * CROPS_OF_ROW
        real = lax.broadcasted_iota(jnp.int32, (8, 1), 0) < CROPS_OF_ROW
        loss = jnp.sum(jnp.where(real, log_total - pos, 0.0), axis=0, keepdims=True) * (1.0 / crops)
        grad = (sums[:, :width] / denominator + (pos_weight / denominator - 1.0) * partner_low) * (
            inv_tau / crops
        )
        vectors = pool[0]
        scale = lax.rsqrt(jnp.sum(vectors * vectors, axis=-1, keepdims=True) + unit_eps)
        inner = jnp.sum(vectors * grad, axis=-1, keepdims=True)
        grad = scale * grad - vectors * (scale * scale * scale * inner)
        o_head[:8, :] = grad / jnp.maximum(counts, 1.0)
        o_head[8:, :] = jnp.broadcast_to(loss, (8, width))

    def attention(e):
        wait_w(e)
        if e == 0:
            pl.when(s == 0)(second_weights)

        def project(c, carry):
            @pl.when(s > 0)
            def _():
                for i in range(ROWS // SEND):
                    act_next(e, c * (ROWS // SEND) + i).wait_recv()

            r = pl.multiple_of(c * ROWS, ROWS)
            qkv_rows(X[e, pl.ds(r, ROWS), :], W.at[e], qkv.at[e], r, ROWS)
            return carry

        lax.fori_loop(0, chunks, project, 0)

        def attend(c, carry):
            r = pl.multiple_of(c * ROWS, ROWS)
            rows = pl.ds(r, ROWS)
            attend_rows(
                qkv.at[e], fq, fk, prob if e == 0 else None, inv if e == 0 else None, mixed.at[e], r, ROWS
            )
            branch = attn_out(mixed[e, rows, :], W.at[e], n_qkv)
            y = finish(e, rows, X[e, rows, :].astype(F32) + branch + out_bias[e])
            Y[e, rows, :] = y.astype(BF)
            for i in range(ROWS // SEND):
                act_next(e, c * (ROWS // SEND) + i).start()
            return carry

        lax.fori_loop(0, chunks, attend, 0)

    def pass_on(e, i):
        va_next(e, i).wait_recv()
        va_beside(e, i).start()
        va_core(e, i, 0).start()

    def feed(e):
        if e == 0:
            for i in range(V_PARTS):
                pass_on(0, i)
        for i in range(V_PARTS):
            va_beside(e, i).wait_recv()
            va_core(e, i, 1).start()
        wait_w(e)
        vb_near(e).wait()
        vb_far(e).wait_recv()
        for i in range(V_PARTS):
            va_core(e, i, 0).wait_recv()
            va_core(e, i, 1).wait_recv()

        def one(c, carry):
            if e == 0:
                pass_on(1, c)
            act_next(e, c).wait_recv()
            r = pl.multiple_of(c * SEND, SEND)
            rows = pl.ds(r, SEND)
            x = X[e, rows, :]
            branch = ffn_rows(x, W.at[e], V.at[e], prob if e == 0 else None, r, SEND)
            y = finish(e, rows, x.astype(F32) + branch + out_bias[e])

            @pl.when(s < last)
            def _():
                Y[e, rows, :] = y.astype(BF)
                act_next(e, c).start()

            @pl.when(s == last)
            def _():
                yf[rows, :] = y

            return carry

        lax.fori_loop(0, sends, one, 0)

        @pl.when(s == last)
        def _():
            member = member_rows(seg_row, 8)
            counts = jnp.sum(member, axis=-1, keepdims=True)
            pool[e] = split_mm(member.astype(BF), yf[...]) / jnp.maximum(counts, 1.0)

    queue_copy().start()

    @pl.when(even)
    def _():
        across = jnp.broadcast_to(seg_row.astype(F32), (128, seq))
        fq[...], fk[...] = crop_features(across.T.astype(jnp.int32))

    @pl.when(s > 0)
    def _():
        low_queue()

    @pl.when(s == 2)
    def _():
        for piece in detour:
            detour_0(*piece).wait_recv()
            detour_2(*piece).start()

    for i in range(V_PARTS):
        pl.when(straight(1, i))(va_next(1, i).start)

    @pl.when(s == 3)
    def _():
        for piece in detour:
            detour_2(*piece).wait_recv()
            detour_3(*piece).start()

    for e in range(2):
        @pl.when(even)
        def _():
            attention(e)

        @pl.when(odd)
        def _():
            feed(e)

        if e == 0:
            pl.when(s == last)(share)
            for copy in saves(0):
                copy.start()

    @pl.when(s == 0)
    def _():
        low_queue()

    pl.when(s < last)(share_below)
    pl.when(s == last)(head_end)
    for copy in saves(0):
        copy.wait()
    for piece in detour:
        pl.when(s == 0)(detour_0(*piece).wait_send)
        pl.when(s == 2)(detour_2(*piece).wait_send)
        pl.when(s == 3)(detour_3(*piece).wait_send)

    @pl.when(s < last)
    def _():
        total_up().wait_send()

    @pl.when(s == last)
    def _():
        for t in range(last):
            query_down(t).wait_send()

    each(slots - 1, lambda i: query_to(i).wait_send())
    each(slots - 1, lambda i: block_to(i).wait_send())

    for e in range(2):
        for j in range(4):
            w_far(e, j).wait_send()

        @pl.when(odd)
        def _():
            vb_far(e).wait_send()
            for i in range(V_PARTS):
                va_beside(e, i).wait_send()
                va_core(e, i, 0).wait_send()
                va_core(e, i, 1).wait_send()

        for i in range(V_PARTS):
            pl.when(straight(e, i))(va_next(e, i).wait_send)

        @pl.when(s == 0)
        def _():
            hid_far(e).wait_send()

        @pl.when(s < last)
        def _():
            for c in range(sends):
                act_next(e, c).wait_send()


PIECES = 12
ADOPTED = 3
WAIT_ROOT = 2
LAG = 4


def backward_kernel(
    i_qkv, i_p, i_mixed, i_inv, i_xhat, i_rstd, i_x, i_w, i_v, head, segments, ln_gain,
    o_gin, o_w, o_v, o_aside, o_sum,
    qkv, prob, mixed, inv, xhat, rstd, X, W, V, G, gout, low, resid, gup, gsplit,
    mine, give, taken, part, leave, received, belong, sums, loss,
    i_sem, t_sem, via, gs, gr, is_, ir, xs, xr, ps, pr, fs, fr, as_, ar, vs, vr, ss, sr, ls, lr,
):
    s, d, m = lax.axis_index("section"), lax.axis_index("dp"), lax.axis_index("mp")
    sections, planes = lax.axis_size("section"), lax.axis_size("dp")
    last = sections - 1
    other = 1 - m
    seq, width = X.shape
    chunks = seq // ROWS
    sends = seq // SEND
    n_qkv = qkv.shape[2]
    cols = W.shape[2]
    even = lax.rem(s, 2) == 0
    odd = lax.rem(s, 2) == 1
    tiles = prob.shape[0] // 2
    step = 2 * cols // tiles
    load = {
        name: pltpu.make_async_copy(a, b, i_sem.at[i])
        for i, (name, a, b) in enumerate(
            [("xhat", i_xhat, xhat), ("rstd", i_rstd, rstd),
             ("act", i_p.at[pl.ds(0, tiles)], prob.at[pl.ds(0, tiles)]), ("x", i_x, X),
             ("qkv", i_qkv, qkv), ("mixed", i_mixed, mixed), ("inv", i_inv, inv)]
        )
    }

    def load_tile(kind, t):
        h, c = t * step // cols, t * step % cols
        where = {
            "v": (h, pl.ds(c, step)), "slope": (tiles + t,), "w": (h, slice(None), pl.ds(c, step)),
        }[kind]
        source, target = {"v": (i_v, V), "slope": (i_p, prob), "w": (i_w, W)}[kind]
        at = {"v": 0, "slope": 1, "w": 2}[kind]
        return pltpu.make_async_copy(source.at[where], target.at[where], t_sem.at[at, t])

    def tile_ready(t):
        for kind in ("v", "slope", "w"):
            load_tile(kind, t).wait()

    load["xhat"].start()
    load["rstd"].start()
    for t in range(tiles):
        pl.when(odd)(load_tile("v", t).start)
        load_tile("slope", t).start()
        load_tile("w", t).start()
    load["act"].start()
    load["x"].start()

    @pl.when(even)
    def _():
        for name in ("qkv", "mixed", "inv"):
            load[name].start()

    barrier = pltpu.get_barrier_semaphore()
    for t in range(sections):
        for c in range(2):
            @pl.when((s != t) | (m != c))
            def _():
                pl.semaphore_signal(barrier, inc=1, device_id={"section": t, "mp": c}, device_id_type=MESH)

    def greet(i, carry):
        to = lax.rem(d + 1 + i, planes)
        for c in range(2):
            pl.semaphore_signal(barrier, inc=1, device_id={"dp": to, "mp": c}, device_id_type=MESH)
        return carry

    lax.fori_loop(0, planes - 1, greet, 0)
    pl.semaphore_wait(barrier, 2 * sections - 1 + 2 * (planes - 1))

    def remote(src, dst, send, recv, **to):
        return pltpu.make_async_remote_copy(
            src_ref=src, dst_ref=dst, send_sem=send, recv_sem=recv, device_id=to, device_id_type=MESH
        )

    def grad_prev(c):
        rows = pl.ds(pl.multiple_of(c * SEND, SEND), SEND)
        return remote(gout.at[rows], G.at[rows], gs.at[c], gr.at[c], section=s - 1)

    def via_in(c):
        rows = pl.ds(c * SEND, SEND)
        return remote(gout.at[rows], gout.at[rows], gs.at[c], via.at[0], section=0)

    def via_out(c):
        rows = pl.ds(c * SEND, SEND)
        return remote(gout.at[rows], G.at[rows], via.at[1], gr.at[c], section=1)

    def spread(t, c):
        return remote(
            gsplit.at[t, pl.ds(c * ROWS, ROWS)], o_gin.at[m], is_.at[t * 2 + c], ir.at[m], section=t, mp=c
        )

    load["xhat"].wait()
    load["rstd"].wait()

    own_slot = d * 2 + m
    sums[own_slot] = jnp.zeros_like(sums[own_slot])

    @pl.when(s == last)
    def _():
        sums[own_slot, 3:4, :] = head[8:9, :]
        belong[...] = member_rows(jnp.where(m == 0, segments[0:1, :], segments[1:2, :]), 8)

    @pl.when(s >= last - 1)
    def _():
        taken[ADOPTED] = jnp.zeros_like(taken[ADOPTED])

    def through_norm(rows, g):
        xh = xhat[rows, :]
        grad = norm_back(g, xh, rstd[rows, :1], ln_gain[0])
        sums[own_slot, 0:1, :] += jnp.sum(grad, axis=0, keepdims=True)
        sums[own_slot, 1:2, :] += jnp.sum(g * xh, axis=0, keepdims=True)
        sums[own_slot, 2:3, :] += jnp.sum(g, axis=0, keepdims=True)
        resid[rows, :] = grad
        low[rows, :] = grad.astype(BF)

    half = cols // 4
    step_rows = width // PIECES

    def exchange(slot):
        to = received if slot == ADOPTED else taken.at[slot]
        return remote(give.at[slot], to, xs.at[slot], xr.at[slot], mp=other)

    def adopt(i):
        rows = pl.ds(pl.multiple_of(i * step_rows, step_rows), step_rows)
        to = jnp.where(s == last, last - 1, last)
        return remote(leave.at[rows], mine.at[ADOPTED, rows], as_.at[i], ar.at[i], section=to)

    def weight_grads(left, right, count):
        for h, out in ((other, give), (m, mine)):
            for j in range(4):
                at = slice(j % 2 * half, j % 2 * half + half)
                if j * half < count:
                    out[1 + j // 2, :, at] = mm(left[...], right[h, :, j * half : (j + 1) * half], 0, 0).astype(BF)
                else:
                    for k in range(2):
                        @pl.when(h == k)
                        def _():
                            out[1 + j // 2, :, at] = mm(
                                low[...], mixed[:, k * half : (k + 1) * half], 0, 0
                            ).astype(BF)
                if out is give and j % 2:
                    exchange(1 + j // 2).start()

    def sum_to(i):
        to = lax.rem(own_slot + 1 + i, 2 * planes)
        return remote(
            sums.at[own_slot], sums.at[own_slot], ss.at[i], sr.at[own_slot], dp=to // 2, mp=lax.rem(to, 2)
        )

    def sum_from(i):
        slot = lax.rem(own_slot + 1 + i, 2 * planes)
        return remote(sums.at[slot], sums.at[slot], ss.at[i], sr.at[slot], dp=slot // 2, mp=lax.rem(slot, 2))

    def start_sums():
        def one(i, carry):
            sum_to(i).start()
            return carry

        lax.fori_loop(0, 2 * planes - 1, one, 0)

    @pl.when(odd)
    def _():
        def feed_rows(r, count, ready=None):
            rows = pl.ds(r, count)
            dx = ffn_back_rows(low[rows, :], W, V, prob, gup, r, count, ready)
            gout[rows, :] = (resid[rows, :] + dx).astype(BF)

        @pl.when(s == last)
        def _():
            for r in range(0, seq, ROWS):
                rows = pl.ds(r, ROWS)
                own = belong[:, rows]
                high = head[:8, :].astype(BF).astype(F32)
                through_norm(rows, mm(own, high, 0, 0) + mm(own, head[:8, :] - high, 0, 0))
                feed_rows(r, ROWS, tile_ready if r == 0 else None)
                for c in range(r // SEND, (r + ROWS) // SEND):
                    grad_prev(c).start()

        @pl.when(s < last)
        def _():
            for t in range(tiles):
                tile_ready(t)
            for c in (0, 2, 1, *range(3, sends)):
                rows = pl.ds(c * SEND, SEND)
                grad_prev(c).wait_recv()
                through_norm(rows, G[rows, :].astype(F32))
                feed_rows(c * SEND, SEND)
                grad_prev(c).start()

        load["act"].wait()
        load["x"].wait()
        start_sums()
        unit = 256
        for h, out in ((other, give), (m, mine)):
            for c in range(cols // unit):
                act = prob[h * (cols // 512) + c * unit // 512, :, c * unit % 512 : c * unit % 512 + unit]
                grad = mm(act, low[...], 0, 0).astype(BF)
                r = c * unit % width
                if c * unit < width and out is mine:
                    leave[r : r + unit, :] = grad
                else:
                    out[ADOPTED if c * unit < width else 0, r : r + unit, :] = grad
            if out is give:
                exchange(ADOPTED).start()
                exchange(0).start()
        exchange(ADOPTED).wait_recv()

        def hand_over(i, carry):
            rows = pl.ds(pl.multiple_of(i * step_rows, step_rows), step_rows)
            leave[rows, :] = (leave[rows, :].astype(F32) + received[rows, :].astype(F32)).astype(BF)
            adopt(i).start()
            return carry

        lax.fori_loop(0, PIECES, hand_over, 0)
        exchange(0).wait_recv()

    @pl.when(even)
    def _():
        for t in range(tiles):
            load_tile("slope", t).wait()
            load_tile("w", t).wait()
        for name in ("act", "x", "qkv", "mixed", "inv"):
            load[name].wait()

        @pl.when(s == 0)
        def _():
            via_in(1).wait_recv()
            via_out(1).start()


        def one(c, carry):
            rows = pl.ds(pl.multiple_of(c * SEND, SEND), SEND)
            grad_prev(c).wait_recv()
            through_norm(rows, G[rows, :].astype(F32))
            return carry

        lax.fori_loop(0, sends, one, 0)
        start_sums()
        attn_back_core(low, W, qkv, prob, inv, mixed, gup, n_qkv)

        def back(c, carry):
            rows = pl.ds(pl.multiple_of(c * ROWS, ROWS), ROWS)
            dx = mm(gup[0, rows, :n_qkv], W[0, :, :n_qkv], 1, 1) + mm(
                gup[1, rows, :n_qkv], W[1, :, :n_qkv], 1, 1
            )
            grad = (resid[rows, :] + dx).astype(BF)

            @pl.when(s > 0)
            def _():
                gout[rows, :] = grad
                for i in range(ROWS // SEND):
                    piece = c * (ROWS // SEND) + i
                    pl.when(piece != 1)(grad_prev(piece).start)
                    pl.when(piece == 1)(via_in(1).start)

            @pl.when(s == 0)
            def _():
                part_width = gsplit.shape[2]
                for t in range(sections):
                    gsplit[t, rows, :] = grad[:, t * part_width : (t + 1) * part_width]

            return carry

        lax.fori_loop(0, chunks, back, 0)

        @pl.when(s == 0)
        def _():
            for t in range(sections):
                for c in range(2):
                    if t > 0:
                        spread(t, c).start()
                    else:
                        @pl.when(m != c)
                        def _():
                            spread(t, c).start()

                        @pl.when(m == c)
                        def _():
                            pltpu.make_async_copy(
                                gsplit.at[t, pl.ds(c * ROWS, ROWS)], o_gin.at[m], is_.at[t * 2 + c]
                            ).start()

        weight_grads(X, gup, n_qkv)

    @pl.when(even)
    def _():
        for slot in (1, 2):
            exchange(slot).wait_recv()

    root_a, root_b = (planes - 1) // 2, planes // 2
    first = jnp.where(odd, 0, PIECES)
    total = jnp.where(s >= last - 1, 4 * PIECES, 3 * PIECES)
    lag = WAIT_ROOT + LAG * jnp.maximum(root_b - d, d - root_a)

    def place(i):
        slot = i // PIECES
        rows = pl.ds(pl.multiple_of(lax.rem(i, PIECES) * step_rows, step_rows), step_rows)
        root = jnp.where(lax.rem(i, 2) == 0, root_a, root_b)
        return slot, rows, root

    def part_right(i):
        slot, rows, _ = place(i)
        return remote(mine.at[slot, rows], part.at[0, slot, rows], ps.at[i], pr.at[0, i], dp=d + 1)

    def part_left(i):
        slot, rows, _ = place(i)
        return remote(mine.at[slot, rows], part.at[1, slot, rows], ps.at[i], pr.at[1, i], dp=d - 1)

    def at_home(i, what):
        slot, rows, _ = place(i)
        aside = (slot == ADOPTED) & (s == last)
        for k in (1, 2):
            pl.when(slot == k)(lambda: what(o_w.at[rows, pl.ds((k - 1) * width, width)]))
        pl.when(aside)(lambda: what(o_aside.at[rows]))
        pl.when(((slot == 0) | (slot == ADOPTED)) & ~aside)(lambda: what(o_v.at[rows]))

    def send_whole(i, side, home_too):
        slot, rows, _ = place(i)

        def go(home):
            source = home if home_too else mine.at[slot, rows]
            remote(source, home, fs.at[side, i], fr.at[i], dp=d + (1 if side else -1)).start()

        at_home(i, go)

    def keep_root(i):
        slot, rows, _ = place(i)
        at_home(i, lambda home: pltpu.make_async_copy(mine.at[slot, rows], home, fr.at[i]).start())

    def whole_here(i):
        slot, rows, _ = place(i)
        pltpu.make_async_copy(mine.at[slot, rows], mine.at[slot, rows], fr.at[i]).wait()

    def whole_sent(i, side):
        slot, rows, _ = place(i)
        remote(mine.at[slot, rows], mine.at[slot, rows], fs.at[side, i], fr.at[i], dp=d).wait_send()

    def bring_home(i):
        rows = pl.ds(pl.multiple_of(i * step_rows, step_rows), step_rows)
        return remote(o_aside.at[rows], o_v.at[rows], vs.at[i], vr.at[i], section=0)

    def add(i, *sides):
        slot, rows, _ = place(i)
        value = mine[slot, rows, :].astype(F32) + taken[slot, rows, :].astype(F32)
        for side in sides:
            value = value + part[side, slot, rows, :].astype(F32)
        mine[slot, rows, :] = value.astype(BF)

    def adopted_here(i):
        @pl.when(i >= ADOPTED * PIECES)
        def _():
            adopt(i - ADOPTED * PIECES).wait_recv()

    def up_tile(t):
        j = lax.rem(t, 4)
        at = pl.ds(pl.multiple_of(lax.rem(j, 2) * half, half), half)

        def tile(h):
            return mm(X[...], gup[h, :, pl.ds(pl.multiple_of(j * half, half), half)], 0, 0).astype(BF)

        @pl.when(t < 4)
        def _():
            give[1 + j // 2, :, at] = tile(other)
            pl.when(j == 1)(exchange(1).start)
            pl.when(j == 3)(exchange(2).start)

        @pl.when(t >= 4)
        def _():
            mine[1 + j // 2, :, at] = tile(m)

    def pieces(i, carry):
        root = place(i)[2]
        pl.when(odd & (i < 8))(lambda: up_tile(i))

        @pl.when(odd & (i == PIECES))
        def _():
            for slot in (1, 2):
                exchange(slot).wait_recv()

        @pl.when((i < total) & (d < root))
        def _():
            adopted_here(i)

            @pl.when(d > 0)
            def _():
                part_right(i).wait_recv()
                add(i, 0)

            @pl.when(d == 0)
            def _():
                add(i)

            part_right(i).start()

        @pl.when((i < total) & (d > root))
        def _():
            adopted_here(i)

            @pl.when(d < planes - 1)
            def _():
                part_left(i).wait_recv()
                add(i, 1)

            @pl.when(d == planes - 1)
            def _():
                add(i)

            part_left(i).start()

        k = i - WAIT_ROOT

        @pl.when((k >= first) & (k < total) & (d == place(k)[2]))
        def _():
            adopted_here(k)
            part_right(k).wait_recv()
            part_left(k).wait_recv()
            add(k, 0, 1)
            keep_root(k)
            send_whole(k, 0, False)
            send_whole(k, 1, False)

        @pl.when(i >= first + lag)
        def _():
            j = i - lag
            root = place(j)[2]
            whole_here(j)

            @pl.when((d < root) & (d > 0))
            def _():
                send_whole(j, 0, True)

            @pl.when((d > root) & (d < planes - 1))
            def _():
                send_whole(j, 1, True)

            @pl.when((s == last) & (j >= ADOPTED * PIECES))
            def _():
                bring_home(j - ADOPTED * PIECES).start()

        return carry

    lax.fori_loop(first, total + lag, pieces, 0)

    def settle(i, carry):
        root = place(i)[2]

        @pl.when(d != root)
        def _():
            part_right(i).wait_send()

        @pl.when((d <= root) & (d > 0))
        def _():
            whole_sent(i, 0)

        @pl.when((d >= root) & (d < planes - 1))
        def _():
            whole_sent(i, 1)

        return carry

    lax.fori_loop(first, total, settle, 0)

    def brought(i, carry):
        @pl.when(s == 0)
        def _():
            bring_home(i).wait_recv()

        @pl.when(s == last)
        def _():
            bring_home(i).wait_send()

        @pl.when(odd)
        def _():
            adopt(i).wait_send()

        return carry

    lax.fori_loop(0, PIECES, brought, 0)

    @pl.when(odd)
    def _():
        exchange(0).wait_send()
        exchange(ADOPTED).wait_send()

    for slot in (1, 2):
        exchange(slot).wait_send()

    pl.when(s == 0)(via_out(1).wait_send)

    @pl.when(s > 0)
    def _():
        for c in range(sends):
            grad_prev(c).wait_send()

    @pl.when(s == 0)
    def _():
        for t in range(sections):
            for c in range(2):
                if t > 0:
                    spread(t, c).wait_send()
                else:
                    @pl.when(m != c)
                    def _():
                        spread(t, c).wait_send()

                    @pl.when(m == c)
                    def _():
                        pltpu.make_async_copy(
                            gsplit.at[t, pl.ds(c * ROWS, ROWS)], o_gin.at[m], is_.at[t * 2 + c]
                        ).wait()

    def arrival(r):
        return remote(gsplit.at[0, pl.ds(0, ROWS)], o_gin.at[r], is_.at[0], ir.at[r], section=0, mp=r)

    for r in range(2):
        @pl.when((s != 0) | (m != r))
        def _():
            arrival(r).wait_recv()

    def sums_in(i, carry):
        sum_from(i).wait_recv()
        sum_to(i).wait_send()
        return carry

    def loss_down(t):
        return remote(loss, loss, ls.at[t], lr.at[0], section=t)

    lax.fori_loop(0, 2 * planes - 1, sums_in, 0)
    total_sums = jnp.sum(sums[...], axis=0)

    @pl.when(s == last)
    def _():
        loss[...] = total_sums
        for t in range(last):
            loss_down(t).start()
        for t in range(last):
            loss_down(t).wait_send()

    @pl.when(s < last)
    def _():
        loss_down(0).wait_recv()

    o_sum[...] = total_sums
    o_sum[3:4, :] = loss[3:4, :]


def local(
    hidden_in, segments, partners, queue, first_weight, second_weight, out_bias, ln_gain, ln_bias
):
    width = hidden_in.shape[-1]
    seq = segments.shape[1]
    w1 = jnp.transpose(first_weight[:, 0], (0, 2, 1, 3))
    w2 = second_weight.reshape(2, -1, width)
    half = w1.shape[3]
    cols, n_qkv, heads = 4 * half, 3 * half, 2 * half // HD
    anyspace = pl.BlockSpec(memory_space=pl.ANY)
    vmem = pl.BlockSpec(memory_space=pltpu.VMEM)
    shape = jax.ShapeDtypeStruct
    dma = pltpu.SemaphoreType.DMA
    saved = [
        shape((2, seq, n_qkv), BF), shape((heads, seq, seq), BF), shape((seq, width), BF),
        shape((heads // 2, seq, 128), F32), shape((seq, width), F32), shape((seq, 128), F32), shape((seq, width), BF), shape((2, width, cols), BF),
        shape((2, cols, width), BF),
    ]
    sections, planes = lax.axis_size("section"), lax.axis_size("dp")
    *kept, head = pl.pallas_call(
        forward_kernel,
        out_shape=saved + [shape((16, width), F32)],
        in_specs=[anyspace] * 4 + [vmem] * 5,
        out_specs=[anyspace] * 9 + [vmem],
        scratch_shapes=[
            pltpu.VMEM((2, 2, width, cols), BF), pltpu.VMEM((2, 2, cols, width), BF),
            pltpu.VMEM((2, seq, width), BF), pltpu.VMEM((2, seq, width), BF),
            pltpu.VMEM((2, 2, seq, n_qkv), BF), pltpu.VMEM((heads, seq, seq), BF),
            pltpu.VMEM((2, seq, width), BF), pltpu.VMEM((heads // 2, seq, 128), F32), pltpu.VMEM((seq, width), F32),
            pltpu.VMEM((seq, width), F32), pltpu.VMEM((seq, 128), F32),
            pltpu.VMEM((seq, 128), BF), pltpu.VMEM((seq, 128), BF), pltpu.VMEM((8, 128), jnp.int32),
            pltpu.VMEM((2, 8, width), F32), pltpu.VMEM((2 * planes, 8, width), F32),
            pltpu.VMEM(queue.shape, BF), pltpu.VMEM((2 * planes, 8, width + 128), F32),
            pltpu.VMEM((8, width + 128), F32), pltpu.VMEM((sections - 1, 8, width + 128), F32),
            pltpu.VMEM((2 * planes, 8, width + 128), F32),
            dma((7,)), dma((2, 4)), dma((2, 4)), dma((2, 4)), dma((2,)), dma((2,)), dma((2, V_PARTS)), dma((2, V_PARTS)),
            dma((2, V_PARTS)), dma((2, V_PARTS)), dma((2, 2, V_PARTS)), dma((2, 2, V_PARTS)),
            *[dma((2, V_PARTS))] * 5,
            dma((2,)), dma((2,)), dma((2, seq // SEND)), dma((2, seq // SEND)), dma((9,)),
            dma((2 * planes,)), dma((2 * planes,)), dma((sections - 1,)), dma((1,)), dma((1,)),
            dma((sections - 1,)), dma((2 * planes,)), dma((2 * planes,)),
        ],
        compiler_params=pltpu.CompilerParams(
            collective_id=0, has_side_effects=True, vmem_limit_bytes=VMEM_BYTES
        ),
        name="forward",
    )(hidden_in, w1, w2, queue, segments, partners, out_bias, ln_gain, ln_bias)
    half_width = width // lax.axis_size("section")
    gin, gw, gv, _, sums = pl.pallas_call(
        backward_kernel,
        out_shape=[
            shape((2, seq // 2, half_width), BF), shape((width, cols), BF), shape((width, width), BF),
            shape((width, width), BF), shape((8, width), F32),
        ],
        in_specs=[anyspace] * 9 + [vmem] * 3,
        out_specs=[vmem, anyspace, anyspace, anyspace, vmem],
        scratch_shapes=[pltpu.VMEM(a.shape, a.dtype) for a in saved]
        + [
            pltpu.VMEM((seq, width), BF), pltpu.VMEM((seq, width), BF), pltpu.VMEM((seq, width), BF),
            pltpu.VMEM((seq, width), F32), pltpu.VMEM((2, seq, cols), BF),
            pltpu.VMEM((sections, seq, half_width), BF),
            pltpu.VMEM((4, width, width), BF), pltpu.VMEM((4, width, width), BF),
            pltpu.VMEM((4, width, width), BF), pltpu.VMEM((2, 4, width, width), BF),
            pltpu.VMEM((width, width), BF), pltpu.VMEM((width, width), BF), pltpu.VMEM((8, seq), F32),
            pltpu.VMEM((2 * planes, 8, width), F32), pltpu.VMEM((8, width), F32),
            dma((7,)), dma((3, heads // 2)), dma((2,)), dma((seq // SEND,)), dma((seq // SEND,)), dma((2 * sections,)), dma((2,)),
            dma((4,)), dma((4,)), dma((4 * PIECES,)), dma((2, 4 * PIECES)), dma((2, 4 * PIECES)),
            dma((4 * PIECES,)), dma((PIECES,)), dma((PIECES,)), dma((PIECES,)), dma((PIECES,)), dma((2 * planes,)), dma((2 * planes,)),
            dma((sections - 1,)), dma((1,)),
        ],
        compiler_params=pltpu.CompilerParams(
            collective_id=1, has_side_effects=True, vmem_limit_bytes=VMEM_BYTES
        ),
        name="backward",
    )(*kept, head, segments, ln_gain)
    grad_first = gw.astype(F32).reshape(width, 4, -1)
    grad_second = gv.astype(F32).reshape(second_weight.shape[2:])
    return (
        sums[3, 0], gin, grad_first[None], grad_second[None], sums[0:1], sums[1:2], sums[2:3],
    )


def solution(mesh):
    in_specs = (
        P("dp", "mp", None), P("dp", None), P("dp", None), P(("section", "dp", "mp"), None),
        P(None, "section", None, None, "mp"), P(None, "section", None, "mp", None),
        P(None, "section", None), P(None, "section", None), P(None, "section", None),
    )
    out_specs = (
        P(), P("dp", "mp", "section"), P("section", None, None, "mp"), P("section", None, "mp", None),
        P("section", None), P("section", None), P("section", None),
    )
    return jax.shard_map(local, mesh=mesh, in_specs=in_specs, out_specs=out_specs, check_vma=False)
```
